512 devices in a mesh: panel: 2 (over z_hi), lon: 32 (over y, z_lo), colat: 8 (over x, core).
Axes of the slice: x: 4, y: 4, z: 16 (z_hi: 2, z_lo: 8; z = z_hi * 8 + z_lo), core: 2. Of those that a mesh axis runs over, the one named last changes fastest.
Arguments:
- state_now: float32 [2, 8, 4, 256, 4096], P('panel', None, None, 'colat', 'lon'), may hold values from -1 to 3
- send_row: int32 [2, 32, 8, 128], P('panel', 'lon', 'colat'), may hold values from 0 to 30
- send_col: int32 [2, 32, 8, 128], P('panel', 'lon', 'colat'), may hold values from 0 to 126
- send_weight: float32 [2, 32, 8, 4, 128], P('panel', 'lon', 'colat'), may hold values from 0 to 1, as said below
- ghost_slot: int32 [2, 32, 8, 640], P('panel', 'lon', 'colat'), may hold values from 0 to 32767, as said below
Outputs:
- next_state: float32 [2, 8, 4, 256, 4096], P('panel', None, None, 'colat', 'lon')
The draws below stay inside these ranges and needn't reach their ends.
Inputs may be any that keep to these rules, and one draw needn't show every extreme that they name: `ghost_slot`: slot (l * 8 + c) * 128 + s belongs to tile (l, c) of the other panel. Every entry of tile (l, c) names a slot of a tile (l2, c2) of the other panel that lies within one index of (l, c) along lon and along colat, counted round (index 0 and the last index are neighbours). Entries of ghost positions that do not lie on the panel's edge are never read. All 128 slots of at least one device are named by edge positions of the other panel; a slot may be named more than once. `send_weight`: the four weights of a slot are non-negative and sum to one.
All inputs are finite; a program needn't handle non-finite values.
Results may differ from the reference program's by a relative error of at most 0.0003.
Values sent between devices are 32-bit elements; how exact they have to be, the bound alone decides.
A program may use at most 128 MiB of HBM per device.

```python
import math
import jax
import jax.numpy as jnp
from jax import lax

FIELDS = 8
SHELLS = 4
CT = 32
CP = 128
NT = 256
NP = 4096
GHOSTS = 640
SLOTS = 128
N_LON = 32
N_COLAT = 8


def draw_state_now(key, part):
    key = jax.random.fold_in(key, 11)
    key_density, key_vectors, key_energy = jax.random.split(key, 3)
    density = jnp.exp(jax.random.uniform(key_density, (2, 1, SHELLS, NT, NP), jnp.float32, math.log(0.5), math.log(2.0)))
    vectors = jax.random.uniform(key_vectors, (2, 6, SHELLS, NT, NP), jnp.float32, -1.0, 1.0)
    energy = jax.random.uniform(key_energy, (2, 1, SHELLS, NT, NP), jnp.float32, 1.0, 3.0)
    return jnp.concatenate([density, vectors, energy], axis=1).astype(jnp.float32)


def draw_send_weight(key, part):
    key = jax.random.fold_in(key, 12)
    key_along, key_across = jax.random.split(key, 2)
    along = jax.random.uniform(key_along, (2, N_LON, N_COLAT, 1, SLOTS), jnp.float32, 0.0, 1.0)
    across = jax.random.uniform(key_across, (2, N_LON, N_COLAT, 1, SLOTS), jnp.float32, 0.0, 1.0)
    return jnp.concatenate([(1.0 - along) * (1.0 - across), along * (1.0 - across), (1.0 - along) * across, along * across], axis=3).astype(jnp.float32)


def slot_plan(key, far_read):
    key_lon, key_colat, key_slot, key_order = jax.random.split(key, 4)
    total = N_LON * N_COLAT * SLOTS
    shape = (N_LON, N_COLAT, GHOSTS)
    lon_ids = jnp.arange(N_LON, dtype=jnp.int32)[:, None, None]
    colat_ids = jnp.arange(N_COLAT, dtype=jnp.int32)[None, :, None]
    lon_step = jax.random.randint(key_lon, shape, -1, 2).astype(jnp.int32)
    colat_step = jax.random.randint(key_colat, shape, -1, 2).astype(jnp.int32)
    slot_pick = jax.random.randint(key_slot, shape, 0, SLOTS).astype(jnp.int32)
    owner_lon = jnp.clip(lon_ids + lon_step, 0, N_LON - 1)
    owner_colat = jnp.clip(colat_ids + colat_step, 0, N_COLAT - 1)
    chosen = ((owner_lon * N_COLAT + owner_colat) * SLOTS + slot_pick).astype(jnp.int32)
    position = jnp.arange(GHOSTS, dtype=jnp.int32)
    corner_edge = (position < 2 * CP) | (position >= 4 * CP) & (position < 4 * CP + 2 * CT)
    corner_rank = jnp.cumsum(corner_edge.astype(jnp.int32)) - 1
    shuffled = jax.random.permutation(key_order, SLOTS).astype(jnp.int32)
    forced = jnp.where(corner_edge & (corner_rank < SLOTS), shuffled[jnp.clip(corner_rank, 0, SLOTS - 1)], chosen[0, 0])
    chosen = chosen.at[0, 0].set(forced.astype(jnp.int32))
    chosen = chosen.at[N_LON - 1, N_COLAT - 1, 0].set(jnp.int32(total - 1))
    if far_read == 1:
        chosen = chosen.at[0, 0, 4 * CP + 2 * CT - 1].set(jnp.int32((N_LON * N_COLAT - 1) * SLOTS) + slot_pick[0, 0, 0])
    return chosen.astype(jnp.int32)


def draw_ghost_slot(key, part):
    key = jax.random.fold_in(key, 13)
    plans = [slot_plan(jax.random.fold_in(key, panel_index), panel_index) for panel_index in range(2)]
    return jnp.stack(plans).astype(jnp.int32)


def place_ends(drawn, stream_key, smallest, top_value):
    extent = drawn.shape
    place = [jax.random.randint(jax.random.fold_in(stream_key, axis), (), 0, extent[axis]) for axis in range(len(extent))]
    drawn = drawn.at[tuple(place)].set(smallest)
    longest = extent.index(max(extent))
    place[longest] = (place[longest] + 1) % extent[longest]
    return drawn.at[tuple(place)].set(top_value)


def setup_inputs(seed: int = 0) -> dict:
    splits = jax.random.split(jax.random.key(seed), 6)
    state_now = draw_state_now(jax.random.fold_in(splits[5], 71), 0)
    send_row = place_ends(jax.random.randint(splits[1], (2, N_LON, N_COLAT, SLOTS), 0, CT - 1), jax.random.fold_in(splits[1], 1), 0, (CT - 1) - 1).astype(jnp.int32)
    send_col = place_ends(jax.random.randint(splits[2], (2, N_LON, N_COLAT, SLOTS), 0, CP - 1), jax.random.fold_in(splits[2], 1), 0, (CP - 1) - 1).astype(jnp.int32)
    send_weight = draw_send_weight(jax.random.fold_in(splits[5], 71), 0)
    ghost_slot = draw_ghost_slot(jax.random.fold_in(splits[5], 71), 0)
    return {"state_now": state_now, "send_row": send_row, "send_col": send_col, "send_weight": send_weight, "ghost_slot": ghost_slot}


RADIAL_STEP = 0.65 / 511.0
COURANT = 0.3
ROTATION = 300.0
GRAVITY = 300.0
ADIABATIC = 2.0 / 3.0


def flux_table(values):
    density = values[0]
    moment = values[1:4]
    magnet = values[4:7]
    energy = values[7]
    velocity = moment / density
    magnet_power = jnp.sum(magnet * magnet, axis=0)
    kinetic = 0.5 * jnp.sum(moment * velocity, axis=0)
    pressure = ADIABATIC * (energy - kinetic - 0.5 * magnet_power)
    total_pressure = pressure + 0.5 * magnet_power
    aligned = jnp.sum(velocity * magnet, axis=0)
    identity = jnp.eye(3, dtype=jnp.float32)[:, :, None, None, None]
    momentum_flux = moment[:, None] * velocity[None, :] - magnet[:, None] * magnet[None, :] + identity * total_pressure
    induction_flux = magnet[:, None] * velocity[None, :] - velocity[:, None] * magnet[None, :]
    energy_flux = (energy + total_pressure) * velocity - magnet * aligned
    return jnp.concatenate([moment[None], momentum_flux, induction_flux, energy_flux[None]], axis=0)


def radial_slope(values):
    interior = (values[..., 2:, :, :] - values[..., :-2, :, :]) / (2.0 * RADIAL_STEP)
    lowest = (values[..., 1:2, :, :] - values[..., 0:1, :, :]) / RADIAL_STEP
    highest = (values[..., -1:, :, :] - values[..., -2:-1, :, :]) / RADIAL_STEP
    return jnp.concatenate([lowest, interior, highest], axis=-3)


def advance_section(padded, row_start, col_start, total_rows, total_cols, panel_index):
    fields, shells, tall, broad = padded.shape
    lat_cells = tall - 4
    lon_cells = broad - 4
    polar_step = 0.5 * math.pi / total_rows
    azimuth_step = 1.5 * math.pi / total_cols
    time_step = COURANT / (1.0 / RADIAL_STEP + 1.0 / polar_step + 1.0 / (azimuth_step * math.sin(0.25 * math.pi)))
    colatitude = 0.25 * math.pi + (jnp.asarray(row_start).astype(jnp.float32) + jnp.arange(lat_cells, dtype=jnp.float32) + 0.5) * polar_step
    longitude = -0.75 * math.pi + (jnp.asarray(col_start).astype(jnp.float32) + jnp.arange(lon_cells, dtype=jnp.float32) + 0.5) * azimuth_step
    radius = 1.0 - (shells - 1 - jnp.arange(shells, dtype=jnp.float32)) * RADIAL_STEP
    polar_sine = jnp.sin(colatitude)[:, None]
    polar_cosine = jnp.cos(colatitude)[:, None]
    azimuth_sine = jnp.sin(longitude)[None, :]
    azimuth_cosine = jnp.cos(longitude)[None, :]
    filled = jnp.ones((lat_cells, lon_cells), jnp.float32)
    radial_unit = jnp.stack([polar_sine * azimuth_cosine, polar_sine * azimuth_sine, polar_cosine * filled])
    polar_unit = jnp.stack([polar_cosine * azimuth_cosine, polar_cosine * azimuth_sine, -polar_sine * filled])
    azimuth_unit = jnp.stack([-azimuth_sine * filled, azimuth_cosine * filled, 0.0 * filled])
    inverse_radius = (1.0 / radius)[:, None, None]
    column_flux = flux_table(padded[:, :, :, 2:-2])
    row_flux = flux_table(padded[:, :, 2:-2, :])
    radial_part = radial_slope(column_flux[:, :, :, 2:-2, :])
    polar_part = (column_flux[..., 0:-4, :] - 8.0 * column_flux[..., 1:-3, :] + 8.0 * column_flux[..., 3:-1, :] - column_flux[..., 4:, :]) / (12.0 * polar_step)
    azimuth_part = (row_flux[..., 0:-4] - 8.0 * row_flux[..., 1:-3] + 8.0 * row_flux[..., 3:-1] - row_flux[..., 4:]) / (12.0 * azimuth_step)
    divergence = jnp.sum(radial_unit[None, :, None] * radial_part + polar_unit[None, :, None] * (inverse_radius * polar_part) + azimuth_unit[None, :, None] * (inverse_radius / polar_sine * azimuth_part), axis=1)
    centre = padded[:, :, 2:-2, 2:-2]
    density = centre[0]
    moment = centre[1:4]
    panel_weight = jnp.asarray(panel_index).astype(jnp.float32)
    spin_second = ROTATION * panel_weight
    spin_third = ROTATION * (1.0 - panel_weight)
    coriolis = 2.0 * jnp.stack([spin_second * moment[2] - spin_third * moment[1], spin_third * moment[0], -spin_second * moment[0]])
    moment_rate = -divergence[1:4] - coriolis - GRAVITY * density[None] * radial_unit[:, None]
    energy_rate = -divergence[7] - GRAVITY * jnp.sum(moment * radial_unit[:, None], axis=0)
    rate = jnp.concatenate([-divergence[0:1], moment_rate, -divergence[4:7], energy_rate[None]], axis=0)
    return centre + time_step * rate


def mix_slots(flattened, anchor, stride, weight):
    upper_left = jnp.take(flattened, anchor, axis=1)
    upper_right = jnp.take(flattened, anchor + 1, axis=1)
    lower_left = jnp.take(flattened, anchor + stride, axis=1)
    lower_right = jnp.take(flattened, anchor + stride + 1, axis=1)
    blended = weight[0] * upper_left + weight[1] * upper_right + weight[2] * lower_left + weight[3] * lower_right
    pieces = blended.reshape(8, blended.shape[0] // 8, blended.shape[1])
    rotated = jnp.stack([pieces[0], -pieces[1], pieces[3], pieces[2], -pieces[4], pieces[6], pieces[5], pieces[7]])
    return rotated.reshape(blended.shape)


def panel_slots(values, send_row, send_col, send_weight):
    lon_ids = jnp.arange(N_LON, dtype=jnp.int32)[:, None, None]
    colat_ids = jnp.arange(N_COLAT, dtype=jnp.int32)[None, :, None]
    global_rows = colat_ids * CT + send_row
    global_cols = lon_ids * CP + send_col
    anchor = (global_rows * NP + global_cols).reshape(-1).astype(jnp.int32)
    weight = jnp.moveaxis(send_weight, 2, 0).reshape(4, -1)
    flattened = values.reshape(FIELDS * SHELLS, NT * NP)
    return mix_slots(flattened, anchor, NP, weight)


def reference(state_now, send_row, send_col, send_weight, ghost_slot):
    slot_sets = [panel_slots(state_now[panel_index], send_row[panel_index], send_col[panel_index], send_weight[panel_index]) for panel_index in range(2)]
    outputs = []
    for panel_index in range(2):
        ghosts = jnp.take(slot_sets[1 - panel_index], ghost_slot[panel_index].reshape(-1).astype(jnp.int32), axis=1)
        ghosts = ghosts.reshape(FIELDS, SHELLS, N_LON, N_COLAT, GHOSTS)
        padded = jnp.pad(state_now[panel_index], ((0, 0), (0, 0), (2, 2), (2, 2)))
        north = ghosts[:, :, :, 0, 0:2 * CP].reshape(FIELDS, SHELLS, N_LON, 2, CP).transpose(0, 1, 3, 2, 4).reshape(FIELDS, SHELLS, 2, NP)
        south = ghosts[:, :, :, N_COLAT - 1, 2 * CP:4 * CP].reshape(FIELDS, SHELLS, N_LON, 2, CP).transpose(0, 1, 3, 2, 4).reshape(FIELDS, SHELLS, 2, NP)
        west = ghosts[:, :, 0, :, 4 * CP:4 * CP + 2 * CT].reshape(FIELDS, SHELLS, NT, 2)
        east = ghosts[:, :, N_LON - 1, :, 4 * CP + 2 * CT:].reshape(FIELDS, SHELLS, NT, 2)
        padded = padded.at[:, :, 0:2, 2:NP + 2].set(north)
        padded = padded.at[:, :, NT + 2:NT + 4, 2:NP + 2].set(south)
        padded = padded.at[:, :, 2:NT + 2, 0:2].set(west)
        padded = padded.at[:, :, 2:NT + 2, NP + 2:NP + 4].set(east)

        def one_tile(tile_number):
            colat_at = (tile_number // N_LON).astype(jnp.int32)
            lon_at = (tile_number % N_LON).astype(jnp.int32)
            block = lax.dynamic_slice(padded, (jnp.int32(0), jnp.int32(0), (colat_at * CT).astype(jnp.int32), (lon_at * CP).astype(jnp.int32)), (FIELDS, SHELLS, CT + 4, CP + 4))
            return advance_section(block, colat_at * CT, lon_at * CP, NT, NP, panel_index)

        blocks = lax.map(one_tile, jnp.arange(N_COLAT * N_LON, dtype=jnp.int32))
        whole = blocks.reshape(N_COLAT, N_LON, FIELDS, SHELLS, CT, CP).transpose(2, 3, 0, 4, 1, 5).reshape(FIELDS, SHELLS, NT, NP)
        outputs.append(whole)
    return jnp.stack(outputs)
```

```python
import math

import jax
import jax.numpy as jnp
from jax import lax
from jax.experimental import pallas as pl
from jax.experimental.pallas import tpu as pltpu
from jax.sharding import PartitionSpec as P

RADIAL_STEP = 0.65 / 511.0
COURANT = 0.3
ROTATION = 300.0
GRAVITY = 300.0
ADIABATIC = 2.0 / 3.0

FIELDS = 8
SHELLS = 4
CT = 32
CP = 128
SLOTS = 128
TALL = SHELLS * CT
MESH = pl.DeviceIdType.MESH
AROUND = [(dl, dc) for dl in (-1, 0, 1) for dc in (-1, 0, 1)]
TURNED = [(0, 1.0), (1, -1.0), (3, 1.0), (2, 1.0), (4, -1.0), (6, 1.0), (5, 1.0), (7, 1.0)]


def lanes_at(values, index):
    return jnp.take_along_axis(values, index, axis=1, mode="promise_in_bounds")


def cell_terms(u):
    rho, m, b, energy = u[0], u[1:4], u[4:7], u[7]
    inverse = 1.0 / rho
    v = [a * inverse for a in m]
    power = b[0] * b[0] + b[1] * b[1] + b[2] * b[2]
    moving = m[0] * v[0] + m[1] * v[1] + m[2] * v[2]
    pressure = ADIABATIC * (energy - 0.5 * moving - 0.5 * power) + 0.5 * power
    aligned = v[0] * b[0] + v[1] * b[1] + v[2] * b[2]
    return m, b, v, pressure, energy + pressure, aligned, rho


def flux_along(terms, e):
    m, b, v, pressure, enthalpy, aligned, rho = terms
    ve = v[0] * e[0] + v[1] * e[1]
    be = b[0] * e[0] + b[1] * e[1]
    if e[2] is not None:
        ve = ve + v[2] * e[2]
        be = be + b[2] * e[2]
    out = [rho * ve]
    for i in range(3):
        term = m[i] * ve - b[i] * be
        out.append(term if e[i] is None else term + pressure * e[i])
    for i in range(3):
        out.append(b[i] * ve - v[i] * be)
    out.append(enthalpy * ve - aligned * be)
    return out


def kernel(
    x_hbm, row_hbm, col_hbm, weight_hbm, ghost_hbm, out_hbm,
    x, rows, cols, weight, wanted,
    slots, slots_in, row_out, row_in, col_out, col_in,
    radial, polar, azimuth, acc,
    in_sem, send_sem, recv_sem, out_sem,
):
    p, l, c = lax.axis_index("panel"), lax.axis_index("lon"), lax.axis_index("colat")
    nl, nc = lax.axis_size("lon"), lax.axis_size("colat")
    ht = 0.5 * math.pi / (nc * CT)
    hp = 1.5 * math.pi / (nl * CP)
    tau = COURANT / (1.0 / RADIAL_STEP + 1.0 / ht + 1.0 / (hp * math.sin(0.25 * math.pi)))

    def wrap(a, n):
        return lax.rem(a + n, n)

    def on_edge(la, ca):
        return (la == 0) | (la == nl - 1) | (ca == 0) | (ca == nc - 1)

    up, down, left, right = c > 0, c < nc - 1, l > 0, l < nl - 1
    edge = on_edge(l, c)
    others = [(wrap(l + dl, nl), wrap(c + dc, nc)) for dl, dc in AROUND]

    loads = [
        pltpu.make_async_copy(src, dst, in_sem.at[i])
        for i, (src, dst) in enumerate(
            ((row_hbm, rows), (col_hbm, cols), (weight_hbm, weight), (ghost_hbm, wanted), (x_hbm, x))
        )
    ]
    for load in loads:
        load.start()

    barrier = pltpu.get_barrier_semaphore()

    def greet(device):
        pl.semaphore_signal(barrier, inc=1, device_id=device, device_id_type=MESH)

    pl.when(up)(lambda: greet((p, l, c - 1)))
    pl.when(down)(lambda: greet((p, l, c + 1)))
    pl.when(left)(lambda: greet((p, l - 1, c)))
    pl.when(right)(lambda: greet((p, l + 1, c)))

    @pl.when(edge)
    def _():
        for la, ca in others:
            greet((1 - p, la, ca))

    for load in loads:
        load.wait()

    row_at = lax.broadcasted_iota(jnp.int32, (CT, CP), 0)
    lane8 = lax.broadcasted_iota(jnp.int32, (8, 128), 1)
    sub8 = lax.broadcasted_iota(jnp.int32, (8, 128), 0)
    lane32 = lax.broadcasted_iota(jnp.int32, (CT, CP), 1)
    first = row_at == rows[0, 0]
    second = row_at == rows[0, 0] + 1
    w = weight[0, 0, 0]
    on_left = jnp.where(first, w[0:1], jnp.where(second, w[2:3], 0.0))
    on_right = jnp.where(first, w[1:2], jnp.where(second, w[3:4], 0.0))
    pick = jnp.broadcast_to(cols[0, 0], (CT, CP))

    def one_shell(k, _):
        at = pl.multiple_of(k * CT, CT)
        for f in range(FIELDS):
            plane = x[f, pl.ds(at, CT), :]
            mixed = on_left * lanes_at(plane, pick) + on_right * lanes_at(plane, pick + 1)
            target, sign = TURNED[f]
            slots[target, pl.ds(k, 1), :] = sign * jnp.sum(mixed, axis=0, keepdims=True)
        return 0

    lax.fori_loop(0, SHELLS, one_shell, 0)

    lanes = lax.broadcasted_iota(jnp.int32, (TALL, CP), 1)
    packed = jnp.zeros((TALL, CP), jnp.float32)
    for f in range(FIELDS):
        for r in range(2):
            row_out[0, f, pl.ds(4 * r, 4), :] = x[f, pl.ds(r, SHELLS, stride=CT), :]
            row_out[1, f, pl.ds(4 * r, 4), :] = x[f, pl.ds(CT - 2 + r, SHELLS, stride=CT), :]
        turned = pltpu.roll(x[f], 2 + 4 * f, 1)
        packed = jnp.where(lanes // 4 == f, turned, packed)
    upright = packed.T
    for f in range(FIELDS):
        col_out[1, f] = upright[4 * f : 4 * f + 2]
        col_out[0, f] = upright[4 * f + 2 : 4 * f + 4]

    def one(flag):
        return flag.astype(jnp.int32)

    expected = one(up) + one(down) + one(left) + one(right)
    for la, ca in others:
        expected = expected + one(on_edge(la, ca))
    pl.semaphore_wait(barrier, expected)

    def remote(src, dst, i, device):
        return pltpu.make_async_remote_copy(
            src_ref=src, dst_ref=dst, send_sem=send_sem.at[i], recv_sem=recv_sem.at[i],
            device_id=device, device_id_type=MESH,
        )

    slot_copies = [
        pltpu.make_async_remote_copy(
            src_ref=slots, dst_ref=slots_in.at[8 - j], send_sem=send_sem.at[j], recv_sem=recv_sem.at[8 - j],
            device_id=(1 - p, la, ca), device_id_type=MESH,
        )
        for j, (la, ca) in enumerate(others)
    ]
    for copy, (la, ca) in zip(slot_copies, others):
        pl.when(on_edge(la, ca))(copy.start)
    to_up = remote(row_out.at[0], row_in.at[1], 9, (p, l, c - 1))
    to_down = remote(row_out.at[1], row_in.at[0], 10, (p, l, c + 1))
    to_left = remote(col_out.at[0], col_in.at[1], 11, (p, l - 1, c))
    to_right = remote(col_out.at[1], col_in.at[0], 12, (p, l + 1, c))
    pl.when(left)(to_left.start)
    pl.when(right)(to_right.start)
    pl.when(up)(to_up.start)
    pl.when(down)(to_down.start)

    row0 = (c * CT).astype(jnp.float32) + 0.5
    col0 = (l * CP).astype(jnp.float32) + 0.5

    def angle_t(row):
        return 0.25 * math.pi + (row + row0) * ht

    def angle_f(col):
        return -0.75 * math.pi + (col + col0) * hp

    theta = angle_t(row_at.astype(jnp.float32))
    phi = angle_f(lane8[0:1].astype(jnp.float32))
    st, ct = jnp.sin(theta), jnp.cos(theta)
    sf = jnp.broadcast_to(jnp.sin(phi), (8, CP))
    cf = jnp.broadcast_to(jnp.cos(phi), (8, CP))
    spin_second = ROTATION * p.astype(jnp.float32)
    spin_third = ROTATION - spin_second

    def one_block(n, _):
        at = pl.multiple_of(n * 8, 8)
        th = angle_t((sub8 + lax.rem(n, CT // 8) * 8).astype(jnp.float32))
        s8, c8 = jnp.sin(th), jnp.cos(th)
        u = [x[f, pl.ds(at, 8), :] for f in range(FIELDS)]
        terms = cell_terms(u)
        er = (s8 * cf, s8 * sf, c8)
        for f, value in enumerate(flux_along(terms, er)):
            radial[f, pl.ds(at, 8), :] = value
        for f, value in enumerate(flux_along(terms, (c8 * cf, c8 * sf, -s8))):
            polar[f, pl.ds(at, 8), :] = value
        for f, value in enumerate(flux_along(terms, (-sf, cf, None))):
            azimuth[f, pl.ds(at, 8), :] = value
        rho, m = u[0], u[1:4]
        turn = (
            spin_second * m[2] - spin_third * m[1], spin_third * m[0], -spin_second * m[0]
        )
        acc[0, pl.ds(at, 8), :] = u[0]
        for i in range(3):
            acc[1 + i, pl.ds(at, 8), :] = m[i] - tau * (2.0 * turn[i] + GRAVITY * (rho * er[i]))
            acc[4 + i, pl.ds(at, 8), :] = u[4 + i]
        acc[7, pl.ds(at, 8), :] = u[7] - (tau * GRAVITY) * (m[0] * er[0] + m[1] * er[1] + m[2] * er[2])
        return 0

    lax.fori_loop(0, TALL // 8, one_block, 0)

    ends = {1: 8.0 / 12.0, 2: -1.0 / 12.0}

    def gives(along, across, n, step):
        even = (ends[n] / step * math.cos(n * step)) * along
        odd = (ends[n] / step * math.sin(n * step)) * across
        return even + odd, odd - even

    radius = [1.0 - (SHELLS - 1 - k) * RADIAL_STEP for k in range(SHELLS)]

    def one_field(f, _):
        fr = [radial[f, pl.ds(CT * k, CT), :] for k in range(SHELLS)]
        for k in range(SHELLS):
            here = pl.ds(CT * k, CT)
            ft, fp = polar[f, here, :], azimuth[f, here, :]
            flat = st * fr[k] + ct * ft
            total_t = jnp.zeros((CT, CP), jnp.float32)
            total_p = total_t
            for n in (1, 2):
                before, after = gives(ft, fr[k], n, ht)
                total_t = total_t + jnp.where(row_at < CT - n, pltpu.roll(before, CT - n, 0), 0.0)
                total_t = total_t + jnp.where(row_at >= n, pltpu.roll(after, n, 0), 0.0)
                before, after = gives(fp, flat, n, hp)
                total_p = total_p + jnp.where(lane32 < CP - n, pltpu.roll(before, CP - n, 1), 0.0)
                total_p = total_p + jnp.where(lane32 >= n, pltpu.roll(after, n, 1), 0.0)
            low, high = max(k - 1, 0), min(k + 1, SHELLS - 1)
            slope = (fr[high] - fr[low]) * (1.0 / ((high - low) * RADIAL_STEP))
            whole = slope + (1.0 / radius[k]) * (total_t + total_p / st)
            acc[f, here, :] = acc[f, here, :] - tau * whole
        return 0

    lax.fori_loop(0, FIELDS, one_field, 0)

    pl.when(left)(to_right.wait_recv)
    pl.when(right)(to_left.wait_recv)
    pl.when(up)(to_down.wait_recv)
    pl.when(down)(to_up.wait_recv)

    def ghosts(put, index):
        owner = index // SLOTS
        lane = lax.rem(index, SLOTS)
        for j, (la, ca) in enumerate(others):
            here = owner == la * nc + ca
            for f in range(FIELDS):
                half = slots_in[j, f]
                put(j, f, here, lanes_at(jnp.concatenate([half, half], axis=0), lane))

    @pl.when(edge)
    def _():
        for j in range(9):
            slot_copies[8 - j].wait_recv()

    def row_ghosts(side):
        def put(j, f, here, value):
            row_in[side, f] = jnp.where(here, value, 0.0 if j == 0 else row_in[side, f])

        two = [wanted[0, 0, :, pl.ds(256 * side + 128 * r, 128)] for r in range(2)]
        ghosts(put, jnp.where(sub8 < 4, two[0], two[1]))

    def col_ghosts(side):
        line = jnp.broadcast_to(wanted[0, 0, :, pl.ds(512, 128)], (8, 128))
        index = lanes_at(line, 64 * side + 2 * lax.rem(lane8, CT) + sub8 // 4)
        found = [None] * FIELDS

        def put(j, f, here, value):
            found[f] = jnp.where(here, value, 0.0 if j == 0 else found[f])

        ghosts(put, index)
        for f in range(FIELDS):
            own = jnp.where(lane8 // CT == lax.rem(sub8, 4), found[f], 0.0)
            col_in[side, f, pl.ds(0, 1), :] = jnp.sum(own[0:4], axis=0, keepdims=True)
            col_in[side, f, pl.ds(1, 1), :] = jnp.sum(own[4:8], axis=0, keepdims=True)

    pl.when(c == 0)(lambda: row_ghosts(0))
    pl.when(c == nc - 1)(lambda: row_ghosts(1))
    pl.when(l == 0)(lambda: col_ghosts(0))
    pl.when(l == nl - 1)(lambda: col_ghosts(1))

    def near(n):
        return tau * ends[n]

    shell8 = lax.rem(sub8, 4).astype(jnp.float32)
    inverse_r = 1.0 / (1.0 - (SHELLS - 1 - shell8) * RADIAL_STEP)
    upper = sub8 < 4
    for side in range(2):
        u = [row_in[side, f] for f in range(FIELDS)]
        terms = cell_terms(u)
        if side == 0:
            jobs = ((0, -near(2), -near(1)), (1, 0.0, -near(2)))
        else:
            jobs = ((CT - 1, near(1), near(2)), (CT - 2, near(2), 0.0))
        for row, one_w, two_w in jobs:
            th = angle_t(jnp.full((8, 128), row, jnp.float32))
            s8, c8 = jnp.sin(th), jnp.cos(th)
            scale = jnp.where(upper, one_w / ht, two_w / ht) * inverse_r
            for f, value in enumerate(flux_along(terms, (c8 * cf, c8 * sf, -s8))):
                value = value * scale
                where = pl.ds(row, SHELLS, stride=CT)
                acc[f, where, :] = acc[f, where, :] - (value[0:4] + value[4:8])

    sub4 = lax.broadcasted_iota(jnp.int32, (4, 128), 0)
    lane4 = lax.broadcasted_iota(jnp.int32, (4, 128), 1)
    u = [jnp.concatenate([col_in[0, f], col_in[1, f]], axis=0) for f in range(FIELDS)]
    terms = cell_terms(u)
    th = angle_t(lax.rem(lane4, CT).astype(jnp.float32))
    shell4 = (lane4 // CT).astype(jnp.float32)
    share = 1.0 / ((1.0 - (SHELLS - 1 - shell4) * RADIAL_STEP) * jnp.sin(th) * hp)
    parts = []
    for from_left, from_right, weights in (
        (0, CP - 1, (-near(2), -near(1), near(1), near(2))),
        (1, CP - 2, (0.0, -near(2), near(2), 0.0)),
    ):
        ph = angle_f(jnp.where(sub4 < 2, from_left, from_right).astype(jnp.float32))
        scale = jnp.where(
            sub4 < 2,
            jnp.where(sub4 == 0, weights[0], weights[1]),
            jnp.where(sub4 == 2, weights[2], weights[3]),
        ) * share
        parts.append([v * scale for v in flux_along(terms, (-jnp.sin(ph), jnp.cos(ph), None))])
    lines = []
    for f in range(FIELDS):
        close, far = parts[0][f], parts[1][f]
        lines += [far[2:3] + far[3:4], close[2:3] + close[3:4], close[0:1] + close[1:2], far[0:1] + far[1:2]]
    stood = jnp.concatenate(lines + [jnp.zeros((TALL - 4 * FIELDS, CP), jnp.float32)], axis=0).T
    rim = (lanes < 2) | (lanes >= CP - 2)
    stores = []
    for f in range(FIELDS):
        shift = (CP - 2 - 4 * f) % CP
        acc[f] = acc[f] - jnp.where(rim, pltpu.roll(stood, shift, 1) if shift else stood, 0.0)
        stores.append(pltpu.make_async_copy(acc.at[f], out_hbm.at[f], out_sem.at[f]))
        stores[-1].start()

    for copy, (la, ca) in zip(slot_copies, others):
        pl.when(on_edge(la, ca))(copy.wait_send)
    pl.when(left)(to_left.wait_send)
    pl.when(right)(to_right.wait_send)
    pl.when(up)(to_up.wait_send)
    pl.when(down)(to_down.wait_send)
    for store in stores:
        store.wait()


def body(state_now, send_row, send_col, send_weight, ghost_slot):
    f32, i32 = jnp.float32, jnp.int32
    out = pl.pallas_call(
        kernel,
        out_shape=jax.ShapeDtypeStruct((FIELDS, TALL, CP), f32),
        in_specs=[pl.BlockSpec(memory_space=pl.ANY)] * 5,
        out_specs=pl.BlockSpec(memory_space=pl.ANY),
        scratch_shapes=[
            pltpu.VMEM((FIELDS, TALL, CP), f32),
            pltpu.VMEM((1, 1, 1, SLOTS), i32),
            pltpu.VMEM((1, 1, 1, SLOTS), i32),
            pltpu.VMEM((1, 1, 1, 4, SLOTS), f32),
            pltpu.VMEM((1, 1, 1, 640), i32),
            pltpu.VMEM((FIELDS, SHELLS, SLOTS), f32),
            pltpu.VMEM((9, FIELDS, SHELLS, SLOTS), f32),
            pltpu.VMEM((2, FIELDS, 8, CP), f32),
            pltpu.VMEM((2, FIELDS, 8, CP), f32),
            pltpu.VMEM((2, FIELDS, 2, TALL), f32),
            pltpu.VMEM((2, FIELDS, 2, TALL), f32),
            pltpu.VMEM((FIELDS, TALL, CP), f32),
            pltpu.VMEM((FIELDS, TALL, CP), f32),
            pltpu.VMEM((FIELDS, TALL, CP), f32),
            pltpu.VMEM((FIELDS, TALL, CP), f32),
            pltpu.SemaphoreType.DMA((5,)),
            pltpu.SemaphoreType.DMA((13,)),
            pltpu.SemaphoreType.DMA((13,)),
            pltpu.SemaphoreType.DMA((FIELDS,)),
        ],
        compiler_params=pltpu.CompilerParams(
            collective_id=0, has_side_effects=True, vmem_limit_bytes=32 * 1024 * 1024
        ),
    )(state_now.reshape(FIELDS, TALL, CP), send_row, send_col, send_weight, ghost_slot)
    return out.reshape(1, FIELDS, SHELLS, CT, CP)


def solution(mesh):
    placed = (
        P("panel", None, None, "colat", "lon"),
        P("panel", "lon", "colat", None),
        P("panel", "lon", "colat", None),
        P("panel", "lon", "colat", None, None),
        P("panel", "lon", "colat", None),
    )
    return jax.shard_map(
        body,
        mesh=mesh,
        in_specs=placed,
        out_specs=P("panel", None, None, "colat", "lon"),
        check_vma=False,
    )
```

```python
import math

import jax
import jax.numpy as jnp
from jax import lax
from jax.experimental import pallas as pl
from jax.experimental.pallas import tpu as pltpu
from jax.sharding import PartitionSpec as P

RADIAL_STEP = 0.65 / 511.0
COURANT = 0.3
ROTATION = 300.0
GRAVITY = 300.0
ADIABATIC = 2.0 / 3.0

FIELDS = 8
SHELLS = 4
CT = 32
CP = 128
SLOTS = 128
TALL = SHELLS * CT
MESH = pl.DeviceIdType.MESH
AROUND = [(dl, dc) for dl in (-1, 0, 1) for dc in (-1, 0, 1)]
TURNED = [(0, 1.0), (1, -1.0), (3, 1.0), (2, 1.0), (4, -1.0), (6, 1.0), (5, 1.0), (7, 1.0)]


def lanes_at(values, index):
    return jnp.take_along_axis(values, index, axis=1, mode="promise_in_bounds")


def cell_terms(u):
    rho, m, b, energy = u[0], u[1:4], u[4:7], u[7]
    inverse = 1.0 / rho
    v = [a * inverse for a in m]
    power = b[0] * b[0] + b[1] * b[1] + b[2] * b[2]
    moving = m[0] * v[0] + m[1] * v[1] + m[2] * v[2]
    pressure = ADIABATIC * (energy - 0.5 * moving - 0.5 * power) + 0.5 * power
    aligned = v[0] * b[0] + v[1] * b[1] + v[2] * b[2]
    return m, b, v, pressure, energy + pressure, aligned, rho


def flux_along(terms, e):
    m, b, v, pressure, enthalpy, aligned, rho = terms
    ve = v[0] * e[0] + v[1] * e[1]
    be = b[0] * e[0] + b[1] * e[1]
    if e[2] is not None:
        ve = ve + v[2] * e[2]
        be = be + b[2] * e[2]
    out = [rho * ve]
    for i in range(3):
        term = m[i] * ve - b[i] * be
        out.append(term if e[i] is None else term + pressure * e[i])
    for i in range(3):
        out.append(b[i] * ve - v[i] * be)
    out.append(enthalpy * ve - aligned * be)
    return out


def kernel(
    x_hbm, row_hbm, col_hbm, weight_hbm, ghost_hbm, acc,
    x, rows, cols, weight, wanted,
    slots, slots_in, row_out, row_in, col_out, col_in,
    radial, polar, azimuth,
    in_sem, send_sem, recv_sem,
):
    p, l, c = lax.axis_index("panel"), lax.axis_index("lon"), lax.axis_index("colat")
    nl, nc = lax.axis_size("lon"), lax.axis_size("colat")
    ht = 0.5 * math.pi / (nc * CT)
    hp = 1.5 * math.pi / (nl * CP)
    tau = COURANT / (1.0 / RADIAL_STEP + 1.0 / ht + 1.0 / (hp * math.sin(0.25 * math.pi)))

    def wrap(a, n):
        return lax.rem(a + n, n)

    def on_edge(la, ca):
        return (la == 0) | (la == nl - 1) | (ca == 0) | (ca == nc - 1)

    up, down, left, right = c > 0, c < nc - 1, l > 0, l < nl - 1
    edge = on_edge(l, c)
    others = [(wrap(l + dl, nl), wrap(c + dc, nc)) for dl, dc in AROUND]

    small = [
        pltpu.make_async_copy(src, dst, in_sem.at[FIELDS + i])
        for i, (src, dst) in enumerate(
            ((row_hbm, rows), (col_hbm, cols), (weight_hbm, weight), (ghost_hbm, wanted))
        )
    ]
    large = [pltpu.make_async_copy(x_hbm.at[f], x.at[f], in_sem.at[f]) for f in range(FIELDS)]
    for load in small + large:
        load.start()

    barrier = pltpu.get_barrier_semaphore()

    def greet(device):
        pl.semaphore_signal(barrier, inc=1, device_id=device, device_id_type=MESH)

    @pl.when(edge)
    def _():
        for la, ca in others:
            greet((1 - p, la, ca))

    pl.when(left)(lambda: greet((p, l - 1, c)))
    pl.when(right)(lambda: greet((p, l + 1, c)))
    pl.when(up)(lambda: greet((p, l, c - 1)))
    pl.when(down)(lambda: greet((p, l, c + 1)))

    for load in small:
        load.wait()

    row_at = lax.broadcasted_iota(jnp.int32, (CT, CP), 0)
    lane8 = lax.broadcasted_iota(jnp.int32, (8, 128), 1)
    sub8 = lax.broadcasted_iota(jnp.int32, (8, 128), 0)
    lane32 = lax.broadcasted_iota(jnp.int32, (CT, CP), 1)
    first = row_at == rows[0, 0]
    second = row_at == rows[0, 0] + 1
    w = weight[0, 0, 0]
    on_left = jnp.where(first, w[0:1], jnp.where(second, w[2:3], 0.0))
    on_right = jnp.where(first, w[1:2], jnp.where(second, w[3:4], 0.0))
    pick = jnp.broadcast_to(cols[0, 0], (CT, CP))
    for f in range(FIELDS):
        large[f].wait()
        target, sign = TURNED[f]
        for k in range(SHELLS):
            plane = x[f, CT * k : CT * (k + 1), :]
            mixed = on_left * lanes_at(plane, pick) + on_right * lanes_at(plane, pick + 1)
            slots[target, k : k + 1, :] = sign * jnp.sum(mixed, axis=0, keepdims=True)

    def one(flag):
        return flag.astype(jnp.int32)

    expected = one(up) + one(down) + one(left) + one(right)
    for la, ca in others:
        expected = expected + one(on_edge(la, ca))
    pl.semaphore_wait(barrier, expected)

    def remote(src, dst, i, device):
        return pltpu.make_async_remote_copy(
            src_ref=src, dst_ref=dst, send_sem=send_sem.at[i], recv_sem=recv_sem.at[i],
            device_id=device, device_id_type=MESH,
        )

    slot_copies = [
        pltpu.make_async_remote_copy(
            src_ref=slots, dst_ref=slots_in.at[8 - j], send_sem=send_sem.at[j], recv_sem=recv_sem.at[8 - j],
            device_id=(1 - p, la, ca), device_id_type=MESH,
        )
        for j, (la, ca) in enumerate(others)
    ]
    for copy, (la, ca) in zip(slot_copies, others):
        pl.when(on_edge(la, ca))(copy.start)

    lanes = lax.broadcasted_iota(jnp.int32, (TALL, CP), 1)
    packed = jnp.zeros((TALL, CP), jnp.float32)
    for f in range(FIELDS):
        for r in range(2):
            row_out[0, f, pl.ds(4 * r, 4), :] = x[f, pl.ds(r, SHELLS, stride=CT), :]
            row_out[1, f, pl.ds(4 * r, 4), :] = x[f, pl.ds(CT - 2 + r, SHELLS, stride=CT), :]
        turned = pltpu.roll(x[f], 2 + 4 * f, 1)
        packed = jnp.where(lanes // 4 == f, turned, packed)
    upright = packed.T
    for f in range(FIELDS):
        col_out[1, f] = upright[4 * f : 4 * f + 2]
        col_out[0, f] = upright[4 * f + 2 : 4 * f + 4]

    to_up = remote(row_out.at[0], row_in.at[1], 9, (p, l, c - 1))
    to_down = remote(row_out.at[1], row_in.at[0], 10, (p, l, c + 1))
    to_left = remote(col_out.at[0], col_in.at[1], 11, (p, l - 1, c))
    to_right = remote(col_out.at[1], col_in.at[0], 12, (p, l + 1, c))
    pl.when(left)(to_left.start)
    pl.when(right)(to_right.start)
    pl.when(up)(to_up.start)
    pl.when(down)(to_down.start)

    row0 = (c * CT).astype(jnp.float32) + 0.5
    col0 = (l * CP).astype(jnp.float32) + 0.5

    def angle_t(row):
        return 0.25 * math.pi + (row + row0) * ht

    def angle_f(col):
        return -0.75 * math.pi + (col + col0) * hp

    theta = angle_t(row_at.astype(jnp.float32))
    phi = angle_f(lane8[0:1].astype(jnp.float32))
    st, ct = jnp.sin(theta), jnp.cos(theta)
    sf = jnp.broadcast_to(jnp.sin(phi), (8, CP))
    cf = jnp.broadcast_to(jnp.cos(phi), (8, CP))
    spin_second = ROTATION * p.astype(jnp.float32)
    spin_third = ROTATION - spin_second

    def one_block(n, _):
        at = pl.multiple_of(n * 8, 8)
        th = angle_t((sub8 + lax.rem(n, CT // 8) * 8).astype(jnp.float32))
        s8, c8 = jnp.sin(th), jnp.cos(th)
        u = [x[f, pl.ds(at, 8), :] for f in range(FIELDS)]
        terms = cell_terms(u)
        er = (s8 * cf, s8 * sf, c8)
        for f, value in enumerate(flux_along(terms, er)):
            radial[f, pl.ds(at, 8), :] = value
        for f, value in enumerate(flux_along(terms, (c8 * cf, c8 * sf, -s8))):
            polar[f, pl.ds(at, 8), :] = value
        for f, value in enumerate(flux_along(terms, (-sf, cf, None))):
            azimuth[f, pl.ds(at, 8), :] = value
        rho, m = u[0], u[1:4]
        turn = (
            spin_second * m[2] - spin_third * m[1], spin_third * m[0], -spin_second * m[0]
        )
        acc[0, pl.ds(at, 8), :] = u[0]
        for i in range(3):
            acc[1 + i, pl.ds(at, 8), :] = m[i] - tau * (2.0 * turn[i] + GRAVITY * (rho * er[i]))
            acc[4 + i, pl.ds(at, 8), :] = u[4 + i]
        acc[7, pl.ds(at, 8), :] = u[7] - (tau * GRAVITY) * (m[0] * er[0] + m[1] * er[1] + m[2] * er[2])
        return 0

    lax.fori_loop(0, TALL // 8, one_block, 0)

    ends = {1: 8.0 / 12.0, 2: -1.0 / 12.0}

    def gives(along, across, n, step):
        even = (ends[n] / step * math.cos(n * step)) * along
        odd = (ends[n] / step * math.sin(n * step)) * across
        return even + odd, odd - even

    radius = [1.0 - (SHELLS - 1 - k) * RADIAL_STEP for k in range(SHELLS)]

    def one_field(f, _):
        fr = [radial[f, pl.ds(CT * k, CT), :] for k in range(SHELLS)]
        for k in range(SHELLS):
            here = pl.ds(CT * k, CT)
            ft, fp = polar[f, here, :], azimuth[f, here, :]
            flat = st * fr[k] + ct * ft
            total_t = jnp.zeros((CT, CP), jnp.float32)
            total_p = total_t
            for n in (1, 2):
                before, after = gives(ft, fr[k], n, ht)
                total_t = total_t + jnp.where(row_at < CT - n, pltpu.roll(before, CT - n, 0), 0.0)
                total_t = total_t + jnp.where(row_at >= n, pltpu.roll(after, n, 0), 0.0)
                before, after = gives(fp, flat, n, hp)
                total_p = total_p + jnp.where(lane32 < CP - n, pltpu.roll(before, CP - n, 1), 0.0)
                total_p = total_p + jnp.where(lane32 >= n, pltpu.roll(after, n, 1), 0.0)
            low, high = max(k - 1, 0), min(k + 1, SHELLS - 1)
            slope = (fr[high] - fr[low]) * (1.0 / ((high - low) * RADIAL_STEP))
            whole = slope + (1.0 / radius[k]) * (total_t + total_p / st)
            acc[f, here, :] = acc[f, here, :] - tau * whole
        return 0

    lax.fori_loop(0, FIELDS, one_field, 0)

    def near(n):
        return tau * ends[n]

    shell8 = lax.rem(sub8, 4).astype(jnp.float32)
    inverse_r = 1.0 / ((1.0 - (SHELLS - 1 - shell8) * RADIAL_STEP) * ht)
    upper = sub8 < 4

    def add_rows(side):
        u = [row_in[side, f] for f in range(FIELDS)]
        terms = cell_terms(u)
        if side == 0:
            jobs = ((0, -near(2), -near(1)), (1, 0.0, -near(2)))
        else:
            jobs = ((CT - 1, near(1), near(2)), (CT - 2, near(2), 0.0))
        for row, one_w, two_w in jobs:
            th = angle_t(jnp.full((8, 128), row, jnp.float32))
            s8, c8 = jnp.sin(th), jnp.cos(th)
            scale = jnp.where(upper, one_w, two_w) * inverse_r
            where = pl.ds(row, SHELLS, stride=CT)
            for f, value in enumerate(flux_along(terms, (c8 * cf, c8 * sf, -s8))):
                value = value * scale
                acc[f, where, :] = acc[f, where, :] - (value[0:4] + value[4:8])

    rim = (lanes < 2) | (lanes >= CP - 2)

    def add_columns():
        sub4 = lax.broadcasted_iota(jnp.int32, (4, 128), 0)
        lane4 = lax.broadcasted_iota(jnp.int32, (4, 128), 1)
        u = [jnp.concatenate([col_in[0, f], col_in[1, f]], axis=0) for f in range(FIELDS)]
        terms = cell_terms(u)
        th = angle_t(lax.rem(lane4, CT).astype(jnp.float32))
        shell4 = (lane4 // CT).astype(jnp.float32)
        share = 1.0 / ((1.0 - (SHELLS - 1 - shell4) * RADIAL_STEP) * jnp.sin(th) * hp)
        parts = []
        for from_left, from_right, weights in (
            (0, CP - 1, (-near(2), -near(1), near(1), near(2))),
            (1, CP - 2, (0.0, -near(2), near(2), 0.0)),
        ):
            ph = angle_f(jnp.where(sub4 < 2, from_left, from_right).astype(jnp.float32))
            scale = jnp.where(
                sub4 < 2,
                jnp.where(sub4 == 0, weights[0], weights[1]),
                jnp.where(sub4 == 2, weights[2], weights[3]),
            ) * share
            parts.append([v * scale for v in flux_along(terms, (-jnp.sin(ph), jnp.cos(ph), None))])
        lines = []
        for f in range(FIELDS):
            close, far = parts[0][f], parts[1][f]
            lines += [far[2:3] + far[3:4], close[2:3] + close[3:4], close[0:1] + close[1:2], far[0:1] + far[1:2]]
        stood = jnp.concatenate(lines + [jnp.zeros((TALL - 4 * FIELDS, CP), jnp.float32)], axis=0).T
        for f in range(FIELDS):
            shift = (CP - 2 - 4 * f) % CP
            acc[f] = acc[f] - jnp.where(rim, pltpu.roll(stood, shift, 1) if shift else stood, 0.0)

    def ghosts(index, put):
        owner = index // SLOTS
        lane = lax.rem(index, SLOTS)
        here = [owner == la * nc + ca for la, ca in others]

        def one_field(f, _):
            found = jnp.zeros((8, 128), jnp.float32)
            for j in range(9):
                half = slots_in[j, f]
                found = jnp.where(here[j], lanes_at(jnp.concatenate([half, half], axis=0), lane), found)
            put(f, found)
            return 0

        lax.fori_loop(0, FIELDS, one_field, 0)

    def row_ghosts(side):
        def put(f, found):
            row_in[side, f] = found

        two = [wanted[0, 0, :, pl.ds(256 * side + 128 * r, 128)] for r in range(2)]
        ghosts(jnp.where(sub8 < 4, two[0], two[1]), put)

    def column_ghosts(side):
        def put(f, found):
            own = jnp.where(lane8 // CT == lax.rem(sub8, 4), found, 0.0)
            col_in[side, f, pl.ds(0, 1), :] = jnp.sum(own[0:4], axis=0, keepdims=True)
            col_in[side, f, pl.ds(1, 1), :] = jnp.sum(own[4:8], axis=0, keepdims=True)

        line = jnp.broadcast_to(wanted[0, 0, :, pl.ds(512, 128)], (8, 128))
        ghosts(lanes_at(line, 64 * side + 2 * lax.rem(lane8, CT) + sub8 // 4), put)

    pl.when(left)(to_right.wait_recv)
    pl.when(right)(to_left.wait_recv)
    pl.when(left & right)(add_columns)

    @pl.when(up)
    def _():
        to_down.wait_recv()
        add_rows(0)

    @pl.when(down)
    def _():
        to_up.wait_recv()
        add_rows(1)

    @pl.when(edge)
    def _():
        for j in range(9):
            slot_copies[8 - j].wait_recv()

    pl.when(l == 0)(lambda: column_ghosts(0))
    pl.when(l == nl - 1)(lambda: column_ghosts(1))
    pl.when((l == 0) | (l == nl - 1))(add_columns)

    @pl.when(c == 0)
    def _():
        row_ghosts(0)
        add_rows(0)

    @pl.when(c == nc - 1)
    def _():
        row_ghosts(1)
        add_rows(1)

    for copy, (la, ca) in zip(slot_copies, others):
        pl.when(on_edge(la, ca))(copy.wait_send)
    pl.when(left)(to_left.wait_send)
    pl.when(right)(to_right.wait_send)
    pl.when(up)(to_up.wait_send)
    pl.when(down)(to_down.wait_send)


def body(state_now, send_row, send_col, send_weight, ghost_slot):
    f32, i32 = jnp.float32, jnp.int32
    out = pl.pallas_call(
        kernel,
        out_shape=pltpu.VMEM((FIELDS, TALL, CP), f32),
        in_specs=[pl.BlockSpec(memory_space=pltpu.HBM)] * 5,
        out_specs=pl.BlockSpec(memory_space=pltpu.VMEM),
        scratch_shapes=[
            pltpu.VMEM((FIELDS, TALL, CP), f32),
            pltpu.VMEM((1, 1, 1, SLOTS), i32),
            pltpu.VMEM((1, 1, 1, SLOTS), i32),
            pltpu.VMEM((1, 1, 1, 4, SLOTS), f32),
            pltpu.VMEM((1, 1, 1, 640), i32),
            pltpu.VMEM((FIELDS, SHELLS, SLOTS), f32),
            pltpu.VMEM((9, FIELDS, SHELLS, SLOTS), f32),
            pltpu.VMEM((2, FIELDS, 8, CP), f32),
            pltpu.VMEM((2, FIELDS, 8, CP), f32),
            pltpu.VMEM((2, FIELDS, 2, TALL), f32),
            pltpu.VMEM((2, FIELDS, 2, TALL), f32),
            pltpu.VMEM((FIELDS, TALL, CP), f32),
            pltpu.VMEM((FIELDS, TALL, CP), f32),
            pltpu.VMEM((FIELDS, TALL, CP), f32),
            pltpu.SemaphoreType.DMA((12,)),
            pltpu.SemaphoreType.DMA((13,)),
            pltpu.SemaphoreType.DMA((13,)),
        ],
        compiler_params=pltpu.CompilerParams(
            collective_id=0, has_side_effects=True, vmem_limit_bytes=32 * 1024 * 1024
        ),
    )(*[pltpu.with_memory_space_constraint(a, pltpu.HBM) for a in (state_now.reshape(FIELDS, TALL, CP), send_row, send_col, send_weight, ghost_slot)])
    return out.reshape(1, FIELDS, SHELLS, CT, CP)


def solution(mesh):
    placed = (
        P("panel", None, None, "colat", "lon"),
        P("panel", "lon", "colat", None),
        P("panel", "lon", "colat", None),
        P("panel", "lon", "colat", None, None),
        P("panel", "lon", "colat", None),
    )
    return jax.shard_map(
        body,
        mesh=mesh,
        in_specs=placed,
        out_specs=P("panel", None, None, "colat", "lon"),
        check_vma=False,
    )
```

```python
import math

import jax
import jax.numpy as jnp
from jax import lax
from jax.experimental import pallas as pl
from jax.experimental.pallas import tpu as pltpu
from jax.sharding import PartitionSpec as P

RADIAL_STEP = 0.65 / 511.0
COURANT = 0.3
ROTATION = 300.0
GRAVITY = 300.0
ADIABATIC = 2.0 / 3.0

FIELDS = 8
SHELLS = 4
CT = 32
CP = 128
SLOTS = 128
TALL = SHELLS * CT
MESH = pl.DeviceIdType.MESH
RUN = 8
AROUND = [(dl, dc) for dl in (-1, 0, 1) for dc in (-1, 0, 1)]
TURNED = [(0, 1.0), (1, -1.0), (3, 1.0), (2, 1.0), (4, -1.0), (6, 1.0), (5, 1.0), (7, 1.0)]


def lanes_at(values, index):
    return jnp.take_along_axis(values, index, axis=1, mode="promise_in_bounds")


def cell_terms(u):
    rho, m, b, energy = u[0], u[1:4], u[4:7], u[7]
    inverse = 1.0 / rho
    v = [a * inverse for a in m]
    power = b[0] * b[0] + b[1] * b[1] + b[2] * b[2]
    moving = m[0] * v[0] + m[1] * v[1] + m[2] * v[2]
    pressure = ADIABATIC * (energy - 0.5 * moving - 0.5 * power) + 0.5 * power
    aligned = v[0] * b[0] + v[1] * b[1] + v[2] * b[2]
    return m, b, v, pressure, energy + pressure, aligned, rho


def flux_along(terms, e):
    m, b, v, pressure, enthalpy, aligned, rho = terms
    ve = v[0] * e[0] + v[1] * e[1]
    be = b[0] * e[0] + b[1] * e[1]
    if e[2] is not None:
        ve = ve + v[2] * e[2]
        be = be + b[2] * e[2]
    out = [rho * ve]
    for i in range(3):
        term = m[i] * ve - b[i] * be
        out.append(term if e[i] is None else term + pressure * e[i])
    for i in range(3):
        out.append(b[i] * ve - v[i] * be)
    out.append(enthalpy * ve - aligned * be)
    return out


def kernel(
    x_hbm, row_hbm, col_hbm, weight_hbm, ghost_hbm, acc,
    x, rows, cols, weight, wanted,
    slots, slots_in, row_out, row_in, col_out, col_in,
    radial, polar, azimuth, picked, named,
    in_sem, send_sem, recv_sem, told,
):
    p, l, c = lax.axis_index("panel"), lax.axis_index("lon"), lax.axis_index("colat")
    nl, nc = lax.axis_size("lon"), lax.axis_size("colat")
    ht = 0.5 * math.pi / (nc * CT)
    hp = 1.5 * math.pi / (nl * CP)
    tau = COURANT / (1.0 / RADIAL_STEP + 1.0 / ht + 1.0 / (hp * math.sin(0.25 * math.pi)))

    def wrap(a, n):
        return lax.rem(a + n, n)

    def on_row(ca):
        return (ca == 0) | (ca == nc - 1)

    def on_edge(la, ca):
        return (la == 0) | (la == nl - 1) | on_row(ca)

    small = [
        pltpu.make_async_copy(src, dst, in_sem.at[FIELDS + i])
        for i, (src, dst) in enumerate(
            ((row_hbm, rows), (col_hbm, cols), (weight_hbm, weight), (ghost_hbm, wanted))
        )
    ]
    large = [pltpu.make_async_copy(x_hbm.at[f], x.at[f], in_sem.at[f]) for f in range(FIELDS)]
    for load in small + large:
        load.start()

    up, down, left, right = c > 0, c < nc - 1, l > 0, l < nl - 1
    edge = on_edge(l, c)
    others = [(wrap(l + dl, nl), wrap(c + dc, nc)) for dl, dc in AROUND]

    late = 4
    place = lax.rem(l, RUN)

    def passed(panel, tile, la):
        far = (panel == 1) | ((lax.rem(tile, RUN) >= late) & (lax.rem(la, RUN) != RUN - 1))
        return far & (tile // RUN == la // RUN)

    flows_out, direct_in, shut_out, shut_in = [], [], [], []
    to_panel_1 = p == 0
    for (la, ca), (dl, dc) in zip(others, AROUND):
        flow, got = on_edge(la, ca), edge
        if dl:
            flow = flow & ~(on_row(ca) & passed(1 - p, la, l))
            got = got & ~(on_row(c) & passed(p, l, la))
        if dc != 1:
            flow = flow & ~((p == 1) & (la == 0) & (lax.rem(ca, 2) == 0))
        if dc != -1:
            got = got & ~((p == 0) & (l == 0) & (lax.rem(c, 2) == 0))
        flows_out.append(flow)
        direct_in.append(got)
        shut_out.append((p == 1) & (((place == RUN - 1) & (dl <= 0)) | ((place == 0) & (dl == -1))))
        shut_in.append((p == 0) & (((place == RUN - 1) & (dl >= 0)) | ((place == RUN - 2) & (dl == 1))))
    row_edge = on_row(c)
    take_left, take_right = row_edge & left & passed(p, l, l - 1), row_edge & right & passed(p, l, l + 1)
    pass_left, pass_right = row_edge & left & passed(p, l - 1, l), row_edge & right & passed(p, l + 1, l)
    mate_gives = (p == 0) & (l == 0) & (lax.rem(c, 2) == 1)
    mate_takes = (p == 0) & (l == 0) & (lax.rem(c, 2) == 0)

    inner = jnp.clip(c, 2, nc - 3)
    at_seam = (place == 0) | (place == RUN - 1)
    at_end = (l == 0) | (l == nl - 1)
    beside = (c < 2) | (c >= nc - 2)
    helped_1 = (p == 1) & at_seam & (beside | at_end)
    helped_0 = (p == 0) & (place == RUN - 1) & (beside | at_end)
    at_helper = (c == 2) | (c == nc - 3)
    helper_1 = (p == 1) & at_seam & ~at_end & at_helper
    helper_0 = (p == 0) & (place == RUN - 1) & ~at_end & at_helper
    end_helper = (l == nl - 2) & ~beside
    over_left, over_right = left & (place == 0), right & (place == RUN - 1)
    seam_by_help = helped_1 & ~at_end
    near_left, near_right = left & ~(over_left & seam_by_help), right & ~(over_right & seam_by_help)

    barrier = pltpu.get_barrier_semaphore()

    def greet(*device):
        pl.semaphore_signal(barrier, inc=1, device_id=device, device_id_type=MESH)

    for j, (la, ca) in enumerate(others):
        by_help = (p == 1) & (lax.rem(la, RUN) == RUN - 1)
        to_l = jnp.where(by_help & (la == nl - 1), nl - 2, la)
        to_c = jnp.where(by_help, jnp.clip(ca, 2, nc - 3), ca)
        pl.when(direct_in[j] & ~shut_in[j])(lambda: greet(1 - p, to_l, to_c))

    pl.when(near_left)(lambda: greet(p, l - 1, c))
    pl.when(near_right)(lambda: greet(p, l + 1, c))
    pl.when(up)(lambda: greet(p, l, c - 1))
    pl.when(down)(lambda: greet(p, l, c + 1))

    @pl.when(helped_0 | helped_1)
    def _():
        greet(p, jnp.where(at_end, nl - 2, l), inner)
        pl.when(seam_by_help)(lambda: greet(p, jnp.where(place == 0, l - 1, l + 1), inner))

    @pl.when((p == 0) & (l < nl - 1) & row_edge & (place >= RUN - 2))
    def _():
        end = l == nl - 2
        last = jnp.where(end, l, l - place + RUN - 1)
        for helper in (2, nc - 3):
            greet(1, last, helper)
            pl.when(place == RUN - 1)(lambda: greet(1, l + 1, helper))

    @pl.when((p == 0) & (l == nl - 1))
    def _():
        for helper in range(2, nc - 2):
            reach = (c >= helper - 1) & (c <= helper + 1)
            if helper == 2:
                reach = (c <= helper + 1) | (c == nc - 1)
            if helper == nc - 3:
                reach = (c >= helper - 1) | (c == 0)
            pl.when(reach)(lambda: greet(1, nl - 2, helper))

    for load in small:
        load.wait()

    row_at = lax.broadcasted_iota(jnp.int32, (CT, CP), 0)
    lane8 = lax.broadcasted_iota(jnp.int32, (8, 128), 1)
    sub8 = lax.broadcasted_iota(jnp.int32, (8, 128), 0)
    lane32 = lax.broadcasted_iota(jnp.int32, (CT, CP), 1)
    first = row_at == rows[0, 0]
    second = row_at == rows[0, 0] + 1
    w = weight[0, 0, 0]
    on_left = jnp.where(first, w[0:1], jnp.where(second, w[2:3], 0.0))
    on_right = jnp.where(first, w[1:2], jnp.where(second, w[3:4], 0.0))
    pick = jnp.broadcast_to(cols[0, 0], (CT, CP))
    for f in range(FIELDS):
        large[f].wait()
        target, sign = TURNED[f]
        for k in range(SHELLS):
            plane = x[f, CT * k : CT * (k + 1), :]
            mixed = on_left * lanes_at(plane, pick) + on_right * lanes_at(plane, pick + 1)
            slots[target, k : k + 1, :] = sign * jnp.sum(mixed, axis=0, keepdims=True)

    def one(flag):
        return flag.astype(jnp.int32)

    expected = one(up) + one(down) + one(near_left) + one(near_right)
    for flow, shut in zip(flows_out, shut_out):
        expected = expected + one(flow & ~shut & ~helped_0)
    expected = expected + one(helper_1) * (6 + 2 * one(place == RUN - 1)) + 8 * one(helper_0)
    served = jnp.where(at_helper, 3, 1)
    at_panel_1 = 2 * served + jnp.where(at_helper, 7, 3)
    expected = expected + one(end_helper) * jnp.where(p == 1, at_panel_1, 7 * served)
    pl.semaphore_wait(barrier, expected)

    def remote(src, dst, i, *device):
        return pltpu.make_async_remote_copy(
            src_ref=src, dst_ref=dst, send_sem=send_sem.at[i], recv_sem=recv_sem.at[i],
            device_id=device, device_id_type=MESH,
        )

    slot_copies = [
        pltpu.make_async_remote_copy(
            src_ref=slots, dst_ref=slots_in.at[8 - j], send_sem=send_sem.at[j], recv_sem=recv_sem.at[8 - j],
            device_id=(1 - p, la, ca), device_id_type=MESH,
        )
        for j, (la, ca) in enumerate(others)
    ]

    def send_slots(wave):
        for j, (la, ca) in enumerate(others):
            spot = lax.rem(la, RUN)
            turn = jnp.where(p == 0, 0, jnp.where(spot == 0, 0, jnp.where(spot < 3, 0, jnp.where(spot < 5, 0, 0))))
            pl.when(flows_out[j] & ~shut_out[j] & ~helped_0 & (turn == wave))(slot_copies[j].start)

    send_slots(0)

    def tell(*device):
        pl.semaphore_signal(told, inc=1, device_id=device, device_id_type=MESH)

    @pl.when(helper_0 | helper_1)
    def _():
        first = jnp.where(c == 2, 0, nc - 2)
        tell(p, l, first)
        tell(p, l, first + 1)

    @pl.when(end_helper)
    def _():
        tell(p, nl - 1, c)
        pl.when(p == 1)(lambda: tell(p, 0, c))

        @pl.when(at_helper)
        def _():
            first = jnp.where(c == 2, 0, nc - 2)
            for more in range(2):
                tell(p, nl - 1, first + more)
                pl.when(p == 1)(lambda: tell(p, 0, first + more))

    lanes = lax.broadcasted_iota(jnp.int32, (TALL, CP), 1)
    packed = jnp.zeros((TALL, CP), jnp.float32)
    for f in range(FIELDS):
        for r in range(2):
            row_out[0, f, pl.ds(4 * r, 4), :] = x[f, pl.ds(r, SHELLS, stride=CT), :]
            row_out[1, f, pl.ds(4 * r, 4), :] = x[f, pl.ds(CT - 2 + r, SHELLS, stride=CT), :]
        turned = pltpu.roll(x[f], 2 + 4 * f, 1)
        packed = jnp.where(lanes // 4 == f, turned, packed)
    upright = packed.T
    for f in range(FIELDS):
        col_out[1, f] = upright[4 * f : 4 * f + 2]
        col_out[0, f] = upright[4 * f + 2 : 4 * f + 4]

    to_up = remote(row_out.at[0], row_in.at[1], 9, p, l, c - 1)
    to_down = remote(row_out.at[1], row_in.at[0], 10, p, l, c + 1)
    to_left = remote(col_out.at[0], col_in.at[1], 11, p, l - 1, c)
    to_right = remote(col_out.at[1], col_in.at[0], 12, p, l + 1, c)
    pl.when(near_left)(to_left.start)
    pl.when(near_right)(to_right.start)
    pl.when(up)(to_up.start)
    pl.when(down)(to_down.start)

    row0 = (c * CT).astype(jnp.float32) + 0.5
    col0 = (l * CP).astype(jnp.float32) + 0.5

    def angle_t(row):
        return 0.25 * math.pi + (row + row0) * ht

    def angle_f(col):
        return -0.75 * math.pi + (col + col0) * hp

    theta = angle_t(row_at.astype(jnp.float32))
    phi = angle_f(lane8[0:1].astype(jnp.float32))
    st, ct = jnp.sin(theta), jnp.cos(theta)
    sf = jnp.broadcast_to(jnp.sin(phi), (8, CP))
    cf = jnp.broadcast_to(jnp.cos(phi), (8, CP))
    spin_second = ROTATION * p.astype(jnp.float32)
    spin_third = ROTATION - spin_second

    def one_block(n, _):
        at = pl.multiple_of(n * 8, 8)
        th = angle_t((sub8 + lax.rem(n, CT // 8) * 8).astype(jnp.float32))
        s8, c8 = jnp.sin(th), jnp.cos(th)
        u = [x[f, pl.ds(at, 8), :] for f in range(FIELDS)]
        terms = cell_terms(u)
        er = (s8 * cf, s8 * sf, c8)
        for f, value in enumerate(flux_along(terms, er)):
            radial[f, pl.ds(at, 8), :] = value
        for f, value in enumerate(flux_along(terms, (c8 * cf, c8 * sf, -s8))):
            polar[f, pl.ds(at, 8), :] = value
        for f, value in enumerate(flux_along(terms, (-sf, cf, None))):
            azimuth[f, pl.ds(at, 8), :] = value
        rho, m = u[0], u[1:4]
        turn = (
            spin_second * m[2] - spin_third * m[1], spin_third * m[0], -spin_second * m[0]
        )
        acc[0, pl.ds(at, 8), :] = u[0]
        for i in range(3):
            acc[1 + i, pl.ds(at, 8), :] = m[i] - tau * (2.0 * turn[i] + GRAVITY * (rho * er[i]))
            acc[4 + i, pl.ds(at, 8), :] = u[4 + i]
        acc[7, pl.ds(at, 8), :] = u[7] - (tau * GRAVITY) * (m[0] * er[0] + m[1] * er[1] + m[2] * er[2])
        return 0

    lax.fori_loop(0, TALL // 8, one_block, 0)

    ends = {1: 8.0 / 12.0, 2: -1.0 / 12.0}

    def gives(along, across, n, step):
        even = (ends[n] / step * math.cos(n * step)) * along
        odd = (ends[n] / step * math.sin(n * step)) * across
        return even + odd, odd - even

    radius = [1.0 - (SHELLS - 1 - k) * RADIAL_STEP for k in range(SHELLS)]

    def one_field(f, _):
        fr = [radial[f, pl.ds(CT * k, CT), :] for k in range(SHELLS)]
        for k in range(SHELLS):
            here = pl.ds(CT * k, CT)
            ft, fp = polar[f, here, :], azimuth[f, here, :]
            flat = st * fr[k] + ct * ft
            total_t = jnp.zeros((CT, CP), jnp.float32)
            total_p = total_t
            for n in (1, 2):
                before, after = gives(ft, fr[k], n, ht)
                total_t = total_t + jnp.where(row_at < CT - n, pltpu.roll(before, CT - n, 0), 0.0)
                total_t = total_t + jnp.where(row_at >= n, pltpu.roll(after, n, 0), 0.0)
                before, after = gives(fp, flat, n, hp)
                total_p = total_p + jnp.where(lane32 < CP - n, pltpu.roll(before, CP - n, 1), 0.0)
                total_p = total_p + jnp.where(lane32 >= n, pltpu.roll(after, n, 1), 0.0)
            low, high = max(k - 1, 0), min(k + 1, SHELLS - 1)
            slope = (fr[high] - fr[low]) * (1.0 / ((high - low) * RADIAL_STEP))
            whole = slope + (1.0 / radius[k]) * (total_t + total_p / st)
            acc[f, here, :] = acc[f, here, :] - tau * whole
        return 0

    lax.fori_loop(0, FIELDS, one_field, 0)

    @pl.when(helped_0 | helped_1)
    def _():
        pl.semaphore_wait(told, 1)
        pl.when(over_left & seam_by_help)(to_left.start)
        pl.when(over_right & seam_by_help)(to_right.start)
        for j in range(9):
            pl.when(flows_out[j] & (shut_out[j] | helped_0))(slot_copies[j].start)

    def near(n):
        return tau * ends[n]

    shell8 = lax.rem(sub8, 4).astype(jnp.float32)
    inverse_r = 1.0 / ((1.0 - (SHELLS - 1 - shell8) * RADIAL_STEP) * ht)
    upper = sub8 < 4

    def add_rows(side, rim):
        u = [rim[f] for f in range(FIELDS)]
        terms = cell_terms(u)
        if side == 0:
            jobs = ((0, -near(2), -near(1)), (1, 0.0, -near(2)))
        else:
            jobs = ((CT - 1, near(1), near(2)), (CT - 2, near(2), 0.0))
        for row, one_w, two_w in jobs:
            th = angle_t(jnp.full((8, 128), row, jnp.float32))
            s8, c8 = jnp.sin(th), jnp.cos(th)
            scale = jnp.where(upper, one_w, two_w) * inverse_r
            where = pl.ds(row, SHELLS, stride=CT)
            for f, value in enumerate(flux_along(terms, (c8 * cf, c8 * sf, -s8))):
                value = value * scale
                acc[f, where, :] = acc[f, where, :] - (value[0:4] + value[4:8])

    rim = (lanes < 2) | (lanes >= CP - 2)

    def add_columns():
        sub4 = lax.broadcasted_iota(jnp.int32, (4, 128), 0)
        lane4 = lax.broadcasted_iota(jnp.int32, (4, 128), 1)
        u = [jnp.concatenate([col_in[0, f], col_in[1, f]], axis=0) for f in range(FIELDS)]
        terms = cell_terms(u)
        th = angle_t(lax.rem(lane4, CT).astype(jnp.float32))
        shell4 = (lane4 // CT).astype(jnp.float32)
        share = 1.0 / ((1.0 - (SHELLS - 1 - shell4) * RADIAL_STEP) * jnp.sin(th) * hp)
        parts = []
        for from_left, from_right, weights in (
            (0, CP - 1, (-near(2), -near(1), near(1), near(2))),
            (1, CP - 2, (0.0, -near(2), near(2), 0.0)),
        ):
            ph = angle_f(jnp.where(sub4 < 2, from_left, from_right).astype(jnp.float32))
            scale = jnp.where(
                sub4 < 2,
                jnp.where(sub4 == 0, weights[0], weights[1]),
                jnp.where(sub4 == 2, weights[2], weights[3]),
            ) * share
            parts.append([v * scale for v in flux_along(terms, (-jnp.sin(ph), jnp.cos(ph), None))])
        lines = []
        for f in range(FIELDS):
            close, far = parts[0][f], parts[1][f]
            lines += [far[2:3] + far[3:4], close[2:3] + close[3:4], close[0:1] + close[1:2], far[0:1] + far[1:2]]
        stood = jnp.concatenate(lines + [jnp.zeros((TALL - 4 * FIELDS, CP), jnp.float32)], axis=0).T
        for f in range(FIELDS):
            shift = (CP - 2 - 4 * f) % CP
            acc[f] = acc[f] - jnp.where(rim, pltpu.roll(stood, shift, 1) if shift else stood, 0.0)

    pl.when(left)(to_right.wait_recv)
    pl.when(right)(to_left.wait_recv)
    pl.when(left & right)(add_columns)

    @pl.when(up)
    def _():
        to_down.wait_recv()
        add_rows(0, row_in.at[0])

    @pl.when(down)
    def _():
        to_up.wait_recv()
        add_rows(1, row_in.at[1])

    def name_row(side):
        two = [wanted[0, 0, :, pl.ds(256 * side + 128 * r, 128)] for r in range(2)]
        named[0] = jnp.where(sub8 < 4, two[0], two[1])

    def name_column(side):
        line = jnp.broadcast_to(wanted[0, 0, :, pl.ds(512, 128)], (8, 128))
        named[1] = lanes_at(line, 64 * side + 2 * lax.rem(lane8, CT) + sub8 // 4)

    pl.when(c == 0)(lambda: name_row(0))
    pl.when(c == nc - 1)(lambda: name_row(1))
    pl.when(l == 0)(lambda: name_column(0))
    pl.when(l == nl - 1)(lambda: name_column(1))

    def pick_ghosts(kind, group, fresh):
        index = named[kind]
        owner = index // SLOTS
        lane = lax.rem(index, SLOTS)
        three = range(3 * group, 3 * group + 3)
        here = [owner == others[j][0] * nc + others[j][1] for j in three]

        def one_field(f, _):
            found = jnp.zeros((8, 128), jnp.float32) if fresh else picked[kind, f]
            for mine, j in zip(here, three):
                half = slots_in[j, f]
                found = jnp.where(mine, lanes_at(jnp.concatenate([half, half], axis=0), lane), found)
            picked[kind, f] = found
            return 0

        lax.fori_loop(0, FIELDS, one_field, 0)

    pass_on = [
        remote(slots_in.at[3:6], slots_in.at[6:9], 13, p, l - 1, c),
        remote(slots_in.at[3:6], slots_in.at[0:3], 14, p, l + 1, c),
    ]
    to_mate = [
        remote(slots_in.at[3 * group : 3 * group + 2], slots_in.at[3 * group + 1 : 3 * group + 3], 15 + group, p, l, c - 1)
        for group in range(3)
    ]
    for turn, group in enumerate((1, 0, 2)):
        for j in range(3 * group, 3 * group + 3):
            pl.when(direct_in[j])(slot_copies[8 - j].wait_recv)
        if group == 0:
            pl.when(take_left)(pass_on[1].wait_recv)
        if group == 1:
            pl.when(pass_left)(pass_on[0].start)
            pl.when(pass_right)(pass_on[1].start)
        if group == 2:
            pl.when(take_right)(pass_on[0].wait_recv)
        pl.when(mate_gives)(to_mate[group].start)
        pl.when(mate_takes)(to_mate[group].wait_recv)
        pl.when(row_edge)(lambda: pick_ghosts(0, group, turn == 0))
        pl.when(at_end)(lambda: pick_ghosts(1, group, turn == 0))

    @pl.when(at_end)
    def _():
        side = jnp.where(l == 0, 0, 1)
        for f in range(FIELDS):
            own = jnp.where(lane8 // CT == lax.rem(sub8, 4), picked[1, f], 0.0)
            col_in[side, f, pl.ds(0, 1), :] = jnp.sum(own[0:4], axis=0, keepdims=True)
            col_in[side, f, pl.ds(1, 1), :] = jnp.sum(own[4:8], axis=0, keepdims=True)
        add_columns()

    pl.when(c == 0)(lambda: add_rows(0, picked.at[0]))
    pl.when(c == nc - 1)(lambda: add_rows(1, picked.at[0]))

    for j in range(9):
        pl.when(flows_out[j])(slot_copies[j].wait_send)
    pl.when(pass_left)(pass_on[0].wait_send)
    pl.when(pass_right)(pass_on[1].wait_send)
    for copy in to_mate:
        pl.when(mate_gives)(copy.wait_send)
    pl.when(left)(to_left.wait_send)
    pl.when(right)(to_right.wait_send)
    pl.when(up)(to_up.wait_send)
    pl.when(down)(to_down.wait_send)


def body(state_now, send_row, send_col, send_weight, ghost_slot):
    f32, i32 = jnp.float32, jnp.int32
    out = pl.pallas_call(
        kernel,
        out_shape=pltpu.VMEM((FIELDS, TALL, CP), f32),
        in_specs=[pl.BlockSpec(memory_space=pltpu.HBM)] * 5,
        out_specs=pl.BlockSpec(memory_space=pltpu.VMEM),
        scratch_shapes=[
            pltpu.VMEM((FIELDS, TALL, CP), f32),
            pltpu.VMEM((1, 1, 1, SLOTS), i32),
            pltpu.VMEM((1, 1, 1, SLOTS), i32),
            pltpu.VMEM((1, 1, 1, 4, SLOTS), f32),
            pltpu.VMEM((1, 1, 1, 640), i32),
            pltpu.VMEM((FIELDS, SHELLS, SLOTS), f32),
            pltpu.VMEM((9, FIELDS, SHELLS, SLOTS), f32),
            pltpu.VMEM((2, FIELDS, 8, CP), f32),
            pltpu.VMEM((2, FIELDS, 8, CP), f32),
            pltpu.VMEM((2, FIELDS, 2, TALL), f32),
            pltpu.VMEM((2, FIELDS, 2, TALL), f32),
            pltpu.VMEM((FIELDS, TALL, CP), f32),
            pltpu.VMEM((FIELDS, TALL, CP), f32),
            pltpu.VMEM((FIELDS, TALL, CP), f32),
            pltpu.VMEM((2, FIELDS, 8, CP), f32),
            pltpu.VMEM((2, 8, CP), i32),
            pltpu.SemaphoreType.DMA((12,)),
            pltpu.SemaphoreType.DMA((18,)),
            pltpu.SemaphoreType.DMA((18,)),
            pltpu.SemaphoreType.REGULAR,
        ],
        compiler_params=pltpu.CompilerParams(
            collective_id=0, has_side_effects=True, vmem_limit_bytes=32 * 1024 * 1024
        ),
    )(*[pltpu.with_memory_space_constraint(a, pltpu.HBM) for a in (state_now.reshape(FIELDS, TALL, CP), send_row, send_col, send_weight, ghost_slot)])
    return out.reshape(1, FIELDS, SHELLS, CT, CP)


def solution(mesh):
    placed = (
        P("panel", None, None, "colat", "lon"),
        P("panel", "lon", "colat", None),
        P("panel", "lon", "colat", None),
        P("panel", "lon", "colat", None, None),
        P("panel", "lon", "colat", None),
    )
    return jax.shard_map(
        body,
        mesh=mesh,
        in_specs=placed,
        out_specs=P("panel", None, None, "colat", "lon"),
        check_vma=False,
    )
```

```python
import math

import jax
import jax.numpy as jnp
from jax import lax
from jax.experimental import pallas as pl
from jax.experimental.pallas import tpu as pltpu
from jax.sharding import PartitionSpec as P

RADIAL_STEP = 0.65 / 511.0
COURANT = 0.3
ROTATION = 300.0
GRAVITY = 300.0
ADIABATIC = 2.0 / 3.0

FIELDS = 8
SHELLS = 4
CT = 32
CP = 128
SLOTS = 128
TALL = SHELLS * CT
MESH = pl.DeviceIdType.MESH
RUN = 8
AROUND = [(dl, dc) for dl in (-1, 0, 1) for dc in (-1, 0, 1)]
SEND_ORDER = (2, 1, 0, 5, 4, 3, 8, 7, 6)
TURNED = [(0, 1.0), (1, -1.0), (3, 1.0), (2, 1.0), (4, -1.0), (6, 1.0), (5, 1.0), (7, 1.0)]


def lanes_at(values, index):
    return jnp.take_along_axis(values, index, axis=1, mode="promise_in_bounds")


def cell_terms(u):
    rho, m, b, energy = u[0], u[1:4], u[4:7], u[7]
    inverse = 1.0 / rho
    v = [a * inverse for a in m]
    power = b[0] * b[0] + b[1] * b[1] + b[2] * b[2]
    moving = m[0] * v[0] + m[1] * v[1] + m[2] * v[2]
    pressure = ADIABATIC * (energy - 0.5 * moving - 0.5 * power) + 0.5 * power
    aligned = v[0] * b[0] + v[1] * b[1] + v[2] * b[2]
    return m, b, v, pressure, energy + pressure, aligned, rho


def flux_along(terms, e):
    m, b, v, pressure, enthalpy, aligned, rho = terms
    ve = v[0] * e[0] + v[1] * e[1]
    be = b[0] * e[0] + b[1] * e[1]
    if e[2] is not None:
        ve = ve + v[2] * e[2]
        be = be + b[2] * e[2]
    out = [rho * ve]
    for i in range(3):
        term = m[i] * ve - b[i] * be
        out.append(term if e[i] is None else term + pressure * e[i])
    for i in range(3):
        out.append(b[i] * ve - v[i] * be)
    out.append(enthalpy * ve - aligned * be)
    return out


def kernel(
    x_hbm, row_hbm, col_hbm, weight_hbm, ghost_hbm, acc,
    x, rows, cols, weight, wanted,
    slots, slots_in, row_out, row_in, col_out, col_in,
    radial, polar, azimuth, picked, named,
    in_sem, send_sem, recv_sem, told,
):
    p, l, c = lax.axis_index("panel"), lax.axis_index("lon"), lax.axis_index("colat")
    nl, nc = lax.axis_size("lon"), lax.axis_size("colat")
    ht = 0.5 * math.pi / (nc * CT)
    hp = 1.5 * math.pi / (nl * CP)
    tau = COURANT / (1.0 / RADIAL_STEP + 1.0 / ht + 1.0 / (hp * math.sin(0.25 * math.pi)))

    def wrap(a, n):
        return lax.rem(a + n, n)

    def on_row(ca):
        return (ca == 0) | (ca == nc - 1)

    def on_edge(la, ca):
        return (la == 0) | (la == nl - 1) | on_row(ca)

    small = [
        pltpu.make_async_copy(src, dst, in_sem.at[FIELDS + i])
        for i, (src, dst) in enumerate(
            ((row_hbm, rows), (col_hbm, cols), (weight_hbm, weight), (ghost_hbm, wanted))
        )
    ]
    large = [pltpu.make_async_copy(x_hbm.at[f], x.at[f], in_sem.at[f]) for f in range(FIELDS)]
    for load in small + large:
        load.start()

    up, down, left, right = c > 0, c < nc - 1, l > 0, l < nl - 1
    edge = on_edge(l, c)
    others = [(wrap(l + dl, nl), wrap(c + dc, nc)) for dl, dc in AROUND]

    late_left, late_right = 4, 4
    place = lax.rem(l, RUN)

    def passed(panel, tile, la):
        late = jnp.where(la < tile, late_left, late_right)
        far = (panel == 1) | ((lax.rem(tile, RUN) >= late) & (lax.rem(la, RUN) != RUN - 1))
        return far & (tile // RUN == la // RUN)

    flows_out, direct_in, shut_out, shut_in = [], [], [], []
    to_panel_1 = p == 0
    for (la, ca), (dl, dc) in zip(others, AROUND):
        flow, got = on_edge(la, ca), edge
        if dl:
            flow = flow & ~(on_row(ca) & passed(1 - p, la, l))
            got = got & ~(on_row(c) & passed(p, l, la))
        if dc != 1:
            flow = flow & ~((p == 1) & (la == 0) & (lax.rem(ca, 2) == 0))
        if dc != -1:
            got = got & ~((p == 0) & (l == 0) & (lax.rem(c, 2) == 0))
        flows_out.append(flow)
        direct_in.append(got)
        shut_out.append((p == 1) & (((place == RUN - 1) & (dl <= 0)) | ((place == 0) & (dl == -1))))
        shut_in.append((p == 0) & (((place == RUN - 1) & (dl >= 0)) | ((place == RUN - 2) & (dl == 1))))
    row_edge = on_row(c)
    take_left, take_right = row_edge & left & passed(p, l, l - 1), row_edge & right & passed(p, l, l + 1)
    pass_left, pass_right = row_edge & left & passed(p, l - 1, l), row_edge & right & passed(p, l + 1, l)
    mate_gives = (p == 0) & (l == 0) & (lax.rem(c, 2) == 1)
    mate_takes = (p == 0) & (l == 0) & (lax.rem(c, 2) == 0)

    inner = jnp.clip(c, 2, nc - 3)
    at_seam = (place == 0) | (place == RUN - 1)
    at_end = (l == 0) | (l == nl - 1)
    beside = (c < 2) | (c >= nc - 2)
    helped_1 = (p == 1) & at_seam & (beside | at_end)
    helped_0 = (p == 0) & (place == RUN - 1) & (beside | at_end)
    at_helper = (c == 2) | (c == nc - 3)
    helper_1 = (p == 1) & at_seam & ~at_end & at_helper
    helper_0 = (p == 0) & (place == RUN - 2) & (l != nl - 2) & at_helper
    end_helper = (l == nl - 2) & ~beside
    over_left, over_right = left & (place == 0), right & (place == RUN - 1)
    seam_by_help = helped_1 & ~at_end
    near_left, near_right = left & ~(over_left & seam_by_help), right & ~(over_right & seam_by_help)

    barrier = pltpu.get_barrier_semaphore()

    def greet(*device):
        pl.semaphore_signal(barrier, inc=1, device_id=device, device_id_type=MESH)

    for j, (la, ca) in enumerate(others):
        by_help = (p == 1) & (lax.rem(la, RUN) == RUN - 1)
        to_l = jnp.where(by_help, la - 1, la)
        to_c = jnp.where(by_help, jnp.clip(ca, 2, nc - 3), ca)
        pl.when(direct_in[j] & ~shut_in[j])(lambda: greet(1 - p, to_l, to_c))

    pl.when(near_left)(lambda: greet(p, l - 1, c))
    pl.when(near_right)(lambda: greet(p, l + 1, c))
    pl.when(up)(lambda: greet(p, l, c - 1))
    pl.when(down)(lambda: greet(p, l, c + 1))

    @pl.when(helped_0 | helped_1)
    def _():
        greet(p, jnp.where(at_end, nl - 2, jnp.where(p == 0, l - 1, l)), inner)
        pl.when(seam_by_help)(lambda: greet(p, jnp.where(place == 0, l - 1, l + 1), inner))

    @pl.when((p == 0) & (l < nl - 1) & row_edge & (place >= RUN - 2))
    def _():
        end = l == nl - 2
        last = jnp.where(end, l, l - place + RUN - 1)
        for helper in (2, nc - 3):
            greet(1, last, helper)
            pl.when(place == RUN - 1)(lambda: greet(1, l + 1, helper))

    @pl.when((p == 0) & (l == nl - 1))
    def _():
        for helper in range(2, nc - 2):
            reach = (c >= helper - 1) & (c <= helper + 1)
            if helper == 2:
                reach = (c <= helper + 1) | (c == nc - 1)
            if helper == nc - 3:
                reach = (c >= helper - 1) | (c == 0)
            pl.when(reach)(lambda: greet(1, nl - 2, helper))

    for load in small:
        load.wait()

    row_at = lax.broadcasted_iota(jnp.int32, (CT, CP), 0)
    lane8 = lax.broadcasted_iota(jnp.int32, (8, 128), 1)
    sub8 = lax.broadcasted_iota(jnp.int32, (8, 128), 0)
    lane32 = lax.broadcasted_iota(jnp.int32, (CT, CP), 1)
    first = row_at == rows[0, 0]
    second = row_at == rows[0, 0] + 1
    w = weight[0, 0, 0]
    on_left = jnp.where(first, w[0:1], jnp.where(second, w[2:3], 0.0))
    on_right = jnp.where(first, w[1:2], jnp.where(second, w[3:4], 0.0))
    pick = jnp.broadcast_to(cols[0, 0], (CT, CP))
    pick_next = pick + 1
    halves = [(h, lax.rem(sub8 // h, 2) == 0) for h in (4, 2)]

    def fold(a, b, step):
        h, low = halves[step]
        if h == 4:
            return jnp.where(low, a, b) + pltpu.roll(jnp.where(low, b, a), 4, 0)
        return jnp.where(low, a + pltpu.roll(a, 6, 0), b + pltpu.roll(b, 2, 0))

    for f in range(FIELDS):
        large[f].wait()
        target, sign = TURNED[f]
        sums = []
        for k in range(SHELLS):
            plane = x[f, CT * k : CT * (k + 1), :]
            mixed = on_left * lanes_at(plane, pick) + on_right * lanes_at(plane, pick_next)
            sums.append((mixed[0:8] + mixed[8:16]) + (mixed[16:24] + mixed[24:32]))
        four = fold(fold(sums[0], sums[2], 0), fold(sums[1], sums[3], 0), 1)
        both = four + pltpu.roll(four, 7, 0)
        for k in range(SHELLS):
            line = both[2 * k : 2 * k + 1]
            at = SHELLS * target + k
            slots[at : at + 1, :] = line if sign > 0 else -line

    def one(flag):
        return flag.astype(jnp.int32)

    expected = one(up) + one(down) + one(near_left) + one(near_right)
    for flow, shut in zip(flows_out, shut_out):
        expected = expected + one(flow & ~shut & ~helped_0)
    expected = expected + one(helper_1) * (6 + 2 * one(place == RUN - 1)) + 8 * one(helper_0)
    served = jnp.where(at_helper, 3, 1)
    at_panel_1 = 2 * served + jnp.where(at_helper, 7, 3)
    expected = expected + one(end_helper) * jnp.where(p == 1, at_panel_1, 7 * served)
    pl.semaphore_wait(barrier, expected)

    def remote(src, dst, i, *device):
        return pltpu.make_async_remote_copy(
            src_ref=src, dst_ref=dst, send_sem=send_sem.at[i], recv_sem=recv_sem.at[i],
            device_id=device, device_id_type=MESH,
        )

    slot_copies = [
        pltpu.make_async_remote_copy(
            src_ref=slots, dst_ref=slots_in.at[8 - j], send_sem=send_sem.at[j], recv_sem=recv_sem.at[8 - j],
            device_id=(1 - p, la, ca), device_id_type=MESH,
        )
        for j, (la, ca) in enumerate(others)
    ]

    def send_slots(wave):
        for j in SEND_ORDER:
            la, ca = others[j]
            spot = lax.rem(la, RUN)
            turn = jnp.where(p == 0, 0, jnp.where(spot == 0, 0, jnp.where(spot < 3, 0, jnp.where(spot < 5, 0, 0))))
            pl.when(flows_out[j] & ~shut_out[j] & ~helped_0 & (turn == wave))(slot_copies[j].start)

    send_slots(0)

    def tell(*device):
        pl.semaphore_signal(told, inc=1, device_id=device, device_id_type=MESH)

    @pl.when(helper_0 | helper_1)
    def _():
        first = jnp.where(c == 2, 0, nc - 2)
        for more in range(2):
            tell(p, jnp.where(p == 0, l + 1, l), first + more)

    @pl.when(end_helper)
    def _():
        tell(p, nl - 1, c)
        pl.when(p == 1)(lambda: tell(p, 0, c))

        @pl.when(at_helper)
        def _():
            first = jnp.where(c == 2, 0, nc - 2)
            for more in range(2):
                tell(p, nl - 1, first + more)
                pl.when(p == 1)(lambda: tell(p, 0, first + more))

    lanes = lax.broadcasted_iota(jnp.int32, (TALL, CP), 1)
    packed = jnp.zeros((TALL, CP), jnp.float32)
    for f in range(FIELDS):
        for r in range(2):
            row_out[0, f, pl.ds(4 * r, 4), :] = x[f, pl.ds(r, SHELLS, stride=CT), :]
            row_out[1, f, pl.ds(4 * r, 4), :] = x[f, pl.ds(CT - 2 + r, SHELLS, stride=CT), :]
        turned = pltpu.roll(x[f], 2 + 4 * f, 1)
        packed = jnp.where(lanes // 4 == f, turned, packed)
    upright = packed.T
    for f in range(FIELDS):
        col_out[1, f] = upright[4 * f : 4 * f + 2]
        col_out[0, f] = upright[4 * f + 2 : 4 * f + 4]

    to_up = remote(row_out.at[0], row_in.at[1], 9, p, l, c - 1)
    to_down = remote(row_out.at[1], row_in.at[0], 10, p, l, c + 1)
    to_left = remote(col_out.at[0], col_in.at[1], 11, p, l - 1, c)
    to_right = remote(col_out.at[1], col_in.at[0], 12, p, l + 1, c)
    pl.when(near_left)(to_left.start)
    pl.when(near_right)(to_right.start)
    pl.when(up)(to_up.start)
    pl.when(down)(to_down.start)

    row0 = (c * CT).astype(jnp.float32) + 0.5
    col0 = (l * CP).astype(jnp.float32) + 0.5

    def angle_t(row):
        return 0.25 * math.pi + (row + row0) * ht

    def angle_f(col):
        return -0.75 * math.pi + (col + col0) * hp

    theta = angle_t(row_at.astype(jnp.float32))
    phi = angle_f(lane8[0:1].astype(jnp.float32))
    st, ct = jnp.sin(theta), jnp.cos(theta)
    sf = jnp.broadcast_to(jnp.sin(phi), (8, CP))
    cf = jnp.broadcast_to(jnp.cos(phi), (8, CP))
    spin_second = ROTATION * p.astype(jnp.float32)
    spin_third = ROTATION - spin_second

    def one_block(n, _):
        at = pl.multiple_of(n * 8, 8)
        th = angle_t((sub8 + lax.rem(n, CT // 8) * 8).astype(jnp.float32))
        s8, c8 = jnp.sin(th), jnp.cos(th)
        u = [x[f, pl.ds(at, 8), :] for f in range(FIELDS)]
        terms = cell_terms(u)
        er = (s8 * cf, s8 * sf, c8)
        for f, value in enumerate(flux_along(terms, er)):
            radial[f, pl.ds(at, 8), :] = value
        for f, value in enumerate(flux_along(terms, (c8 * cf, c8 * sf, -s8))):
            polar[f, pl.ds(at, 8), :] = value
        for f, value in enumerate(flux_along(terms, (-sf, cf, None))):
            azimuth[f, pl.ds(at, 8), :] = value
        rho, m = u[0], u[1:4]
        turn = (
            spin_second * m[2] - spin_third * m[1], spin_third * m[0], -spin_second * m[0]
        )
        acc[0, pl.ds(at, 8), :] = u[0]
        for i in range(3):
            acc[1 + i, pl.ds(at, 8), :] = m[i] - tau * (2.0 * turn[i] + GRAVITY * (rho * er[i]))
            acc[4 + i, pl.ds(at, 8), :] = u[4 + i]
        acc[7, pl.ds(at, 8), :] = u[7] - (tau * GRAVITY) * (m[0] * er[0] + m[1] * er[1] + m[2] * er[2])
        return 0

    lax.fori_loop(0, TALL // 8, one_block, 0)

    ends = {1: 8.0 / 12.0, 2: -1.0 / 12.0}

    def gives(along, across, n, step):
        even = (ends[n] / step * math.cos(n * step)) * along
        odd = (ends[n] / step * math.sin(n * step)) * across
        return even + odd, odd - even

    radius = [1.0 - (SHELLS - 1 - k) * RADIAL_STEP for k in range(SHELLS)]

    def one_field(f, _):
        fr = [radial[f, pl.ds(CT * k, CT), :] for k in range(SHELLS)]
        for k in range(SHELLS):
            here = pl.ds(CT * k, CT)
            ft, fp = polar[f, here, :], azimuth[f, here, :]
            flat = st * fr[k] + ct * ft
            total_t = jnp.zeros((CT, CP), jnp.float32)
            total_p = total_t
            for n in (1, 2):
                before, after = gives(ft, fr[k], n, ht)
                total_t = total_t + jnp.where(row_at < CT - n, pltpu.roll(before, CT - n, 0), 0.0)
                total_t = total_t + jnp.where(row_at >= n, pltpu.roll(after, n, 0), 0.0)
                before, after = gives(fp, flat, n, hp)
                total_p = total_p + jnp.where(lane32 < CP - n, pltpu.roll(before, CP - n, 1), 0.0)
                total_p = total_p + jnp.where(lane32 >= n, pltpu.roll(after, n, 1), 0.0)
            low, high = max(k - 1, 0), min(k + 1, SHELLS - 1)
            slope = (fr[high] - fr[low]) * (1.0 / ((high - low) * RADIAL_STEP))
            whole = slope + (1.0 / radius[k]) * (total_t + total_p / st)
            acc[f, here, :] = acc[f, here, :] - tau * whole
        return 0

    lax.fori_loop(0, FIELDS, one_field, 0)

    @pl.when(helped_0 | helped_1)
    def _():
        pl.semaphore_wait(told, 1)
        pl.when(over_left & seam_by_help)(to_left.start)
        pl.when(over_right & seam_by_help)(to_right.start)
        for j in SEND_ORDER:
            pl.when(flows_out[j] & (shut_out[j] | helped_0))(slot_copies[j].start)

    def near(n):
        return tau * ends[n]

    shell8 = lax.rem(sub8, 4).astype(jnp.float32)
    inverse_r = 1.0 / ((1.0 - (SHELLS - 1 - shell8) * RADIAL_STEP) * ht)
    upper = sub8 < 4

    row_jobs = []
    for jobs in (
        ((0, -near(2), -near(1)), (1, 0.0, -near(2))),
        ((CT - 1, near(1), near(2)), (CT - 2, near(2), 0.0)),
    ):
        row_jobs.append([])
        for row, one_w, two_w in jobs:
            th = angle_t(jnp.full((8, 128), row, jnp.float32))
            s8, c8 = jnp.sin(th), jnp.cos(th)
            row_jobs[-1].append((row, jnp.where(upper, one_w, two_w) * inverse_r, (c8 * cf, c8 * sf, -s8)))

    def add_rows(side, fields):
        terms = cell_terms(fields)
        for row, scale, e in row_jobs[side]:
            where = pl.ds(row, SHELLS, stride=CT)
            for f, value in enumerate(flux_along(terms, e)):
                value = value * scale
                acc[f, where, :] = acc[f, where, :] - (value[0:4] + value[4:8])

    rim = (lanes < 2) | (lanes >= CP - 2)

    sub4 = lax.broadcasted_iota(jnp.int32, (4, 128), 0)
    lane4 = lax.broadcasted_iota(jnp.int32, (4, 128), 1)
    th = angle_t(lax.rem(lane4, CT).astype(jnp.float32))
    shell4 = (lane4 // CT).astype(jnp.float32)
    share = 1.0 / ((1.0 - (SHELLS - 1 - shell4) * RADIAL_STEP) * jnp.sin(th) * hp)
    column_jobs = []
    for from_left, from_right, weights in (
        (0, CP - 1, (-near(2), -near(1), near(1), near(2))),
        (1, CP - 2, (0.0, -near(2), near(2), 0.0)),
    ):
        ph = angle_f(jnp.where(sub4 < 2, from_left, from_right).astype(jnp.float32))
        scale = jnp.where(
            sub4 < 2,
            jnp.where(sub4 == 0, weights[0], weights[1]),
            jnp.where(sub4 == 2, weights[2], weights[3]),
        ) * share
        column_jobs.append((scale, (-jnp.sin(ph), jnp.cos(ph), None)))

    def add_columns():
        u = [jnp.concatenate([col_in[0, f], col_in[1, f]], axis=0) for f in range(FIELDS)]
        terms = cell_terms(u)
        parts = [[v * scale for v in flux_along(terms, e)] for scale, e in column_jobs]
        lines = []
        for f in range(FIELDS):
            close, far = parts[0][f], parts[1][f]
            lines += [far[2:3] + far[3:4], close[2:3] + close[3:4], close[0:1] + close[1:2], far[0:1] + far[1:2]]
        stood = jnp.concatenate(lines + [jnp.zeros((TALL - 4 * FIELDS, CP), jnp.float32)], axis=0).T
        for f in range(FIELDS):
            shift = (CP - 2 - 4 * f) % CP
            acc[f] = acc[f] - jnp.where(rim, pltpu.roll(stood, shift, 1) if shift else stood, 0.0)

    pl.when(left)(to_right.wait_recv)
    pl.when(right)(to_left.wait_recv)
    pl.when(left & right)(add_columns)

    @pl.when(up)
    def _():
        to_down.wait_recv()
        add_rows(0, [row_in[0, f] for f in range(FIELDS)])

    @pl.when(down)
    def _():
        to_up.wait_recv()
        add_rows(1, [row_in[1, f] for f in range(FIELDS)])

    def name(kind, lines):
        for r, line in enumerate(lines):
            named[kind, r] = line

    def name_row(side):
        name(0, [jnp.broadcast_to(wanted[0, 0, :, pl.ds(256 * side + 128 * r, 128)], (8, 128)) for r in range(2)])

    def name_column(side):
        line = jnp.broadcast_to(wanted[0, 0, :, pl.ds(512, 128)], (8, 128))
        name(1, [lanes_at(line, 64 * side + 2 * lax.rem(lane8, CT) + r) for r in range(2)])

    pl.when(c == 0)(lambda: name_row(0))
    pl.when(c == nc - 1)(lambda: name_row(1))
    pl.when(l == 0)(lambda: name_column(0))
    pl.when(l == nl - 1)(lambda: name_column(1))

    def pick_ghosts(kind, group, fresh):
        for r in range(2):
            index = named[kind, r]
            owner = index // SLOTS
            lane = lax.rem(index, SLOTS)
            found = [None if fresh else picked[kind, r, 8 * m : 8 * m + 8, :] for m in range(4)]
            for j in range(3 * group, 3 * group + 3):
                here = owner == others[j][0] * nc + others[j][1]
                for m in range(4):
                    value = lanes_at(slots_in[j, 8 * m : 8 * m + 8, :], lane)
                    found[m] = value if found[m] is None else jnp.where(here, value, found[m])
            for m in range(4):
                picked[kind, r, 8 * m : 8 * m + 8, :] = found[m]

    pass_on = [
        remote(slots_in.at[3:6], slots_in.at[6:9], 13, p, l - 1, c),
        remote(slots_in.at[3:6], slots_in.at[0:3], 14, p, l + 1, c),
    ]
    to_mate = [
        remote(slots_in.at[3 * group : 3 * group + 2], slots_in.at[3 * group + 1 : 3 * group + 3], 15 + group, p, l, c - 1)
        for group in range(3)
    ]
    for turn, group in enumerate((1, 0, 2)):
        for j in range(3 * group, 3 * group + 3):
            pl.when(direct_in[j])(slot_copies[8 - j].wait_recv)
        if group == 0:
            pl.when(take_left)(pass_on[1].wait_recv)
        if group == 1:
            pl.when(pass_left)(pass_on[0].start)
            pl.when(pass_right)(pass_on[1].start)
        if group == 2:
            pl.when(take_right)(pass_on[0].wait_recv)
        pl.when(mate_gives)(to_mate[group].start)
        pl.when(mate_takes)(to_mate[group].wait_recv)
        pl.when(row_edge)(lambda: pick_ghosts(0, group, turn == 0))
        pl.when(at_end)(lambda: pick_ghosts(1, group, turn == 0))

    @pl.when(at_end)
    def _():
        side = jnp.where(l == 0, 0, 1)
        mine = lane8 // CT == lax.rem(sub8, 4)
        for r in range(2):
            for m in range(4):
                own = jnp.where(mine, picked[1, r, 8 * m : 8 * m + 8, :], 0.0)
                own = own + pltpu.roll(own, 7, 0)
                own = own + pltpu.roll(own, 6, 0)
                col_in[side, 2 * m, r : r + 1, :] = own[0:1]
                col_in[side, 2 * m + 1, r : r + 1, :] = own[4:5]
        add_columns()

    def add_ghost_rows(side):
        fields = [
            jnp.concatenate([picked[0, r, SHELLS * f : SHELLS * f + SHELLS, :] for r in range(2)], axis=0)
            for f in range(FIELDS)
        ]
        add_rows(side, fields)

    pl.when(c == 0)(lambda: add_ghost_rows(0))
    pl.when(c == nc - 1)(lambda: add_ghost_rows(1))

    for j in range(9):
        pl.when(flows_out[j])(slot_copies[j].wait_send)
    pl.when(pass_left)(pass_on[0].wait_send)
    pl.when(pass_right)(pass_on[1].wait_send)
    for copy in to_mate:
        pl.when(mate_gives)(copy.wait_send)
    pl.when(left)(to_left.wait_send)
    pl.when(right)(to_right.wait_send)
    pl.when(up)(to_up.wait_send)
    pl.when(down)(to_down.wait_send)


def body(state_now, send_row, send_col, send_weight, ghost_slot):
    f32, i32 = jnp.float32, jnp.int32
    out = pl.pallas_call(
        kernel,
        out_shape=pltpu.VMEM((FIELDS, TALL, CP), f32),
        in_specs=[pl.BlockSpec(memory_space=pltpu.HBM)] * 5,
        out_specs=pl.BlockSpec(memory_space=pltpu.VMEM),
        scratch_shapes=[
            pltpu.VMEM((FIELDS, TALL, CP), f32),
            pltpu.VMEM((1, 1, 1, SLOTS), i32),
            pltpu.VMEM((1, 1, 1, SLOTS), i32),
            pltpu.VMEM((1, 1, 1, 4, SLOTS), f32),
            pltpu.VMEM((1, 1, 1, 640), i32),
            pltpu.VMEM((FIELDS * SHELLS, SLOTS), f32),
            pltpu.VMEM((9, FIELDS * SHELLS, SLOTS), f32),
            pltpu.VMEM((2, FIELDS, 8, CP), f32),
            pltpu.VMEM((2, FIELDS, 8, CP), f32),
            pltpu.VMEM((2, FIELDS, 2, TALL), f32),
            pltpu.VMEM((2, FIELDS, 2, TALL), f32),
            pltpu.VMEM((FIELDS, TALL, CP), f32),
            pltpu.VMEM((FIELDS, TALL, CP), f32),
            pltpu.VMEM((FIELDS, TALL, CP), f32),
            pltpu.VMEM((2, 2, FIELDS * SHELLS, CP), f32),
            pltpu.VMEM((2, 2, 8, CP), i32),
            pltpu.SemaphoreType.DMA((12,)),
            pltpu.SemaphoreType.DMA((18,)),
            pltpu.SemaphoreType.DMA((18,)),
            pltpu.SemaphoreType.REGULAR,
        ],
        compiler_params=pltpu.CompilerParams(
            collective_id=0, has_side_effects=True, vmem_limit_bytes=32 * 1024 * 1024
        ),
    )(*[pltpu.with_memory_space_constraint(a, pltpu.HBM) for a in (state_now.reshape(FIELDS, TALL, CP), send_row, send_col, send_weight, ghost_slot)])
    return out.reshape(1, FIELDS, SHELLS, CT, CP)


def solution(mesh):
    placed = (
        P("panel", None, None, "colat", "lon"),
        P("panel", "lon", "colat", None),
        P("panel", "lon", "colat", None),
        P("panel", "lon", "colat", None, None),
        P("panel", "lon", "colat", None),
    )
    return jax.shard_map(
        body,
        mesh=mesh,
        in_specs=placed,
        out_specs=P("panel", None, None, "colat", "lon"),
        check_vma=False,
    )
```

```python
import math

import jax
import jax.numpy as jnp
from jax import lax
from jax.experimental import pallas as pl
from jax.experimental.pallas import tpu as pltpu
from jax.sharding import PartitionSpec as P

RADIAL_STEP = 0.65 / 511.0
COURANT = 0.3
ROTATION = 300.0
GRAVITY = 300.0
ADIABATIC = 2.0 / 3.0

FIELDS = 8
SHELLS = 4
CT = 32
CP = 128
SLOTS = 128
TALL = SHELLS * CT
MESH = pl.DeviceIdType.MESH
RUN = 8
AROUND = [(dl, dc) for dl in (-1, 0, 1) for dc in (-1, 0, 1)]
SEND_ORDER = (2, 1, 0, 5, 4, 3, 8, 7, 6)
TURNED = [(0, 1.0), (1, -1.0), (3, 1.0), (2, 1.0), (4, -1.0), (6, 1.0), (5, 1.0), (7, 1.0)]


def lanes_at(values, index):
    return jnp.take_along_axis(values, index, axis=1, mode="promise_in_bounds")


def cell_terms(u):
    rho, m, b, energy = u[0], u[1:4], u[4:7], u[7]
    inverse = 1.0 / rho
    v = [a * inverse for a in m]
    power = b[0] * b[0] + b[1] * b[1] + b[2] * b[2]
    moving = m[0] * v[0] + m[1] * v[1] + m[2] * v[2]
    pressure = ADIABATIC * (energy - 0.5 * moving - 0.5 * power) + 0.5 * power
    aligned = v[0] * b[0] + v[1] * b[1] + v[2] * b[2]
    return m, b, v, pressure, energy + pressure, aligned, rho


def flux_along(terms, e):
    m, b, v, pressure, enthalpy, aligned, rho = terms
    ve = v[0] * e[0] + v[1] * e[1]
    be = b[0] * e[0] + b[1] * e[1]
    if e[2] is not None:
        ve = ve + v[2] * e[2]
        be = be + b[2] * e[2]
    out = [rho * ve]
    for i in range(3):
        term = m[i] * ve - b[i] * be
        out.append(term if e[i] is None else term + pressure * e[i])
    for i in range(3):
        out.append(b[i] * ve - v[i] * be)
    out.append(enthalpy * ve - aligned * be)
    return out


def kernel(
    x_hbm, row_hbm, col_hbm, weight_hbm, ghost_hbm, acc,
    x, rows, cols, weight, wanted,
    slots, slots_in, row_out, row_in, col_out, col_in,
    radial, polar, azimuth, picked, named,
    in_sem, send_sem, recv_sem, told,
):
    p, l, c = lax.axis_index("panel"), lax.axis_index("lon"), lax.axis_index("colat")
    nl, nc = lax.axis_size("lon"), lax.axis_size("colat")
    ht = 0.5 * math.pi / (nc * CT)
    hp = 1.5 * math.pi / (nl * CP)
    tau = COURANT / (1.0 / RADIAL_STEP + 1.0 / ht + 1.0 / (hp * math.sin(0.25 * math.pi)))

    def wrap(a, n):
        return lax.rem(a + n, n)

    def on_row(ca):
        return (ca == 0) | (ca == nc - 1)

    def on_edge(la, ca):
        return (la == 0) | (la == nl - 1) | on_row(ca)

    small = [
        pltpu.make_async_copy(src, dst, in_sem.at[2 + i])
        for i, (src, dst) in enumerate(
            ((row_hbm, rows), (col_hbm, cols), (weight_hbm, weight), (ghost_hbm, wanted))
        )
    ]
    half = FIELDS // 2
    large = [
        pltpu.make_async_copy(x_hbm.at[half * i : half * (i + 1)], x.at[half * i : half * (i + 1)], in_sem.at[i]) for i in range(2)
    ]
    for load in small + large:
        load.start()

    up, down, left, right = c > 0, c < nc - 1, l > 0, l < nl - 1
    edge = on_edge(l, c)
    others = [(wrap(l + dl, nl), wrap(c + dc, nc)) for dl, dc in AROUND]

    late_left, late_right = 4, 4
    place = lax.rem(l, RUN)

    def passed(panel, tile, la):
        late = jnp.where(la < tile, late_left, late_right)
        far = (panel == 1) | ((lax.rem(tile, RUN) >= late) & (lax.rem(la, RUN) != RUN - 1))
        return far & (tile // RUN == la // RUN)

    flows_out, direct_in, shut_out, shut_in = [], [], [], []
    beside = (c < 2) | (c >= nc - 2)
    to_panel_1 = p == 0
    for (la, ca), (dl, dc) in zip(others, AROUND):
        flow, got = on_edge(la, ca), edge
        if dl:
            flow = flow & ~(on_row(ca) & passed(1 - p, la, l))
            got = got & ~(on_row(c) & passed(p, l, la))
        if dc != 1:
            flow = flow & ~((p == 1) & (la == 0) & (lax.rem(ca, 2) == 0))
        if dc != -1:
            got = got & ~((p == 0) & (l == 0) & (lax.rem(c, 2) == 0))
        flows_out.append(flow)
        direct_in.append(got)
        shut = ((place == RUN - 1) & (dl <= 0)) | ((place == 0) & (dl == -1))
        if dl == 1:
            shut = shut | ((l == nl - 2) & beside)
        shut_out.append((p == 1) & shut)
        shut = ((place == RUN - 1) & (dl >= 0)) | ((place == RUN - 2) & (dl == 1))
        if dl == -1:
            shut = shut | ((l == nl - 1) & ((ca < 2) | (ca >= nc - 2)))
        shut_in.append((p == 0) & shut)
    row_edge = on_row(c)
    pass_left, pass_right = row_edge & left & passed(p, l - 1, l), row_edge & right & passed(p, l + 1, l)
    mate_gives = (p == 0) & (l == 0) & (lax.rem(c, 2) == 1)
    mate_takes = (p == 0) & (l == 0) & (lax.rem(c, 2) == 0)

    inner = jnp.clip(c, 2, nc - 3)
    at_seam = (place == 0) | (place == RUN - 1)
    at_end = (l == 0) | (l == nl - 1)
    helped_1 = (p == 1) & ((at_seam & (beside | at_end)) | ((l == nl - 2) & beside))
    helped_0 = (p == 0) & (place == RUN - 1) & (beside | at_end)
    at_helper = (c == 2) | (c == nc - 3)
    helper_1 = (p == 1) & at_seam & ~at_end & at_helper
    helper_0 = (p == 0) & (place == RUN - 2) & (l != nl - 2) & at_helper
    end_helper = (l == nl - 2) & ~beside
    over_left, over_right = left & (place == 0), right & (place == RUN - 1)
    seam_by_help = helped_1 & at_seam & ~at_end
    near_left, near_right = left & ~(over_left & seam_by_help), right & ~(over_right & seam_by_help)

    barrier = pltpu.get_barrier_semaphore()

    def greet(*device):
        pl.semaphore_signal(barrier, inc=1, device_id=device, device_id_type=MESH)

    for j, (la, ca) in enumerate(others):
        by_help = (p == 1) & (lax.rem(la, RUN) == RUN - 1)
        to_l = jnp.where(by_help, la - 1, la)
        to_c = jnp.where(by_help, jnp.clip(ca, 2, nc - 3), ca)
        pl.when(direct_in[j] & ~shut_in[j])(lambda: greet(1 - p, to_l, to_c))

    pl.when(near_left)(lambda: greet(p, l - 1, c))
    pl.when(near_right)(lambda: greet(p, l + 1, c))
    pl.when(up)(lambda: greet(p, l, c - 1))
    pl.when(down)(lambda: greet(p, l, c + 1))

    @pl.when(helped_0 | helped_1)
    def _():
        greet(p, jnp.where(at_end, nl - 2, jnp.where(p == 0, l - 1, l)), inner)
        pl.when(seam_by_help)(lambda: greet(p, jnp.where(place == 0, l - 1, l + 1), inner))

    @pl.when((p == 0) & (l < nl - 1) & row_edge & (place >= RUN - 2))
    def _():
        end = l == nl - 2
        last = jnp.where(end, l, l - place + RUN - 1)
        for helper in (2, nc - 3):
            greet(1, last, helper)
            pl.when(place == RUN - 1)(lambda: greet(1, l + 1, helper))

    @pl.when((p == 0) & (l == nl - 1))
    def _():
        for helper in range(2, nc - 2):
            reach = (c >= helper - 1) & (c <= helper + 1)
            if helper == 2:
                reach = (c <= helper + 1) | (c == nc - 1)
            if helper == nc - 3:
                reach = (c >= helper - 1) | (c == 0)
            pl.when(reach)(lambda: greet(1, nl - 2, helper))

    for load in small:
        load.wait()

    row_at = lax.broadcasted_iota(jnp.int32, (CT, CP), 0)
    lane8 = lax.broadcasted_iota(jnp.int32, (8, 128), 1)
    sub8 = lax.broadcasted_iota(jnp.int32, (8, 128), 0)
    lane32 = lax.broadcasted_iota(jnp.int32, (CT, CP), 1)
    first = row_at == rows[0, 0]
    second = row_at == rows[0, 0] + 1
    w = weight[0, 0, 0]
    on_left = jnp.where(first, w[0:1], jnp.where(second, w[2:3], 0.0))
    on_right = jnp.where(first, w[1:2], jnp.where(second, w[3:4], 0.0))
    pick = jnp.broadcast_to(cols[0, 0], (CT, CP))
    pick_next = pick + 1
    halves = [(h, lax.rem(sub8 // h, 2) == 0) for h in (4, 2)]

    def fold(a, b, step):
        h, low = halves[step]
        if h == 4:
            return jnp.where(low, a, b) + pltpu.roll(jnp.where(low, b, a), 4, 0)
        return jnp.where(low, a + pltpu.roll(a, 6, 0), b + pltpu.roll(b, 2, 0))

    for f in range(FIELDS):
        if f % half == 0:
            large[f // half].wait()
        target, sign = TURNED[f]
        sums = []
        for k in range(SHELLS):
            plane = x[f, CT * k : CT * (k + 1), :]
            mixed = on_left * lanes_at(plane, pick) + on_right * lanes_at(plane, pick_next)
            sums.append((mixed[0:8] + mixed[8:16]) + (mixed[16:24] + mixed[24:32]))
        four = fold(fold(sums[0], sums[2], 0), fold(sums[1], sums[3], 0), 1)
        both = four + pltpu.roll(four, 7, 0)
        for k in range(SHELLS):
            line = both[2 * k : 2 * k + 1]
            at = SHELLS * target + k
            slots[at : at + 1, :] = line if sign > 0 else -line

    def one(flag):
        return flag.astype(jnp.int32)

    expected = one(up) + one(down) + one(near_left) + one(near_right)
    for flow, shut in zip(flows_out, shut_out):
        expected = expected + one(flow & ~shut & ~helped_0)
    expected = expected + one(helper_1) * (6 + 2 * one(place == RUN - 1)) + 8 * one(helper_0)
    served = jnp.where(at_helper, 3, 1)
    at_panel_1 = 2 * served + jnp.where(at_helper, 9, 3)
    expected = expected + one(end_helper) * jnp.where(p == 1, at_panel_1, 7 * served)
    pl.semaphore_wait(barrier, expected)

    def remote(src, dst, sent, arrived, *device):
        return pltpu.make_async_remote_copy(
            src_ref=src, dst_ref=dst, send_sem=send_sem.at[sent], recv_sem=recv_sem.at[arrived],
            device_id=device, device_id_type=MESH,
        )

    slot_copies = [
        remote(slots, slots_in.at[8 - j], 0, (8 - j) // 3, 1 - p, la, ca) for j, (la, ca) in enumerate(others)
    ]

    def whole(sent, arrived, sets):
        return remote(sets, sets, sent, arrived, 1 - p, l, c)

    def send_slots(wave):
        for j in SEND_ORDER:
            la, ca = others[j]
            spot = lax.rem(la, RUN)
            turn = jnp.where(p == 0, 0, jnp.where(spot == 0, 0, jnp.where(spot < 3, 0, jnp.where(spot < 5, 0, 0))))
            pl.when(flows_out[j] & ~shut_out[j] & ~helped_0 & (turn == wave))(slot_copies[j].start)

    send_slots(0)

    def tell(*device):
        pl.semaphore_signal(told, inc=1, device_id=device, device_id_type=MESH)

    @pl.when(helper_0 | helper_1)
    def _():
        first = jnp.where(c == 2, 0, nc - 2)
        for more in range(2):
            tell(p, jnp.where(p == 0, l + 1, l), first + more)

    @pl.when(end_helper)
    def _():
        tell(p, nl - 1, c)
        pl.when(p == 1)(lambda: tell(p, 0, c))

        @pl.when(at_helper)
        def _():
            first = jnp.where(c == 2, 0, nc - 2)
            for more in range(2):
                tell(p, nl - 1, first + more)
                pl.when(p == 1)(lambda: tell(p, 0, first + more))
                pl.when(p == 1)(lambda: tell(p, nl - 2, first + more))

    lanes = lax.broadcasted_iota(jnp.int32, (TALL, CP), 1)
    packed = jnp.zeros((TALL, CP), jnp.float32)
    for f in range(FIELDS):
        for r in range(2):
            row_out[0, f, pl.ds(4 * r, 4), :] = x[f, pl.ds(r, SHELLS, stride=CT), :]
            row_out[1, f, pl.ds(4 * r, 4), :] = x[f, pl.ds(CT - 2 + r, SHELLS, stride=CT), :]
        turned = pltpu.roll(x[f], 2 + 4 * f, 1)
        packed = jnp.where(lanes // 4 == f, turned, packed)
    upright = packed.T
    for f in range(FIELDS):
        col_out[1, f] = upright[4 * f : 4 * f + 2]
        col_out[0, f] = upright[4 * f + 2 : 4 * f + 4]

    to_up = remote(row_out.at[0], row_in.at[1], 1, 4, p, l, c - 1)
    to_down = remote(row_out.at[1], row_in.at[0], 1, 3, p, l, c + 1)
    to_left = remote(col_out.at[0], col_in.at[1], 2, 6, p, l - 1, c)
    to_right = remote(col_out.at[1], col_in.at[0], 2, 5, p, l + 1, c)
    pl.when(near_left)(to_left.start)
    pl.when(near_right)(to_right.start)
    pl.when(up)(to_up.start)
    pl.when(down)(to_down.start)

    row0 = (c * CT).astype(jnp.float32) + 0.5
    col0 = (l * CP).astype(jnp.float32) + 0.5

    def angle_t(row):
        return 0.25 * math.pi + (row + row0) * ht

    def angle_f(col):
        return -0.75 * math.pi + (col + col0) * hp

    theta = angle_t(row_at.astype(jnp.float32))
    phi = angle_f(lane8[0:1].astype(jnp.float32))
    st, ct = jnp.sin(theta), jnp.cos(theta)
    sf = jnp.broadcast_to(jnp.sin(phi), (8, CP))
    cf = jnp.broadcast_to(jnp.cos(phi), (8, CP))
    spin_second = ROTATION * p.astype(jnp.float32)
    spin_third = ROTATION - spin_second

    def one_block(n, _):
        at = pl.multiple_of(n * 8, 8)
        th = angle_t((sub8 + lax.rem(n, CT // 8) * 8).astype(jnp.float32))
        s8, c8 = jnp.sin(th), jnp.cos(th)
        u = [x[f, pl.ds(at, 8), :] for f in range(FIELDS)]
        terms = cell_terms(u)
        er = (s8 * cf, s8 * sf, c8)
        for f, value in enumerate(flux_along(terms, er)):
            radial[f, pl.ds(at, 8), :] = value
        for f, value in enumerate(flux_along(terms, (c8 * cf, c8 * sf, -s8))):
            polar[f, pl.ds(at, 8), :] = value
        for f, value in enumerate(flux_along(terms, (-sf, cf, None))):
            azimuth[f, pl.ds(at, 8), :] = value
        rho, m = u[0], u[1:4]
        turn = (
            spin_second * m[2] - spin_third * m[1], spin_third * m[0], -spin_second * m[0]
        )
        acc[0, pl.ds(at, 8), :] = u[0]
        for i in range(3):
            acc[1 + i, pl.ds(at, 8), :] = m[i] - tau * (2.0 * turn[i] + GRAVITY * (rho * er[i]))
            acc[4 + i, pl.ds(at, 8), :] = u[4 + i]
        acc[7, pl.ds(at, 8), :] = u[7] - (tau * GRAVITY) * (m[0] * er[0] + m[1] * er[1] + m[2] * er[2])
        return 0

    lax.fori_loop(0, TALL // 8, one_block, 0)

    ends = {1: 8.0 / 12.0, 2: -1.0 / 12.0}

    def gives(along, across, n, step):
        even = (ends[n] / step * math.cos(n * step)) * along
        odd = (ends[n] / step * math.sin(n * step)) * across
        return even + odd, odd - even

    radius = [1.0 - (SHELLS - 1 - k) * RADIAL_STEP for k in range(SHELLS)]

    def one_field(f, _):
        fr = [radial[f, pl.ds(CT * k, CT), :] for k in range(SHELLS)]
        for k in range(SHELLS):
            here = pl.ds(CT * k, CT)
            ft, fp = polar[f, here, :], azimuth[f, here, :]
            flat = st * fr[k] + ct * ft
            total_t = jnp.zeros((CT, CP), jnp.float32)
            total_p = total_t
            for n in (1, 2):
                before, after = gives(ft, fr[k], n, ht)
                total_t = total_t + jnp.where(row_at < CT - n, pltpu.roll(before, CT - n, 0), 0.0)
                total_t = total_t + jnp.where(row_at >= n, pltpu.roll(after, n, 0), 0.0)
                before, after = gives(fp, flat, n, hp)
                total_p = total_p + jnp.where(lane32 < CP - n, pltpu.roll(before, CP - n, 1), 0.0)
                total_p = total_p + jnp.where(lane32 >= n, pltpu.roll(after, n, 1), 0.0)
            low, high = max(k - 1, 0), min(k + 1, SHELLS - 1)
            slope = (fr[high] - fr[low]) * (1.0 / ((high - low) * RADIAL_STEP))
            whole = slope + (1.0 / radius[k]) * (total_t + total_p / st)
            acc[f, here, :] = acc[f, here, :] - tau * whole
        return 0

    lax.fori_loop(0, FIELDS, one_field, 0)

    @pl.when(helped_0 | helped_1)
    def _():
        pl.semaphore_wait(told, 1)
        pl.when(over_left & seam_by_help)(to_left.start)
        pl.when(over_right & seam_by_help)(to_right.start)
        for j in SEND_ORDER:
            pl.when(flows_out[j] & (shut_out[j] | helped_0))(slot_copies[j].start)

    def near(n):
        return tau * ends[n]

    shell8 = lax.rem(sub8, 4).astype(jnp.float32)
    inverse_r = 1.0 / ((1.0 - (SHELLS - 1 - shell8) * RADIAL_STEP) * ht)
    upper = sub8 < 4

    row_jobs = []
    for jobs in (
        ((0, -near(2), -near(1)), (1, 0.0, -near(2))),
        ((CT - 1, near(1), near(2)), (CT - 2, near(2), 0.0)),
    ):
        row_jobs.append([])
        for row, one_w, two_w in jobs:
            th = angle_t(jnp.full((8, 128), row, jnp.float32))
            s8, c8 = jnp.sin(th), jnp.cos(th)
            row_jobs[-1].append((row, jnp.where(upper, one_w, two_w) * inverse_r, (c8 * cf, c8 * sf, -s8)))

    def add_rows(side, fields):
        terms = cell_terms(fields)
        for row, scale, e in row_jobs[side]:
            where = pl.ds(row, SHELLS, stride=CT)
            for f, value in enumerate(flux_along(terms, e)):
                value = value * scale
                acc[f, where, :] = acc[f, where, :] - (value[0:4] + value[4:8])

    rim = (lanes < 2) | (lanes >= CP - 2)

    sub4 = lax.broadcasted_iota(jnp.int32, (4, 128), 0)
    lane4 = lax.broadcasted_iota(jnp.int32, (4, 128), 1)
    th = angle_t(lax.rem(lane4, CT).astype(jnp.float32))
    shell4 = (lane4 // CT).astype(jnp.float32)
    share = 1.0 / ((1.0 - (SHELLS - 1 - shell4) * RADIAL_STEP) * jnp.sin(th) * hp)
    column_jobs = []
    for from_left, from_right, weights in (
        (0, CP - 1, (-near(2), -near(1), near(1), near(2))),
        (1, CP - 2, (0.0, -near(2), near(2), 0.0)),
    ):
        ph = angle_f(jnp.where(sub4 < 2, from_left, from_right).astype(jnp.float32))
        scale = jnp.where(
            sub4 < 2,
            jnp.where(sub4 == 0, weights[0], weights[1]),
            jnp.where(sub4 == 2, weights[2], weights[3]),
        ) * share
        column_jobs.append((scale, (-jnp.sin(ph), jnp.cos(ph), None)))

    def add_columns():
        u = [jnp.concatenate([col_in[0, f], col_in[1, f]], axis=0) for f in range(FIELDS)]
        terms = cell_terms(u)
        parts = [[v * scale for v in flux_along(terms, e)] for scale, e in column_jobs]
        lines = []
        for f in range(FIELDS):
            close, far = parts[0][f], parts[1][f]
            lines += [far[2:3] + far[3:4], close[2:3] + close[3:4], close[0:1] + close[1:2], far[0:1] + far[1:2]]
        stood = jnp.concatenate(lines + [jnp.zeros((TALL - 4 * FIELDS, CP), jnp.float32)], axis=0).T
        for f in range(FIELDS):
            shift = (CP - 2 - 4 * f) % CP
            acc[f] = acc[f] - jnp.where(rim, pltpu.roll(stood, shift, 1) if shift else stood, 0.0)

    pl.when(left)(to_right.wait_recv)
    pl.when(right)(to_left.wait_recv)
    pl.when(left & right)(add_columns)

    @pl.when(up)
    def _():
        to_down.wait_recv()
        add_rows(0, [row_in[0, f] for f in range(FIELDS)])

    @pl.when(down)
    def _():
        to_up.wait_recv()
        add_rows(1, [row_in[1, f] for f in range(FIELDS)])

    def name(kind, lines):
        for r, line in enumerate(lines):
            named[kind, r] = line

    def name_row(side):
        name(0, [jnp.broadcast_to(wanted[0, 0, :, pl.ds(256 * side + 128 * r, 128)], (8, 128)) for r in range(2)])

    def name_column(side):
        line = jnp.broadcast_to(wanted[0, 0, :, pl.ds(512, 128)], (8, 128))
        name(1, [lanes_at(line, 64 * side + 2 * lax.rem(lane8, CT) + r) for r in range(2)])

    pl.when(c == 0)(lambda: name_row(0))
    pl.when(c == nc - 1)(lambda: name_row(1))
    pl.when(l == 0)(lambda: name_column(0))
    pl.when(l == nl - 1)(lambda: name_column(1))

    def pick_ghosts(kind, group, fresh):
        for r in range(2):
            index = named[kind, r]
            owner = index // SLOTS
            lane = lax.rem(index, SLOTS)
            found = [None if fresh else picked[kind, r, 8 * m : 8 * m + 8, :] for m in range(4)]
            for j in range(3 * group, 3 * group + 3):
                here = owner == others[j][0] * nc + others[j][1]
                for m in range(4):
                    value = lanes_at(slots_in[j, 8 * m : 8 * m + 8, :], lane)
                    found[m] = value if found[m] is None else jnp.where(here, value, found[m])
            for m in range(4):
                picked[kind, r, 8 * m : 8 * m + 8, :] = found[m]

    pass_on = [
        remote(slots_in.at[3:6], slots_in.at[6:9], 3, 2, p, l - 1, c),
        remote(slots_in.at[3:6], slots_in.at[0:3], 3, 0, p, l + 1, c),
    ]
    to_mate = [
        remote(slots_in.at[3 * group : 3 * group + 2], slots_in.at[3 * group + 1 : 3 * group + 3], 4, group, p, l, c - 1)
        for group in range(3)
    ]
    for turn, group in enumerate((1, 0, 2)):
        pl.when(edge)(whole(0, group, slots_in.at[3 * group : 3 * group + 3]).wait_recv)
        if group == 1:
            pl.when(pass_left)(pass_on[0].start)
            pl.when(pass_right)(pass_on[1].start)
        pl.when(mate_gives)(to_mate[group].start)
        pl.when(row_edge)(lambda: pick_ghosts(0, group, turn == 0))
        pl.when(at_end)(lambda: pick_ghosts(1, group, turn == 0))

    @pl.when(at_end)
    def _():
        side = jnp.where(l == 0, 0, 1)
        mine = lane8 // CT == lax.rem(sub8, 4)
        for r in range(2):
            for m in range(4):
                own = jnp.where(mine, picked[1, r, 8 * m : 8 * m + 8, :], 0.0)
                own = own + pltpu.roll(own, 7, 0)
                own = own + pltpu.roll(own, 6, 0)
                col_in[side, 2 * m, r : r + 1, :] = own[0:1]
                col_in[side, 2 * m + 1, r : r + 1, :] = own[4:5]
        add_columns()

    def add_ghost_rows(side):
        fields = [
            jnp.concatenate([picked[0, r, SHELLS * f : SHELLS * f + SHELLS, :] for r in range(2)], axis=0)
            for f in range(FIELDS)
        ]
        add_rows(side, fields)

    pl.when(c == 0)(lambda: add_ghost_rows(0))
    pl.when(c == nc - 1)(lambda: add_ghost_rows(1))

    def wait_sent(sent, number, sets):
        for n in range(1, len(sets) + 1):
            pl.when(number == n)(whole(sent, 0, sets[n - 1]).wait_send)

    number = 0
    for flow in flows_out:
        number = number + one(flow)
    wait_sent(0, number, [slots_in.at[0:n] for n in range(1, 10)])
    wait_sent(1, one(up) + one(down), [row_in.at[0:n] for n in (1, 2)])
    wait_sent(2, one(left) + one(right), [col_in.at[0:n] for n in (1, 2)])
    wait_sent(3, one(pass_left) + one(pass_right), [slots_in.at[0:n] for n in (3, 6)])
    pl.when(mate_gives)(whole(4, 0, slots_in.at[0:6]).wait_send)


def body(state_now, send_row, send_col, send_weight, ghost_slot):
    f32, i32 = jnp.float32, jnp.int32
    out = pl.pallas_call(
        kernel,
        out_shape=pltpu.VMEM((FIELDS, TALL, CP), f32),
        in_specs=[pl.BlockSpec(memory_space=pltpu.HBM)] * 5,
        out_specs=pl.BlockSpec(memory_space=pltpu.VMEM),
        scratch_shapes=[
            pltpu.VMEM((FIELDS, TALL, CP), f32),
            pltpu.VMEM((1, 1, 1, SLOTS), i32),
            pltpu.VMEM((1, 1, 1, SLOTS), i32),
            pltpu.VMEM((1, 1, 1, 4, SLOTS), f32),
            pltpu.VMEM((1, 1, 1, 640), i32),
            pltpu.VMEM((FIELDS * SHELLS, SLOTS), f32),
            pltpu.VMEM((9, FIELDS * SHELLS, SLOTS), f32),
            pltpu.VMEM((2, FIELDS, 8, CP), f32),
            pltpu.VMEM((2, FIELDS, 8, CP), f32),
            pltpu.VMEM((2, FIELDS, 2, TALL), f32),
            pltpu.VMEM((2, FIELDS, 2, TALL), f32),
            pltpu.VMEM((FIELDS, TALL, CP), f32),
            pltpu.VMEM((FIELDS, TALL, CP), f32),
            pltpu.VMEM((FIELDS, TALL, CP), f32),
            pltpu.VMEM((2, 2, FIELDS * SHELLS, CP), f32),
            pltpu.VMEM((2, 2, 8, CP), i32),
            pltpu.SemaphoreType.DMA((6,)),
            pltpu.SemaphoreType.DMA((5,)),
            pltpu.SemaphoreType.DMA((7,)),
            pltpu.SemaphoreType.REGULAR,
        ],
        compiler_params=pltpu.CompilerParams(
            collective_id=0, has_side_effects=True, vmem_limit_bytes=32 * 1024 * 1024
        ),
    )(*[pltpu.with_memory_space_constraint(a, pltpu.HBM) for a in (state_now.reshape(FIELDS, TALL, CP), send_row, send_col, send_weight, ghost_slot)])
    return out.reshape(1, FIELDS, SHELLS, CT, CP)


def solution(mesh):
    placed = (
        P("panel", None, None, "colat", "lon"),
        P("panel", "lon", "colat", None),
        P("panel", "lon", "colat", None),
        P("panel", "lon", "colat", None, None),
        P("panel", "lon", "colat", None),
    )
    return jax.shard_map(
        body,
        mesh=mesh,
        in_specs=placed,
        out_specs=P("panel", None, None, "colat", "lon"),
        check_vma=False,
    )
```

```python
import math

import jax
import jax.numpy as jnp
from jax import lax
from jax.experimental import pallas as pl
from jax.experimental.pallas import tpu as pltpu
from jax.sharding import PartitionSpec as P

RADIAL_STEP = 0.65 / 511.0
COURANT = 0.3
ROTATION = 300.0
GRAVITY = 300.0
ADIABATIC = 2.0 / 3.0

FIELDS = 8
SHELLS = 4
CT = 32
CP = 128
SLOTS = 128
TALL = SHELLS * CT
MESH = pl.DeviceIdType.MESH
RUN = 8
AROUND = [(dl, dc) for dl in (-1, 0, 1) for dc in (-1, 0, 1)]
SEND_ORDER = (2, 1, 0, 5, 4, 3, 8, 7, 6)
TURNED = [(0, 1.0), (1, -1.0), (3, 1.0), (2, 1.0), (4, -1.0), (6, 1.0), (5, 1.0), (7, 1.0)]


def lanes_at(values, index):
    return jnp.take_along_axis(values, index, axis=1, mode="promise_in_bounds")


def cell_terms(u):
    rho, m, b, energy = u[0], u[1:4], u[4:7], u[7]
    inverse = 1.0 / rho
    v = [a * inverse for a in m]
    power = b[0] * b[0] + b[1] * b[1] + b[2] * b[2]
    moving = m[0] * v[0] + m[1] * v[1] + m[2] * v[2]
    pressure = ADIABATIC * (energy - 0.5 * moving - 0.5 * power) + 0.5 * power
    aligned = v[0] * b[0] + v[1] * b[1] + v[2] * b[2]
    return m, b, v, pressure, energy + pressure, aligned, rho


def flux_along(terms, e):
    m, b, v, pressure, enthalpy, aligned, rho = terms
    ve = v[0] * e[0] + v[1] * e[1]
    be = b[0] * e[0] + b[1] * e[1]
    if e[2] is not None:
        ve = ve + v[2] * e[2]
        be = be + b[2] * e[2]
    out = [rho * ve]
    for i in range(3):
        term = m[i] * ve - b[i] * be
        out.append(term if e[i] is None else term + pressure * e[i])
    for i in range(3):
        out.append(b[i] * ve - v[i] * be)
    out.append(enthalpy * ve - aligned * be)
    return out


def kernel(
    x_hbm, row_hbm, col_hbm, weight_hbm, ghost_hbm, acc,
    x, rows, cols, weight, wanted,
    slots, slots_in, row_out, row_in, col_out, col_in,
    radial, polar, azimuth, picked, named,
    in_sem, send_sem, recv_sem, told,
):
    p, l, c = lax.axis_index("panel"), lax.axis_index("lon"), lax.axis_index("colat")
    nl, nc = lax.axis_size("lon"), lax.axis_size("colat")
    ht = 0.5 * math.pi / (nc * CT)
    hp = 1.5 * math.pi / (nl * CP)
    tau = COURANT / (1.0 / RADIAL_STEP + 1.0 / ht + 1.0 / (hp * math.sin(0.25 * math.pi)))

    def wrap(a, n):
        return lax.rem(a + n, n)

    def on_row(ca):
        return (ca == 0) | (ca == nc - 1)

    def on_edge(la, ca):
        return (la == 0) | (la == nl - 1) | on_row(ca)

    small = [
        pltpu.make_async_copy(src, dst, in_sem.at[2 + i])
        for i, (src, dst) in enumerate(
            ((row_hbm, rows), (col_hbm, cols), (weight_hbm, weight), (ghost_hbm, wanted))
        )
    ]
    half = FIELDS // 2
    large = [
        pltpu.make_async_copy(x_hbm.at[half * i : half * (i + 1)], x.at[half * i : half * (i + 1)], in_sem.at[i]) for i in range(2)
    ]
    for load in small + large:
        load.start()

    up, down, left, right = c > 0, c < nc - 1, l > 0, l < nl - 1
    edge = on_edge(l, c)
    others = [(wrap(l + dl, nl), wrap(c + dc, nc)) for dl, dc in AROUND]

    late_left, late_right = 4, 4
    place = lax.rem(l, RUN)

    def passed(panel, tile, la):
        late = jnp.where(la < tile, late_left, late_right)
        far = (panel == 1) | ((lax.rem(tile, RUN) >= late) & (lax.rem(la, RUN) != RUN - 1))
        return far & (tile // RUN == la // RUN)

    def straight_from(panel, tile, ca, la):
        return (panel == 0) & (lax.rem(tile, RUN) == 5) & (ca == 0) & (la > tile)

    flows_out, direct_in, shut_out, shut_in = [], [], [], []
    beside = (c < 2) | (c >= nc - 2)
    to_panel_1 = p == 0
    for (la, ca), (dl, dc) in zip(others, AROUND):
        flow, got = on_edge(la, ca), edge
        if dl:
            flow = flow & ~(on_row(ca) & passed(1 - p, la, l) & ~straight_from(1 - p, la, ca, l))
            got = got & ~(on_row(c) & passed(p, l, la) & ~straight_from(p, l, c, la))
        if dc != 1:
            flow = flow & ~((p == 1) & (la == 0) & (lax.rem(ca, 2) == 0))
        else:
            flow = flow & ~((p == 1) & (la == 0) & (ca == 0))
        if dc != -1:
            got = got & ~((p == 0) & (l == 0) & (lax.rem(c, 2) == 0))
        else:
            got = got & ~((p == 0) & (l == 0) & (c == 0))
        flows_out.append(flow)
        direct_in.append(got)
        shut = ((place == RUN - 1) & (dl <= 0)) | ((place == 0) & (dl == -1))
        if dl == 1:
            shut = shut | ((l == nl - 2) & beside)
        shut_out.append((p == 1) & shut)
        shut = ((place == RUN - 1) & (dl >= 0)) | ((place == RUN - 2) & (dl == 1))
        if dl == -1:
            shut = shut | ((l == nl - 1) & ((ca < 2) | (ca >= nc - 2)))
        shut_in.append((p == 0) & shut)
    row_edge = on_row(c)
    pass_left = row_edge & left & passed(p, l - 1, l) & ~straight_from(p, l - 1, c, l)
    pass_right = row_edge & right & passed(p, l + 1, l)
    mate_gives = (p == 0) & (l == 0) & (lax.rem(c, 2) == 1)
    mate_takes = (p == 0) & (l == 0) & (lax.rem(c, 2) == 0)

    inner = jnp.clip(c, 2, nc - 3)
    at_seam = (place == 0) | (place == RUN - 1)
    at_end = (l == 0) | (l == nl - 1)
    helped_1 = (p == 1) & ((at_seam & (beside | at_end)) | ((l == nl - 2) & beside))
    helped_0 = (p == 0) & (place == RUN - 1) & (beside | at_end)
    at_helper = (c == 2) | (c == nc - 3)
    helper_1 = (p == 1) & at_seam & ~at_end & at_helper
    helper_0 = (p == 0) & (place == RUN - 2) & (l != nl - 2) & at_helper
    end_helper = (l == nl - 2) & ~beside
    over_left, over_right = left & (place == 0), right & (place == RUN - 1)
    seam_by_help = helped_1 & at_seam & ~at_end
    near_left, near_right = left & ~(over_left & seam_by_help), right & ~(over_right & seam_by_help)

    barrier = pltpu.get_barrier_semaphore()

    def greet(*device):
        pl.semaphore_signal(barrier, inc=1, device_id=device, device_id_type=MESH)

    for j, (la, ca) in enumerate(others):
        by_help = (p == 1) & (lax.rem(la, RUN) == RUN - 1)
        to_l = jnp.where(by_help, la - 1, la)
        to_c = jnp.where(by_help, jnp.clip(ca, 2, nc - 3), ca)
        pl.when(direct_in[j] & ~shut_in[j])(lambda: greet(1 - p, to_l, to_c))

    corner, opposite = (p == 0) & (l == 0) & (c == 0), (p == 0) & (l == 0) & (c == nc - 1)
    pl.when(corner)(lambda: greet(p, l, nc - 1))
    pl.when(near_left)(lambda: greet(p, l - 1, c))
    pl.when(near_right)(lambda: greet(p, l + 1, c))
    pl.when(up)(lambda: greet(p, l, c - 1))
    pl.when(down)(lambda: greet(p, l, c + 1))

    @pl.when(helped_0 | helped_1)
    def _():
        greet(p, jnp.where(at_end, nl - 2, jnp.where(p == 0, l - 1, l)), inner)
        pl.when(seam_by_help)(lambda: greet(p, jnp.where(place == 0, l - 1, l + 1), inner))

    @pl.when((p == 0) & (l < nl - 1) & row_edge & (place >= RUN - 2))
    def _():
        end = l == nl - 2
        last = jnp.where(end, l, l - place + RUN - 1)
        for helper in (2, nc - 3):
            greet(1, last, helper)
            pl.when(place == RUN - 1)(lambda: greet(1, l + 1, helper))

    @pl.when((p == 0) & (l == nl - 1))
    def _():
        for helper in range(2, nc - 2):
            reach = (c >= helper - 1) & (c <= helper + 1)
            if helper == 2:
                reach = (c <= helper + 1) | (c == nc - 1)
            if helper == nc - 3:
                reach = (c >= helper - 1) | (c == 0)
            pl.when(reach)(lambda: greet(1, nl - 2, helper))

    for load in small:
        load.wait()

    row_at = lax.broadcasted_iota(jnp.int32, (CT, CP), 0)
    lane8 = lax.broadcasted_iota(jnp.int32, (8, 128), 1)
    sub8 = lax.broadcasted_iota(jnp.int32, (8, 128), 0)
    lane32 = lax.broadcasted_iota(jnp.int32, (CT, CP), 1)
    first = row_at == rows[0, 0]
    second = row_at == rows[0, 0] + 1
    w = weight[0, 0, 0]
    on_left = jnp.where(first, w[0:1], jnp.where(second, w[2:3], 0.0))
    on_right = jnp.where(first, w[1:2], jnp.where(second, w[3:4], 0.0))
    pick = jnp.broadcast_to(cols[0, 0], (CT, CP))
    pick_next = pick + 1
    halves = [(h, lax.rem(sub8 // h, 2) == 0) for h in (4, 2)]

    def fold(a, b, step):
        h, low = halves[step]
        if h == 4:
            return jnp.where(low, a, b) + pltpu.roll(jnp.where(low, b, a), 4, 0)
        return jnp.where(low, a + pltpu.roll(a, 6, 0), b + pltpu.roll(b, 2, 0))

    for f in range(FIELDS):
        if f % half == 0:
            large[f // half].wait()
        target, sign = TURNED[f]
        sums = []
        for k in range(SHELLS):
            plane = x[f, CT * k : CT * (k + 1), :]
            mixed = on_left * lanes_at(plane, pick) + on_right * lanes_at(plane, pick_next)
            sums.append((mixed[0:8] + mixed[8:16]) + (mixed[16:24] + mixed[24:32]))
        four = fold(fold(sums[0], sums[2], 0), fold(sums[1], sums[3], 0), 1)
        both = four + pltpu.roll(four, 7, 0)
        for k in range(SHELLS):
            line = both[2 * k : 2 * k + 1]
            at = SHELLS * target + k
            slots[at : at + 1, :] = line if sign > 0 else -line

    lanes = lax.broadcasted_iota(jnp.int32, (TALL, CP), 1)
    packed = jnp.zeros((TALL, CP), jnp.float32)
    for f in range(FIELDS):
        for r in range(2):
            row_out[0, f, pl.ds(4 * r, 4), :] = x[f, pl.ds(r, SHELLS, stride=CT), :]
            row_out[1, f, pl.ds(4 * r, 4), :] = x[f, pl.ds(CT - 2 + r, SHELLS, stride=CT), :]
        turned = pltpu.roll(x[f], 2 + 4 * f, 1)
        packed = jnp.where(lanes // 4 == f, turned, packed)
    upright = packed.T
    for f in range(FIELDS):
        col_out[1, f] = upright[4 * f : 4 * f + 2]
        col_out[0, f] = upright[4 * f + 2 : 4 * f + 4]

    row0 = (c * CT).astype(jnp.float32) + 0.5
    col0 = (l * CP).astype(jnp.float32) + 0.5

    def angle_t(row):
        return 0.25 * math.pi + (row + row0) * ht

    def angle_f(col):
        return -0.75 * math.pi + (col + col0) * hp

    theta = angle_t(row_at.astype(jnp.float32))
    phi = angle_f(lane8[0:1].astype(jnp.float32))
    st, ct = jnp.sin(theta), jnp.cos(theta)
    sf = jnp.broadcast_to(jnp.sin(phi), (8, CP))
    cf = jnp.broadcast_to(jnp.cos(phi), (8, CP))
    spin_second = ROTATION * p.astype(jnp.float32)
    spin_third = ROTATION - spin_second

    def one_block(n, _):
        at = pl.multiple_of(n * 8, 8)
        th = angle_t((sub8 + lax.rem(n, CT // 8) * 8).astype(jnp.float32))
        s8, c8 = jnp.sin(th), jnp.cos(th)
        u = [x[f, pl.ds(at, 8), :] for f in range(FIELDS)]
        terms = cell_terms(u)
        er = (s8 * cf, s8 * sf, c8)
        for f, value in enumerate(flux_along(terms, er)):
            radial[f, pl.ds(at, 8), :] = value
        for f, value in enumerate(flux_along(terms, (c8 * cf, c8 * sf, -s8))):
            polar[f, pl.ds(at, 8), :] = value
        for f, value in enumerate(flux_along(terms, (-sf, cf, None))):
            azimuth[f, pl.ds(at, 8), :] = value
        rho, m = u[0], u[1:4]
        turn = (
            spin_second * m[2] - spin_third * m[1], spin_third * m[0], -spin_second * m[0]
        )
        acc[0, pl.ds(at, 8), :] = u[0]
        for i in range(3):
            acc[1 + i, pl.ds(at, 8), :] = m[i] - tau * (2.0 * turn[i] + GRAVITY * (rho * er[i]))
            acc[4 + i, pl.ds(at, 8), :] = u[4 + i]
        acc[7, pl.ds(at, 8), :] = u[7] - (tau * GRAVITY) * (m[0] * er[0] + m[1] * er[1] + m[2] * er[2])
        return 0

    ends = {1: 8.0 / 12.0, 2: -1.0 / 12.0}

    def gives(along, across, n, step):
        even = (ends[n] / step * math.cos(n * step)) * along
        odd = (ends[n] / step * math.sin(n * step)) * across
        return even + odd, odd - even

    radius = [1.0 - (SHELLS - 1 - k) * RADIAL_STEP for k in range(SHELLS)]

    def one_field(f, _):
        fr = [radial[f, pl.ds(CT * k, CT), :] for k in range(SHELLS)]
        for k in range(SHELLS):
            here = pl.ds(CT * k, CT)
            ft, fp = polar[f, here, :], azimuth[f, here, :]
            flat = st * fr[k] + ct * ft
            total_t = jnp.zeros((CT, CP), jnp.float32)
            total_p = total_t
            for n in (1, 2):
                before, after = gives(ft, fr[k], n, ht)
                total_t = total_t + jnp.where(row_at < CT - n, pltpu.roll(before, CT - n, 0), 0.0)
                total_t = total_t + jnp.where(row_at >= n, pltpu.roll(after, n, 0), 0.0)
                before, after = gives(fp, flat, n, hp)
                total_p = total_p + jnp.where(lane32 < CP - n, pltpu.roll(before, CP - n, 1), 0.0)
                total_p = total_p + jnp.where(lane32 >= n, pltpu.roll(after, n, 1), 0.0)
            low, high = max(k - 1, 0), min(k + 1, SHELLS - 1)
            slope = (fr[high] - fr[low]) * (1.0 / ((high - low) * RADIAL_STEP))
            whole = slope + (1.0 / radius[k]) * (total_t + total_p / st)
            acc[f, here, :] = acc[f, here, :] - tau * whole
        return 0

    def own_cells():
        lax.fori_loop(0, TALL // 8, one_block, 0)
        lax.fori_loop(0, FIELDS, one_field, 0)

    idle = (p == 0) & (place < RUN - 1)
    pl.when(idle)(own_cells)

    def one(flag):
        return flag.astype(jnp.int32)

    expected = one(up) + one(down) + one(near_left) + one(near_right)
    for flow, shut in zip(flows_out, shut_out):
        expected = expected + one(flow & ~shut & ~helped_0)
    expected = expected + one(opposite)
    expected = expected + one(helper_1) * (6 + 2 * one(place == RUN - 1)) + 8 * one(helper_0)
    served = jnp.where(at_helper, 3, 1)
    at_panel_1 = 2 * served + jnp.where(at_helper, 9, 3)
    expected = expected + one(end_helper) * jnp.where(p == 1, at_panel_1, 7 * served)
    pl.semaphore_wait(barrier, expected)

    def remote(src, dst, sent, arrived, *device):
        return pltpu.make_async_remote_copy(
            src_ref=src, dst_ref=dst, send_sem=send_sem.at[sent], recv_sem=recv_sem.at[arrived],
            device_id=device, device_id_type=MESH,
        )

    slot_copies = [
        remote(slots, slots_in.at[8 - j], 0, (8 - j) // 3, 1 - p, la, ca) for j, (la, ca) in enumerate(others)
    ]

    def whole(sent, arrived, sets):
        return remote(sets, sets, sent, arrived, 1 - p, l, c)

    def send_slots(wave):
        for j in SEND_ORDER:
            la, ca = others[j]
            spot = lax.rem(la, RUN)
            turn = jnp.where((p == 0) | ((spot == 5) & (place == 6)), 2, jnp.where(spot == 1, 0, 1))
            pl.when(flows_out[j] & ~shut_out[j] & ~helped_0 & (turn == wave))(slot_copies[j].start)

    send_slots(0)
    send_slots(1)

    def tell(*device):
        pl.semaphore_signal(told, inc=1, device_id=device, device_id_type=MESH)

    @pl.when(helper_0 | helper_1)
    def _():
        first = jnp.where(c == 2, 0, nc - 2)
        for more in range(2):
            tell(p, jnp.where(p == 0, l + 1, l), first + more)

    @pl.when(end_helper)
    def _():
        tell(p, nl - 1, c)
        pl.when(p == 1)(lambda: tell(p, 0, c))

        @pl.when(at_helper)
        def _():
            first = jnp.where(c == 2, 0, nc - 2)
            for more in range(2):
                tell(p, nl - 1, first + more)
                pl.when(p == 1)(lambda: tell(p, 0, first + more))
                pl.when(p == 1)(lambda: tell(p, nl - 2, first + more))

    to_up = remote(row_out.at[0], row_in.at[1], 1, 4, p, l, c - 1)
    to_down = remote(row_out.at[1], row_in.at[0], 1, 3, p, l, c + 1)
    to_left = remote(col_out.at[0], col_in.at[1], 2, 6, p, l - 1, c)
    to_right = remote(col_out.at[1], col_in.at[0], 2, 5, p, l + 1, c)
    pl.when(near_left)(to_left.start)
    pl.when(near_right)(to_right.start)
    pl.when(up)(to_up.start)
    pl.when(down)(to_down.start)
    send_slots(2)

    pl.when(~idle)(own_cells)

    @pl.when(helped_0 | helped_1)
    def _():
        pl.semaphore_wait(told, 1)
        pl.when(over_left & seam_by_help)(to_left.start)
        pl.when(over_right & seam_by_help)(to_right.start)
        for j in SEND_ORDER:
            pl.when(flows_out[j] & (shut_out[j] | helped_0))(slot_copies[j].start)

    def near(n):
        return tau * ends[n]

    shell8 = lax.rem(sub8, 4).astype(jnp.float32)
    inverse_r = 1.0 / ((1.0 - (SHELLS - 1 - shell8) * RADIAL_STEP) * ht)
    upper = sub8 < 4

    row_jobs = []
    for jobs in (
        ((0, -near(2), -near(1)), (1, 0.0, -near(2))),
        ((CT - 1, near(1), near(2)), (CT - 2, near(2), 0.0)),
    ):
        row_jobs.append([])
        for row, one_w, two_w in jobs:
            th = angle_t(jnp.full((8, 128), row, jnp.float32))
            s8, c8 = jnp.sin(th), jnp.cos(th)
            row_jobs[-1].append((row, jnp.where(upper, one_w, two_w) * inverse_r, (c8 * cf, c8 * sf, -s8)))

    def add_rows(side, fields):
        terms = cell_terms(fields)
        for row, scale, e in row_jobs[side]:
            where = pl.ds(row, SHELLS, stride=CT)
            for f, value in enumerate(flux_along(terms, e)):
                value = value * scale
                acc[f, where, :] = acc[f, where, :] - (value[0:4] + value[4:8])

    rim = (lanes < 2) | (lanes >= CP - 2)

    sub4 = lax.broadcasted_iota(jnp.int32, (4, 128), 0)
    lane4 = lax.broadcasted_iota(jnp.int32, (4, 128), 1)
    th = angle_t(lax.rem(lane4, CT).astype(jnp.float32))
    shell4 = (lane4 // CT).astype(jnp.float32)
    share = 1.0 / ((1.0 - (SHELLS - 1 - shell4) * RADIAL_STEP) * jnp.sin(th) * hp)
    column_jobs = []
    for from_left, from_right, weights in (
        (0, CP - 1, (-near(2), -near(1), near(1), near(2))),
        (1, CP - 2, (0.0, -near(2), near(2), 0.0)),
    ):
        ph = angle_f(jnp.where(sub4 < 2, from_left, from_right).astype(jnp.float32))
        scale = jnp.where(
            sub4 < 2,
            jnp.where(sub4 == 0, weights[0], weights[1]),
            jnp.where(sub4 == 2, weights[2], weights[3]),
        ) * share
        column_jobs.append((scale, (-jnp.sin(ph), jnp.cos(ph), None)))

    def add_columns():
        u = [jnp.concatenate([col_in[0, f], col_in[1, f]], axis=0) for f in range(FIELDS)]
        terms = cell_terms(u)
        parts = [[v * scale for v in flux_along(terms, e)] for scale, e in column_jobs]
        lines = []
        for f in range(FIELDS):
            close, far = parts[0][f], parts[1][f]
            lines += [far[2:3] + far[3:4], close[2:3] + close[3:4], close[0:1] + close[1:2], far[0:1] + far[1:2]]
        stood = jnp.concatenate(lines + [jnp.zeros((TALL - 4 * FIELDS, CP), jnp.float32)], axis=0).T
        for f in range(FIELDS):
            shift = (CP - 2 - 4 * f) % CP
            acc[f] = acc[f] - jnp.where(rim, pltpu.roll(stood, shift, 1) if shift else stood, 0.0)

    def name(kind, lines):
        for r, line in enumerate(lines):
            named[kind, r] = line

    def name_row(side):
        name(0, [jnp.broadcast_to(wanted[0, 0, :, pl.ds(256 * side + 128 * r, 128)], (8, 128)) for r in range(2)])

    def name_column(side):
        line = jnp.broadcast_to(wanted[0, 0, :, pl.ds(512, 128)], (8, 128))
        name(1, [lanes_at(line, 64 * side + 2 * lax.rem(lane8, CT) + r) for r in range(2)])

    pl.when(c == 0)(lambda: name_row(0))
    pl.when(c == nc - 1)(lambda: name_row(1))
    pl.when(l == 0)(lambda: name_column(0))
    pl.when(l == nl - 1)(lambda: name_column(1))

    def pick_ghosts(kind, group, fresh):
        for r in range(2):
            index = named[kind, r]
            owner = index // SLOTS
            lane = lax.rem(index, SLOTS)
            found = [None if fresh else picked[kind, r, 8 * m : 8 * m + 8, :] for m in range(4)]
            for j in range(3 * group, 3 * group + 3):
                here = owner == others[j][0] * nc + others[j][1]
                for m in range(4):
                    value = lanes_at(slots_in[j, 8 * m : 8 * m + 8, :], lane)
                    found[m] = value if found[m] is None else jnp.where(here, value, found[m])
            for m in range(4):
                picked[kind, r, 8 * m : 8 * m + 8, :] = found[m]

    def add_panel_rims():
        pl.when(left)(to_right.wait_recv)
        pl.when(right)(to_left.wait_recv)
        pl.when(left & right)(add_columns)

        @pl.when(up)
        def _():
            to_down.wait_recv()
            add_rows(0, [row_in[0, f] for f in range(FIELDS)])

        @pl.when(down)
        def _():
            to_up.wait_recv()
            add_rows(1, [row_in[1, f] for f in range(FIELDS)])

    straight = (p == 0) & (place < 4)
    pl.when(~straight)(add_panel_rims)

    pass_on = [
        remote(slots_in.at[3:6], slots_in.at[6:9], 3, 2, p, l - 1, c),
        remote(slots_in.at[3:6], slots_in.at[0:3], 3, 0, p, l + 1, c),
    ]
    to_mate = [
        remote(slots_in.at[3 * group : 3 * group + 2], slots_in.at[3 * group + 1 : 3 * group + 3], 4, group, p, l, c - 1)
        for group in range(3)
    ]
    to_corner = [remote(slots_in.at[3 * g + 1], slots_in.at[3 * g], 4, g, p, l, 0) for g in range(3)]
    for turn, group in enumerate((1, 0, 2)):
        pl.when(edge)(whole(0, group, slots_in.at[3 * group : 3 * group + 3]).wait_recv)
        if group == 1:
            pl.when(pass_left)(pass_on[0].start)
            pl.when(pass_right)(pass_on[1].start)
        pl.when(mate_gives)(to_mate[group].start)
        pl.when(opposite)(to_corner[group].start)
        pl.when(row_edge)(lambda: pick_ghosts(0, group, turn == 0))
        pl.when(at_end)(lambda: pick_ghosts(1, group, turn == 0))

    pl.when(straight)(add_panel_rims)

    @pl.when(at_end)
    def _():
        side = jnp.where(l == 0, 0, 1)
        mine = lane8 // CT == lax.rem(sub8, 4)
        for r in range(2):
            for m in range(4):
                own = jnp.where(mine, picked[1, r, 8 * m : 8 * m + 8, :], 0.0)
                own = own + pltpu.roll(own, 7, 0)
                own = own + pltpu.roll(own, 6, 0)
                col_in[side, 2 * m, r : r + 1, :] = own[0:1]
                col_in[side, 2 * m + 1, r : r + 1, :] = own[4:5]
        add_columns()

    def add_ghost_rows(side):
        fields = [
            jnp.concatenate([picked[0, r, SHELLS * f : SHELLS * f + SHELLS, :] for r in range(2)], axis=0)
            for f in range(FIELDS)
        ]
        add_rows(side, fields)

    pl.when(c == 0)(lambda: add_ghost_rows(0))
    pl.when(c == nc - 1)(lambda: add_ghost_rows(1))

    def wait_sent(sent, number, sets):
        for n in range(1, len(sets) + 1):
            pl.when(number == n)(whole(sent, 0, sets[n - 1]).wait_send)

    number = 0
    for flow in flows_out:
        number = number + one(flow)
    wait_sent(0, number, [slots_in.at[0:n] for n in range(1, 10)])
    wait_sent(1, one(up) + one(down), [row_in.at[0:n] for n in (1, 2)])
    wait_sent(2, one(left) + one(right), [col_in.at[0:n] for n in (1, 2)])
    wait_sent(3, one(pass_left) + one(pass_right), [slots_in.at[0:n] for n in (3, 6)])
    pl.when(mate_gives & ~opposite)(whole(4, 0, slots_in.at[0:6]).wait_send)
    pl.when(opposite)(whole(4, 0, slots_in.at[0:9]).wait_send)


def body(state_now, send_row, send_col, send_weight, ghost_slot):
    f32, i32 = jnp.float32, jnp.int32
    out = pl.pallas_call(
        kernel,
        out_shape=pltpu.VMEM((FIELDS, TALL, CP), f32),
        in_specs=[pl.BlockSpec(memory_space=pltpu.HBM)] * 5,
        out_specs=pl.BlockSpec(memory_space=pltpu.VMEM),
        scratch_shapes=[
            pltpu.VMEM((FIELDS, TALL, CP), f32),
            pltpu.VMEM((1, 1, 1, SLOTS), i32),
            pltpu.VMEM((1, 1, 1, SLOTS), i32),
            pltpu.VMEM((1, 1, 1, 4, SLOTS), f32),
            pltpu.VMEM((1, 1, 1, 640), i32),
            pltpu.VMEM((FIELDS * SHELLS, SLOTS), f32),
            pltpu.VMEM((9, FIELDS * SHELLS, SLOTS), f32),
            pltpu.VMEM((2, FIELDS, 8, CP), f32),
            pltpu.VMEM((2, FIELDS, 8, CP), f32),
            pltpu.VMEM((2, FIELDS, 2, TALL), f32),
            pltpu.VMEM((2, FIELDS, 2, TALL), f32),
            pltpu.VMEM((FIELDS, TALL, CP), f32),
            pltpu.VMEM((FIELDS, TALL, CP), f32),
            pltpu.VMEM((FIELDS, TALL, CP), f32),
            pltpu.VMEM((2, 2, FIELDS * SHELLS, CP), f32),
            pltpu.VMEM((2, 2, 8, CP), i32),
            pltpu.SemaphoreType.DMA((6,)),
            pltpu.SemaphoreType.DMA((5,)),
            pltpu.SemaphoreType.DMA((7,)),
            pltpu.SemaphoreType.REGULAR,
        ],
        compiler_params=pltpu.CompilerParams(
            collective_id=0, has_side_effects=True, vmem_limit_bytes=32 * 1024 * 1024
        ),
    )(*[pltpu.with_memory_space_constraint(a, pltpu.HBM) for a in (state_now.reshape(FIELDS, TALL, CP), send_row, send_col, send_weight, ghost_slot)])
    return out.reshape(1, FIELDS, SHELLS, CT, CP)


def solution(mesh):
    placed = (
        P("panel", None, None, "colat", "lon"),
        P("panel", "lon", "colat", None),
        P("panel", "lon", "colat", None),
        P("panel", "lon", "colat", None, None),
        P("panel", "lon", "colat", None),
    )
    return jax.shard_map(
        body,
        mesh=mesh,
        in_specs=placed,
        out_specs=P("panel", None, None, "colat", "lon"),
        check_vma=False,
    )
```

```python
import math

import jax
import jax.numpy as jnp
from jax import lax
from jax.experimental import pallas as pl
from jax.experimental.pallas import tpu as pltpu
from jax.sharding import PartitionSpec as P

RADIAL_STEP = 0.65 / 511.0
COURANT = 0.3
ROTATION = 300.0
GRAVITY = 300.0
ADIABATIC = 2.0 / 3.0

FIELDS = 8
SHELLS = 4
CT = 32
CP = 128
SLOTS = 128
TALL = SHELLS * CT
MESH = pl.DeviceIdType.MESH
RUN = 8
AROUND = [(dl, dc) for dl in (-1, 0, 1) for dc in (-1, 0, 1)]
SEND_ORDER = (2, 1, 0, 5, 4, 3, 8, 7, 6)
TURNED = [(0, 1.0), (1, -1.0), (3, 1.0), (2, 1.0), (4, -1.0), (6, 1.0), (5, 1.0), (7, 1.0)]


def lanes_at(values, index):
    return jnp.take_along_axis(values, index, axis=1, mode="promise_in_bounds")


def cell_terms(u):
    rho, m, b, energy = u[0], u[1:4], u[4:7], u[7]
    inverse = 1.0 / rho
    v = [a * inverse for a in m]
    power = b[0] * b[0] + b[1] * b[1] + b[2] * b[2]
    moving = m[0] * v[0] + m[1] * v[1] + m[2] * v[2]
    pressure = ADIABATIC * (energy - 0.5 * moving - 0.5 * power) + 0.5 * power
    aligned = v[0] * b[0] + v[1] * b[1] + v[2] * b[2]
    return m, b, v, pressure, energy + pressure, aligned, rho


def flux_along(terms, e):
    m, b, v, pressure, enthalpy, aligned, rho = terms
    ve = v[0] * e[0] + v[1] * e[1]
    be = b[0] * e[0] + b[1] * e[1]
    if e[2] is not None:
        ve = ve + v[2] * e[2]
        be = be + b[2] * e[2]
    out = [rho * ve]
    for i in range(3):
        term = m[i] * ve - b[i] * be
        out.append(term if e[i] is None else term + pressure * e[i])
    for i in range(3):
        out.append(b[i] * ve - v[i] * be)
    out.append(enthalpy * ve - aligned * be)
    return out


def kernel(
    x_hbm, row_hbm, col_hbm, weight_hbm, ghost_hbm, acc,
    x, rows, cols, weight, wanted,
    slots, slots_in, row_out, row_in, col_out, col_in,
    radial, polar, azimuth, picked, named,
    in_sem, send_sem, recv_sem, told,
):
    p, l, c = lax.axis_index("panel"), lax.axis_index("lon"), lax.axis_index("colat")
    nl, nc = lax.axis_size("lon"), lax.axis_size("colat")
    ht = 0.5 * math.pi / (nc * CT)
    hp = 1.5 * math.pi / (nl * CP)
    tau = COURANT / (1.0 / RADIAL_STEP + 1.0 / ht + 1.0 / (hp * math.sin(0.25 * math.pi)))

    def wrap(a, n):
        return lax.rem(a + n, n)

    def on_row(ca):
        return (ca == 0) | (ca == nc - 1)

    def on_edge(la, ca):
        return (la == 0) | (la == nl - 1) | on_row(ca)

    small = [
        pltpu.make_async_copy(src, dst, in_sem.at[2 + i])
        for i, (src, dst) in enumerate(
            ((row_hbm, rows), (col_hbm, cols), (weight_hbm, weight), (ghost_hbm, wanted))
        )
    ]
    half = FIELDS // 2
    large = [
        pltpu.make_async_copy(x_hbm.at[half * i : half * (i + 1)], x.at[half * i : half * (i + 1)], in_sem.at[i]) for i in range(2)
    ]
    for load in small + large:
        load.start()

    up, down, left, right = c > 0, c < nc - 1, l > 0, l < nl - 1
    edge = on_edge(l, c)
    others = [(wrap(l + dl, nl), wrap(c + dc, nc)) for dl, dc in AROUND]

    late_left, late_right = 4, 4
    place = lax.rem(l, RUN)

    def passed(panel, tile, la):
        late = jnp.where(la < tile, late_left, late_right)
        far = (panel == 1) | ((lax.rem(tile, RUN) >= late) & (lax.rem(la, RUN) != RUN - 1))
        return far & (tile // RUN == la // RUN)

    def straight_from(panel, tile, ca, la):
        return (panel == 0) & (lax.rem(tile, RUN) == 5) & (ca == 0) & (la > tile)

    flows_out, direct_in, shut_out, shut_in = [], [], [], []
    beside = (c < 2) | (c >= nc - 2)
    to_panel_1 = p == 0
    for (la, ca), (dl, dc) in zip(others, AROUND):
        flow, got = on_edge(la, ca), edge
        if dl:
            flow = flow & ~(on_row(ca) & passed(1 - p, la, l) & ~straight_from(1 - p, la, ca, l))
            got = got & ~(on_row(c) & passed(p, l, la) & ~straight_from(p, l, c, la))
        if dc != 1:
            flow = flow & ~((p == 1) & (la == 0) & (lax.rem(ca, 2) == 0))
        else:
            flow = flow & ~((p == 1) & (la == 0) & (ca == 0))
        if dc != -1:
            got = got & ~((p == 0) & (l == 0) & (lax.rem(c, 2) == 0))
        else:
            got = got & ~((p == 0) & (l == 0) & (c == 0))
        flows_out.append(flow)
        direct_in.append(got)
        shut = ((place == RUN - 1) & (dl <= 0)) | ((place == 0) & (dl == -1))
        if dl == 1:
            shut = shut | ((l == nl - 2) & beside)
        shut_out.append((p == 1) & shut)
        shut = ((place == RUN - 1) & (dl >= 0)) | ((place == RUN - 2) & (dl == 1))
        if dl == -1:
            shut = shut | ((l == nl - 1) & ((ca < 2) | (ca >= nc - 2)))
        shut_in.append((p == 0) & shut)
    row_edge = on_row(c)
    pass_left = row_edge & left & passed(p, l - 1, l) & ~straight_from(p, l - 1, c, l)
    pass_right = row_edge & right & passed(p, l + 1, l)
    mate_gives = (p == 0) & (l == 0) & (lax.rem(c, 2) == 1)
    mate_takes = (p == 0) & (l == 0) & (lax.rem(c, 2) == 0)

    inner = jnp.clip(c, 2, nc - 3)
    at_seam = (place == 0) | (place == RUN - 1)
    at_end = (l == 0) | (l == nl - 1)
    helped_1 = (p == 1) & ((at_seam & (beside | at_end)) | ((l == nl - 2) & beside))
    helped_0 = (p == 0) & (place == RUN - 1) & (beside | at_end)
    at_helper = (c == 2) | (c == nc - 3)
    helper_1 = (p == 1) & at_seam & ~at_end & at_helper
    helper_0 = (p == 0) & (place == RUN - 2) & (l != nl - 2) & at_helper
    end_helper = (l == nl - 2) & ~beside
    over_left, over_right = left & (place == 0), right & (place == RUN - 1)
    seam_by_help = helped_1 & at_seam & ~at_end
    near_left, near_right = left & ~(over_left & seam_by_help), right & ~(over_right & seam_by_help)

    barrier = pltpu.get_barrier_semaphore()

    def greet(*device):
        pl.semaphore_signal(barrier, inc=1, device_id=device, device_id_type=MESH)

    for j, (la, ca) in enumerate(others):
        by_help = (p == 1) & (lax.rem(la, RUN) == RUN - 1)
        to_l = jnp.where(by_help, la - 1, la)
        to_c = jnp.where(by_help, jnp.clip(ca, 2, nc - 3), ca)
        pl.when(direct_in[j] & ~shut_in[j])(lambda: greet(1 - p, to_l, to_c))

    corner, opposite = (p == 0) & (l == 0) & (c == 0), (p == 0) & (l == 0) & (c == nc - 1)
    pl.when(corner)(lambda: greet(p, l, nc - 1))
    pl.when(near_left)(lambda: greet(p, l - 1, c))
    pl.when(near_right)(lambda: greet(p, l + 1, c))
    pl.when(up)(lambda: greet(p, l, c - 1))
    pl.when(down)(lambda: greet(p, l, c + 1))

    @pl.when(helped_0 | helped_1)
    def _():
        greet(p, jnp.where(at_end, nl - 2, jnp.where(p == 0, l - 1, l)), inner)
        pl.when(seam_by_help)(lambda: greet(p, jnp.where(place == 0, l - 1, l + 1), inner))

    @pl.when((p == 0) & (l < nl - 1) & row_edge & (place >= RUN - 2))
    def _():
        end = l == nl - 2
        last = jnp.where(end, l, l - place + RUN - 1)
        for helper in (2, nc - 3):
            greet(1, last, helper)
            pl.when(place == RUN - 1)(lambda: greet(1, l + 1, helper))

    @pl.when((p == 0) & (l == nl - 1))
    def _():
        for helper in range(2, nc - 2):
            reach = (c >= helper - 1) & (c <= helper + 1)
            if helper == 2:
                reach = (c <= helper + 1) | (c == nc - 1)
            if helper == nc - 3:
                reach = (c >= helper - 1) | (c == 0)
            pl.when(reach)(lambda: greet(1, nl - 2, helper))

    for load in small:
        load.wait()

    row_at = lax.broadcasted_iota(jnp.int32, (CT, CP), 0)
    lane8 = lax.broadcasted_iota(jnp.int32, (8, 128), 1)
    sub8 = lax.broadcasted_iota(jnp.int32, (8, 128), 0)
    lane32 = lax.broadcasted_iota(jnp.int32, (CT, CP), 1)
    first = row_at == rows[0, 0]
    second = row_at == rows[0, 0] + 1
    w = weight[0, 0, 0]
    on_left = jnp.where(first, w[0:1], jnp.where(second, w[2:3], 0.0))
    on_right = jnp.where(first, w[1:2], jnp.where(second, w[3:4], 0.0))
    pick = jnp.broadcast_to(cols[0, 0], (CT, CP))
    pick_next = pick + 1
    halves = [(h, lax.rem(sub8 // h, 2) == 0) for h in (4, 2)]

    def fold(a, b, step):
        h, low = halves[step]
        if h == 4:
            return jnp.where(low, a, b) + pltpu.roll(jnp.where(low, b, a), 4, 0)
        return jnp.where(low, a + pltpu.roll(a, 6, 0), b + pltpu.roll(b, 2, 0))

    for f in range(FIELDS):
        if f % half == 0:
            large[f // half].wait()
        target, sign = TURNED[f]
        sums = []
        for k in range(SHELLS):
            plane = x[f, CT * k : CT * (k + 1), :]
            mixed = on_left * lanes_at(plane, pick) + on_right * lanes_at(plane, pick_next)
            sums.append((mixed[0:8] + mixed[8:16]) + (mixed[16:24] + mixed[24:32]))
        four = fold(fold(sums[0], sums[2], 0), fold(sums[1], sums[3], 0), 1)
        both = four + pltpu.roll(four, 7, 0)
        for k in range(SHELLS):
            line = both[2 * k : 2 * k + 1]
            at = SHELLS * target + k
            slots[at : at + 1, :] = line if sign > 0 else -line

    lanes = lax.broadcasted_iota(jnp.int32, (TALL, CP), 1)
    packed = jnp.zeros((TALL, CP), jnp.float32)
    for f in range(FIELDS):
        for r in range(2):
            row_out[0, f, pl.ds(4 * r, 4), :] = x[f, pl.ds(r, SHELLS, stride=CT), :]
            row_out[1, f, pl.ds(4 * r, 4), :] = x[f, pl.ds(CT - 2 + r, SHELLS, stride=CT), :]
        turned = pltpu.roll(x[f], 2 + 4 * f, 1)
        packed = jnp.where(lanes // 4 == f, turned, packed)
    upright = packed.T
    for f in range(FIELDS):
        col_out[1, f] = upright[4 * f : 4 * f + 2]
        col_out[0, f] = upright[4 * f + 2 : 4 * f + 4]

    row0 = (c * CT).astype(jnp.float32) + 0.5
    col0 = (l * CP).astype(jnp.float32) + 0.5

    def angle_t(row):
        return 0.25 * math.pi + (row + row0) * ht

    def angle_f(col):
        return -0.75 * math.pi + (col + col0) * hp

    theta = angle_t(row_at.astype(jnp.float32))
    phi = angle_f(lane8[0:1].astype(jnp.float32))
    st, ct = jnp.sin(theta), jnp.cos(theta)
    sf = jnp.broadcast_to(jnp.sin(phi), (8, CP))
    cf = jnp.broadcast_to(jnp.cos(phi), (8, CP))
    spin_second = ROTATION * p.astype(jnp.float32)
    spin_third = ROTATION - spin_second

    def one_block(n, _):
        at = pl.multiple_of(n * 8, 8)
        th = angle_t((sub8 + lax.rem(n, CT // 8) * 8).astype(jnp.float32))
        s8, c8 = jnp.sin(th), jnp.cos(th)
        u = [x[f, pl.ds(at, 8), :] for f in range(FIELDS)]
        terms = cell_terms(u)
        er = (s8 * cf, s8 * sf, c8)
        for f, value in enumerate(flux_along(terms, er)):
            radial[f, pl.ds(at, 8), :] = value
        for f, value in enumerate(flux_along(terms, (c8 * cf, c8 * sf, -s8))):
            polar[f, pl.ds(at, 8), :] = value
        for f, value in enumerate(flux_along(terms, (-sf, cf, None))):
            azimuth[f, pl.ds(at, 8), :] = value
        rho, m = u[0], u[1:4]
        turn = (
            spin_second * m[2] - spin_third * m[1], spin_third * m[0], -spin_second * m[0]
        )
        acc[0, pl.ds(at, 8), :] = u[0]
        for i in range(3):
            acc[1 + i, pl.ds(at, 8), :] = m[i] - tau * (2.0 * turn[i] + GRAVITY * (rho * er[i]))
            acc[4 + i, pl.ds(at, 8), :] = u[4 + i]
        acc[7, pl.ds(at, 8), :] = u[7] - (tau * GRAVITY) * (m[0] * er[0] + m[1] * er[1] + m[2] * er[2])
        return 0

    ends = {1: 8.0 / 12.0, 2: -1.0 / 12.0}

    def gives(along, across, n, step):
        even = (ends[n] / step * math.cos(n * step)) * along
        odd = (ends[n] / step * math.sin(n * step)) * across
        return even + odd, odd - even

    radius = [1.0 - (SHELLS - 1 - k) * RADIAL_STEP for k in range(SHELLS)]

    def one_field(f, _):
        fr = [radial[f, pl.ds(CT * k, CT), :] for k in range(SHELLS)]
        for k in range(SHELLS):
            here = pl.ds(CT * k, CT)
            ft, fp = polar[f, here, :], azimuth[f, here, :]
            flat = st * fr[k] + ct * ft
            total_t = jnp.zeros((CT, CP), jnp.float32)
            total_p = total_t
            for n in (1, 2):
                before, after = gives(ft, fr[k], n, ht)
                total_t = total_t + jnp.where(row_at < CT - n, pltpu.roll(before, CT - n, 0), 0.0)
                total_t = total_t + jnp.where(row_at >= n, pltpu.roll(after, n, 0), 0.0)
                before, after = gives(fp, flat, n, hp)
                total_p = total_p + jnp.where(lane32 < CP - n, pltpu.roll(before, CP - n, 1), 0.0)
                total_p = total_p + jnp.where(lane32 >= n, pltpu.roll(after, n, 1), 0.0)
            low, high = max(k - 1, 0), min(k + 1, SHELLS - 1)
            slope = (fr[high] - fr[low]) * (1.0 / ((high - low) * RADIAL_STEP))
            whole = slope + (1.0 / radius[k]) * (total_t + total_p / st)
            acc[f, here, :] = acc[f, here, :] - tau * whole
        return 0

    def own_cells():
        lax.fori_loop(0, TALL // 8, one_block, 0)
        lax.fori_loop(0, FIELDS, one_field, 0)

    idle = (p == 0) & (place < RUN - 1)
    pl.when(idle)(own_cells)

    def one(flag):
        return flag.astype(jnp.int32)

    expected = one(up) + one(down) + one(near_left) + one(near_right)
    for flow, shut in zip(flows_out, shut_out):
        expected = expected + one(flow & ~shut & ~helped_0)
    expected = expected + one(opposite)
    expected = expected + one(helper_1) * (6 + 2 * one(place == RUN - 1)) + 8 * one(helper_0)
    served = jnp.where(at_helper, 3, 1)
    at_panel_1 = 2 * served + jnp.where(at_helper, 9, 3)
    expected = expected + one(end_helper) * jnp.where(p == 1, at_panel_1, 7 * served)
    pl.semaphore_wait(barrier, expected)

    def remote(src, dst, sent, arrived, *device):
        return pltpu.make_async_remote_copy(
            src_ref=src, dst_ref=dst, send_sem=send_sem.at[sent], recv_sem=recv_sem.at[arrived],
            device_id=device, device_id_type=MESH,
        )

    slot_copies = [
        remote(slots, slots_in.at[8 - j], 0, (8 - j) // 3, 1 - p, la, ca) for j, (la, ca) in enumerate(others)
    ]

    def whole(sent, arrived, sets):
        return remote(sets, sets, sent, arrived, 1 - p, l, c)

    def send_slots(wave):
        for j in SEND_ORDER:
            la, ca = others[j]
            spot = lax.rem(la, RUN)
            turn = jnp.where((p == 0) | ((spot == 5) & (place == 6)), 2, jnp.where(spot == 1, 0, 1))
            pl.when(flows_out[j] & ~shut_out[j] & ~helped_0 & (turn == wave))(slot_copies[j].start)

    send_slots(0)
    send_slots(1)

    def tell(*device):
        pl.semaphore_signal(told, inc=1, device_id=device, device_id_type=MESH)

    @pl.when(helper_0 | helper_1)
    def _():
        first = jnp.where(c == 2, 0, nc - 2)
        for more in range(2):
            tell(p, jnp.where(p == 0, l + 1, l), first + more)

    @pl.when(end_helper)
    def _():
        tell(p, nl - 1, c)
        pl.when(p == 1)(lambda: tell(p, 0, c))

        @pl.when(at_helper)
        def _():
            first = jnp.where(c == 2, 0, nc - 2)
            for more in range(2):
                tell(p, nl - 1, first + more)
                pl.when(p == 1)(lambda: tell(p, 0, first + more))
                pl.when(p == 1)(lambda: tell(p, nl - 2, first + more))

    to_up = remote(row_out.at[0], row_in.at[1], 1, 4, p, l, c - 1)
    to_down = remote(row_out.at[1], row_in.at[0], 1, 3, p, l, c + 1)
    to_left = remote(col_out.at[0], col_in.at[1], 2, 6, p, l - 1, c)
    to_right = remote(col_out.at[1], col_in.at[0], 2, 5, p, l + 1, c)
    pl.when(near_left)(to_left.start)
    pl.when(near_right)(to_right.start)
    pl.when(up)(to_up.start)
    pl.when(down)(to_down.start)
    send_slots(2)

    pl.when(~idle)(own_cells)

    @pl.when(helped_0 | helped_1)
    def _():
        pl.semaphore_wait(told, 1)
        pl.when(over_left & seam_by_help)(to_left.start)
        pl.when(over_right & seam_by_help)(to_right.start)
        for j in SEND_ORDER:
            pl.when(flows_out[j] & (shut_out[j] | helped_0))(slot_copies[j].start)

    def near(n):
        return tau * ends[n]

    shell8 = lax.rem(sub8, 4).astype(jnp.float32)
    inverse_r = 1.0 / ((1.0 - (SHELLS - 1 - shell8) * RADIAL_STEP) * ht)
    upper = sub8 < 4

    row_jobs = []
    for jobs in (
        ((0, -near(2), -near(1)), (1, 0.0, -near(2))),
        ((CT - 1, near(1), near(2)), (CT - 2, near(2), 0.0)),
    ):
        row_jobs.append([])
        for row, one_w, two_w in jobs:
            th = angle_t(jnp.full((8, 128), row, jnp.float32))
            s8, c8 = jnp.sin(th), jnp.cos(th)
            row_jobs[-1].append((row, jnp.where(upper, one_w, two_w) * inverse_r, (c8 * cf, c8 * sf, -s8)))

    def add_rows(side, fields):
        terms = cell_terms(fields)
        for row, scale, e in row_jobs[side]:
            where = pl.ds(row, SHELLS, stride=CT)
            for f, value in enumerate(flux_along(terms, e)):
                value = value * scale
                acc[f, where, :] = acc[f, where, :] - (value[0:4] + value[4:8])

    rim = (lanes < 2) | (lanes >= CP - 2)

    sub4 = lax.broadcasted_iota(jnp.int32, (4, 128), 0)
    lane4 = lax.broadcasted_iota(jnp.int32, (4, 128), 1)
    th = angle_t(lax.rem(lane4, CT).astype(jnp.float32))
    shell4 = (lane4 // CT).astype(jnp.float32)
    share = 1.0 / ((1.0 - (SHELLS - 1 - shell4) * RADIAL_STEP) * jnp.sin(th) * hp)
    column_jobs = []
    for from_left, from_right, weights in (
        (0, CP - 1, (-near(2), -near(1), near(1), near(2))),
        (1, CP - 2, (0.0, -near(2), near(2), 0.0)),
    ):
        ph = angle_f(jnp.where(sub4 < 2, from_left, from_right).astype(jnp.float32))
        scale = jnp.where(
            sub4 < 2,
            jnp.where(sub4 == 0, weights[0], weights[1]),
            jnp.where(sub4 == 2, weights[2], weights[3]),
        ) * share
        column_jobs.append((scale, (-jnp.sin(ph), jnp.cos(ph), None)))

    def add_columns():
        u = [jnp.concatenate([col_in[0, f], col_in[1, f]], axis=0) for f in range(FIELDS)]
        terms = cell_terms(u)
        parts = [[v * scale for v in flux_along(terms, e)] for scale, e in column_jobs]
        lines = []
        for f in range(FIELDS):
            close, far = parts[0][f], parts[1][f]
            lines += [far[2:3] + far[3:4], close[2:3] + close[3:4], close[0:1] + close[1:2], far[0:1] + far[1:2]]
        stood = jnp.concatenate(lines + [jnp.zeros((TALL - 4 * FIELDS, CP), jnp.float32)], axis=0).T
        for f in range(FIELDS):
            shift = (CP - 2 - 4 * f) % CP
            acc[f] = acc[f] - jnp.where(rim, pltpu.roll(stood, shift, 1) if shift else stood, 0.0)

    def name(kind, lines):
        for r, line in enumerate(lines):
            named[kind, r] = line

    def name_row(side):
        name(0, [jnp.broadcast_to(wanted[0, 0, :, pl.ds(256 * side + 128 * r, 128)], (8, 128)) for r in range(2)])

    def name_column(side):
        line = jnp.broadcast_to(wanted[0, 0, :, pl.ds(512, 128)], (8, 128))
        name(1, [lanes_at(line, 64 * side + 2 * lax.rem(lane8, CT) + r) for r in range(2)])

    pl.when(c == 0)(lambda: name_row(0))
    pl.when(c == nc - 1)(lambda: name_row(1))
    pl.when(l == 0)(lambda: name_column(0))
    pl.when(l == nl - 1)(lambda: name_column(1))

    def pick_ghosts(kind, group, fresh):
        for r in range(2):
            index = named[kind, r]
            owner = index // SLOTS
            lane = lax.rem(index, SLOTS)
            found = [None if fresh else picked[kind, r, 8 * m : 8 * m + 8, :] for m in range(4)]
            for j in range(3 * group, 3 * group + 3):
                here = owner == others[j][0] * nc + others[j][1]
                for m in range(4):
                    value = lanes_at(slots_in[j, 8 * m : 8 * m + 8, :], lane)
                    found[m] = value if found[m] is None else jnp.where(here, value, found[m])
            for m in range(4):
                picked[kind, r, 8 * m : 8 * m + 8, :] = found[m]

    def add_panel_rims():
        pl.when(left)(to_right.wait_recv)
        pl.when(right)(to_left.wait_recv)
        pl.when(left & right)(add_columns)

        @pl.when(up)
        def _():
            to_down.wait_recv()
            add_rows(0, [row_in[0, f] for f in range(FIELDS)])

        @pl.when(down)
        def _():
            to_up.wait_recv()
            add_rows(1, [row_in[1, f] for f in range(FIELDS)])

    straight = (p == 0) & (place < 4)
    pl.when(~straight)(add_panel_rims)

    pass_on = [
        remote(slots_in.at[3:6], slots_in.at[6:9], 3, 2, p, l - 1, c),
        remote(slots_in.at[3:6], slots_in.at[0:3], 3, 0, p, l + 1, c),
    ]
    to_mate = [
        remote(slots_in.at[3 * group : 3 * group + 2], slots_in.at[3 * group + 1 : 3 * group + 3], 4, group, p, l, c - 1)
        for group in range(3)
    ]
    to_corner = [remote(slots_in.at[3 * g + 1], slots_in.at[3 * g], 4, g, p, l, 0) for g in range(3)]
    for turn, group in enumerate((1, 2, 0)):
        pl.when(edge)(whole(0, group, slots_in.at[3 * group : 3 * group + 3]).wait_recv)
        if group == 1:
            pl.when(pass_left)(pass_on[0].start)
            pl.when(pass_right)(pass_on[1].start)
        pl.when(mate_gives)(to_mate[group].start)
        pl.when(opposite)(to_corner[group].start)
        pl.when(row_edge)(lambda: pick_ghosts(0, group, turn == 0))
        pl.when(at_end)(lambda: pick_ghosts(1, group, turn == 0))

    pl.when(straight)(add_panel_rims)

    @pl.when(at_end)
    def _():
        side = jnp.where(l == 0, 0, 1)
        mine = lane8 // CT == lax.rem(sub8, 4)
        for r in range(2):
            for m in range(4):
                own = jnp.where(mine, picked[1, r, 8 * m : 8 * m + 8, :], 0.0)
                own = own + pltpu.roll(own, 7, 0)
                own = own + pltpu.roll(own, 6, 0)
                col_in[side, 2 * m, r : r + 1, :] = own[0:1]
                col_in[side, 2 * m + 1, r : r + 1, :] = own[4:5]
        add_columns()

    def add_ghost_rows(side):
        fields = [
            jnp.concatenate([picked[0, r, SHELLS * f : SHELLS * f + SHELLS, :] for r in range(2)], axis=0)
            for f in range(FIELDS)
        ]
        add_rows(side, fields)

    pl.when(c == 0)(lambda: add_ghost_rows(0))
    pl.when(c == nc - 1)(lambda: add_ghost_rows(1))

    def wait_sent(sent, number, sets):
        for n in range(1, len(sets) + 1):
            pl.when(number == n)(whole(sent, 0, sets[n - 1]).wait_send)

    number = 0
    for flow in flows_out:
        number = number + one(flow)
    wait_sent(0, number, [slots_in.at[0:n] for n in range(1, 10)])
    wait_sent(1, one(up) + one(down), [row_in.at[0:n] for n in (1, 2)])
    wait_sent(2, one(left) + one(right), [col_in.at[0:n] for n in (1, 2)])
    wait_sent(3, one(pass_left) + one(pass_right), [slots_in.at[0:n] for n in (3, 6)])
    pl.when(mate_gives & ~opposite)(whole(4, 0, slots_in.at[0:6]).wait_send)
    pl.when(opposite)(whole(4, 0, slots_in.at[0:9]).wait_send)


def body(state_now, send_row, send_col, send_weight, ghost_slot):
    f32, i32 = jnp.float32, jnp.int32
    out = pl.pallas_call(
        kernel,
        out_shape=pltpu.VMEM((FIELDS, TALL, CP), f32),
        in_specs=[pl.BlockSpec(memory_space=pltpu.HBM)] * 5,
        out_specs=pl.BlockSpec(memory_space=pltpu.VMEM),
        scratch_shapes=[
            pltpu.VMEM((FIELDS, TALL, CP), f32),
            pltpu.VMEM((1, 1, 1, SLOTS), i32),
            pltpu.VMEM((1, 1, 1, SLOTS), i32),
            pltpu.VMEM((1, 1, 1, 4, SLOTS), f32),
            pltpu.VMEM((1, 1, 1, 640), i32),
            pltpu.VMEM((FIELDS * SHELLS, SLOTS), f32),
            pltpu.VMEM((9, FIELDS * SHELLS, SLOTS), f32),
            pltpu.VMEM((2, FIELDS, 8, CP), f32),
            pltpu.VMEM((2, FIELDS, 8, CP), f32),
            pltpu.VMEM((2, FIELDS, 2, TALL), f32),
            pltpu.VMEM((2, FIELDS, 2, TALL), f32),
            pltpu.VMEM((FIELDS, TALL, CP), f32),
            pltpu.VMEM((FIELDS, TALL, CP), f32),
            pltpu.VMEM((FIELDS, TALL, CP), f32),
            pltpu.VMEM((2, 2, FIELDS * SHELLS, CP), f32),
            pltpu.VMEM((2, 2, 8, CP), i32),
            pltpu.SemaphoreType.DMA((6,)),
            pltpu.SemaphoreType.DMA((5,)),
            pltpu.SemaphoreType.DMA((7,)),
            pltpu.SemaphoreType.REGULAR,
        ],
        compiler_params=pltpu.CompilerParams(
            collective_id=0, has_side_effects=True, vmem_limit_bytes=32 * 1024 * 1024
        ),
    )(*[pltpu.with_memory_space_constraint(a, pltpu.HBM) for a in (state_now.reshape(FIELDS, TALL, CP), send_row, send_col, send_weight, ghost_slot)])
    return out.reshape(1, FIELDS, SHELLS, CT, CP)


def solution(mesh):
    placed = (
        P("panel", None, None, "colat", "lon"),
        P("panel", "lon", "colat", None),
        P("panel", "lon", "colat", None),
        P("panel", "lon", "colat", None, None),
        P("panel", "lon", "colat", None),
    )
    return jax.shard_map(
        body,
        mesh=mesh,
        in_specs=placed,
        out_specs=P("panel", None, None, "colat", "lon"),
        check_vma=False,
    )
```

```python
import math

import jax
import jax.numpy as jnp
from jax import lax
from jax.experimental import pallas as pl
from jax.experimental.pallas import tpu as pltpu
from jax.sharding import PartitionSpec as P

RADIAL_STEP = 0.65 / 511.0
COURANT = 0.3
ROTATION = 300.0
GRAVITY = 300.0
ADIABATIC = 2.0 / 3.0

FIELDS = 8
SHELLS = 4
CT = 32
CP = 128
SLOTS = 128
TALL = SHELLS * CT
MESH = pl.DeviceIdType.MESH
RUN = 8
AROUND = [(dl, dc) for dl in (-1, 0, 1) for dc in (-1, 0, 1)]
SEND_ORDER = (2, 1, 0, 5, 4, 3, 8, 7, 6)
TURNED = [(0, 1.0), (1, -1.0), (3, 1.0), (2, 1.0), (4, -1.0), (6, 1.0), (5, 1.0), (7, 1.0)]


def lanes_at(values, index):
    return jnp.take_along_axis(values, index, axis=1, mode="promise_in_bounds")


def cell_terms(u):
    rho, m, b, energy = u[0], u[1:4], u[4:7], u[7]
    inverse = 1.0 / rho
    v = [a * inverse for a in m]
    power = b[0] * b[0] + b[1] * b[1] + b[2] * b[2]
    moving = m[0] * v[0] + m[1] * v[1] + m[2] * v[2]
    pressure = ADIABATIC * (energy - 0.5 * moving - 0.5 * power) + 0.5 * power
    aligned = v[0] * b[0] + v[1] * b[1] + v[2] * b[2]
    return m, b, v, pressure, energy + pressure, aligned, rho


def flux_along(terms, e):
    m, b, v, pressure, enthalpy, aligned, rho = terms
    ve = v[0] * e[0] + v[1] * e[1]
    be = b[0] * e[0] + b[1] * e[1]
    if e[2] is not None:
        ve = ve + v[2] * e[2]
        be = be + b[2] * e[2]
    out = [rho * ve]
    for i in range(3):
        term = m[i] * ve - b[i] * be
        out.append(term if e[i] is None else term + pressure * e[i])
    for i in range(3):
        out.append(b[i] * ve - v[i] * be)
    out.append(enthalpy * ve - aligned * be)
    return out


def kernel(
    x_hbm, row_hbm, col_hbm, weight_hbm, ghost_hbm, acc,
    x, rows, cols, weight, wanted,
    slots, slots_in, row_out, row_in, col_out, col_in,
    radial, polar, azimuth, picked, named,
    in_sem, send_sem, recv_sem, told,
):
    p, l, c = lax.axis_index("panel"), lax.axis_index("lon"), lax.axis_index("colat")
    nl, nc = lax.axis_size("lon"), lax.axis_size("colat")
    ht = 0.5 * math.pi / (nc * CT)
    hp = 1.5 * math.pi / (nl * CP)
    tau = COURANT / (1.0 / RADIAL_STEP + 1.0 / ht + 1.0 / (hp * math.sin(0.25 * math.pi)))

    def wrap(a, n):
        return lax.rem(a + n, n)

    def on_row(ca):
        return (ca == 0) | (ca == nc - 1)

    def on_edge(la, ca):
        return (la == 0) | (la == nl - 1) | on_row(ca)

    small = [
        pltpu.make_async_copy(src, dst, in_sem.at[3 + i])
        for i, (src, dst) in enumerate(
            ((row_hbm, rows), (col_hbm, cols), (weight_hbm, weight), (ghost_hbm, wanted))
        )
    ]
    cuts = (0, 4, 6, 8)
    large = [
        pltpu.make_async_copy(x_hbm.at[i:k], x.at[i:k], in_sem.at[n]) for n, (i, k) in enumerate(zip(cuts, cuts[1:]))
    ]
    for load in small + large:
        load.start()

    up, down, left, right = c > 0, c < nc - 1, l > 0, l < nl - 1
    edge = on_edge(l, c)
    others = [(wrap(l + dl, nl), wrap(c + dc, nc)) for dl, dc in AROUND]

    late_left, late_right = 4, 4
    place = lax.rem(l, RUN)

    def passed(panel, tile, la):
        late = jnp.where(la < tile, late_left, late_right)
        far = (panel == 1) | ((lax.rem(tile, RUN) >= late) & (lax.rem(la, RUN) != RUN - 1))
        return far & (tile // RUN == la // RUN)

    def straight_from(panel, tile, ca, la):
        return (panel == 0) & (lax.rem(tile, RUN) == 5) & (ca == 0) & (la > tile)

    flows_out, direct_in, shut_out, shut_in = [], [], [], []
    beside = (c < 2) | (c >= nc - 2)
    to_panel_1 = p == 0
    for (la, ca), (dl, dc) in zip(others, AROUND):
        flow, got = on_edge(la, ca), edge
        if dl:
            flow = flow & ~(on_row(ca) & passed(1 - p, la, l) & ~straight_from(1 - p, la, ca, l))
            got = got & ~(on_row(c) & passed(p, l, la) & ~straight_from(p, l, c, la))
        if dc != 1:
            flow = flow & ~((p == 1) & (la == 0) & (lax.rem(ca, 2) == 0))
        else:
            flow = flow & ~((p == 1) & (la == 0) & (ca == 0))
        if dc != -1:
            got = got & ~((p == 0) & (l == 0) & (lax.rem(c, 2) == 0))
        else:
            got = got & ~((p == 0) & (l == 0) & (c == 0))
        flows_out.append(flow)
        direct_in.append(got)
        shut = ((place == RUN - 1) & (dl <= 0)) | ((place == 0) & (dl == -1))
        if dl == 1:
            shut = shut | ((l == nl - 2) & beside)
        shut_out.append((p == 1) & shut)
        shut = ((place == RUN - 1) & (dl >= 0)) | ((place == RUN - 2) & (dl == 1))
        if dl == -1:
            shut = shut | ((l == nl - 1) & ((ca < 2) | (ca >= nc - 2)))
        shut_in.append((p == 0) & shut)
    row_edge = on_row(c)
    pass_left = row_edge & left & passed(p, l - 1, l) & ~straight_from(p, l - 1, c, l)
    pass_right = row_edge & right & passed(p, l + 1, l)
    mate_gives = (p == 0) & (l == 0) & (lax.rem(c, 2) == 1)
    mate_takes = (p == 0) & (l == 0) & (lax.rem(c, 2) == 0)

    inner = jnp.clip(c, 2, nc - 3)
    at_seam = (place == 0) | (place == RUN - 1)
    at_end = (l == 0) | (l == nl - 1)
    helped_1 = (p == 1) & ((at_seam & (beside | at_end)) | ((l == nl - 2) & beside))
    helped_0 = (p == 0) & (place == RUN - 1) & (beside | at_end)
    at_helper = (c == 2) | (c == nc - 3)
    helper_1 = (p == 1) & at_seam & ~at_end & at_helper
    helper_0 = (p == 0) & (place == RUN - 2) & (l != nl - 2) & at_helper
    end_helper = (l == nl - 2) & ~beside
    over_left, over_right = left & (place == 0), right & (place == RUN - 1)
    seam_by_help = helped_1 & at_seam & ~at_end
    near_left, near_right = left & ~(over_left & seam_by_help), right & ~(over_right & seam_by_help)

    barrier = pltpu.get_barrier_semaphore()

    def greet(*device):
        pl.semaphore_signal(barrier, inc=1, device_id=device, device_id_type=MESH)

    for j, (la, ca) in enumerate(others):
        by_help = (p == 1) & (lax.rem(la, RUN) == RUN - 1)
        to_l = jnp.where(by_help, la - 1, la)
        to_c = jnp.where(by_help, jnp.clip(ca, 2, nc - 3), ca)
        pl.when(direct_in[j] & ~shut_in[j])(lambda: greet(1 - p, to_l, to_c))

    corner, opposite = (p == 0) & (l == 0) & (c == 0), (p == 0) & (l == 0) & (c == nc - 1)
    pl.when(corner)(lambda: greet(p, l, nc - 1))
    pl.when(near_left)(lambda: greet(p, l - 1, c))
    pl.when(near_right)(lambda: greet(p, l + 1, c))
    pl.when(up)(lambda: greet(p, l, c - 1))
    pl.when(down)(lambda: greet(p, l, c + 1))

    @pl.when(helped_0 | helped_1)
    def _():
        greet(p, jnp.where(at_end, nl - 2, jnp.where(p == 0, l - 1, l)), inner)
        pl.when(seam_by_help)(lambda: greet(p, jnp.where(place == 0, l - 1, l + 1), inner))

    @pl.when((p == 0) & (l < nl - 1) & row_edge & (place >= RUN - 2))
    def _():
        end = l == nl - 2
        last = jnp.where(end, l, l - place + RUN - 1)
        for helper in (2, nc - 3):
            greet(1, last, helper)
            pl.when(place == RUN - 1)(lambda: greet(1, l + 1, helper))

    @pl.when((p == 0) & (l == nl - 1))
    def _():
        for helper in range(2, nc - 2):
            reach = (c >= helper - 1) & (c <= helper + 1)
            if helper == 2:
                reach = (c <= helper + 1) | (c == nc - 1)
            if helper == nc - 3:
                reach = (c >= helper - 1) | (c == 0)
            pl.when(reach)(lambda: greet(1, nl - 2, helper))

    for load in small:
        load.wait()

    row_at = lax.broadcasted_iota(jnp.int32, (CT, CP), 0)
    lane8 = lax.broadcasted_iota(jnp.int32, (8, 128), 1)
    sub8 = lax.broadcasted_iota(jnp.int32, (8, 128), 0)
    lane32 = lax.broadcasted_iota(jnp.int32, (CT, CP), 1)
    first = row_at == rows[0, 0]
    second = row_at == rows[0, 0] + 1
    w = weight[0, 0, 0]
    on_left = jnp.where(first, w[0:1], jnp.where(second, w[2:3], 0.0))
    on_right = jnp.where(first, w[1:2], jnp.where(second, w[3:4], 0.0))
    pick = jnp.broadcast_to(cols[0, 0], (CT, CP))
    pick_next = pick + 1
    halves = [(h, lax.rem(sub8 // h, 2) == 0) for h in (4, 2)]

    def fold(a, b, step):
        h, low = halves[step]
        if h == 4:
            return jnp.where(low, a, b) + pltpu.roll(jnp.where(low, b, a), 4, 0)
        return jnp.where(low, a + pltpu.roll(a, 6, 0), b + pltpu.roll(b, 2, 0))

    for f in range(FIELDS):
        if f in cuts:
            large[cuts.index(f)].wait()
        target, sign = TURNED[f]
        sums = []
        for k in range(SHELLS):
            plane = x[f, CT * k : CT * (k + 1), :]
            mixed = on_left * lanes_at(plane, pick) + on_right * lanes_at(plane, pick_next)
            sums.append((mixed[0:8] + mixed[8:16]) + (mixed[16:24] + mixed[24:32]))
        four = fold(fold(sums[0], sums[2], 0), fold(sums[1], sums[3], 0), 1)
        both = four + pltpu.roll(four, 7, 0)
        for k in range(SHELLS):
            line = both[2 * k : 2 * k + 1]
            at = SHELLS * target + k
            slots[at : at + 1, :] = line if sign > 0 else -line

    lanes = lax.broadcasted_iota(jnp.int32, (TALL, CP), 1)
    packed = jnp.zeros((TALL, CP), jnp.float32)
    for f in range(FIELDS):
        for r in range(2):
            row_out[0, f, pl.ds(4 * r, 4), :] = x[f, pl.ds(r, SHELLS, stride=CT), :]
            row_out[1, f, pl.ds(4 * r, 4), :] = x[f, pl.ds(CT - 2 + r, SHELLS, stride=CT), :]
        turned = pltpu.roll(x[f], 2 + 4 * f, 1)
        packed = jnp.where(lanes // 4 == f, turned, packed)
    upright = packed.T
    for f in range(FIELDS):
        col_out[1, f] = upright[4 * f : 4 * f + 2]
        col_out[0, f] = upright[4 * f + 2 : 4 * f + 4]

    row0 = (c * CT).astype(jnp.float32) + 0.5
    col0 = (l * CP).astype(jnp.float32) + 0.5

    def angle_t(row):
        return 0.25 * math.pi + (row + row0) * ht

    def angle_f(col):
        return -0.75 * math.pi + (col + col0) * hp

    theta = angle_t(row_at.astype(jnp.float32))
    phi = angle_f(lane8[0:1].astype(jnp.float32))
    st, ct = jnp.sin(theta), jnp.cos(theta)
    sf = jnp.broadcast_to(jnp.sin(phi), (8, CP))
    cf = jnp.broadcast_to(jnp.cos(phi), (8, CP))
    spin_second = ROTATION * p.astype(jnp.float32)
    spin_third = ROTATION - spin_second

    def one_block(n, _):
        at = pl.multiple_of(n * 8, 8)
        th = angle_t((sub8 + lax.rem(n, CT // 8) * 8).astype(jnp.float32))
        s8, c8 = jnp.sin(th), jnp.cos(th)
        u = [x[f, pl.ds(at, 8), :] for f in range(FIELDS)]
        terms = cell_terms(u)
        er = (s8 * cf, s8 * sf, c8)
        for f, value in enumerate(flux_along(terms, er)):
            radial[f, pl.ds(at, 8), :] = value
        for f, value in enumerate(flux_along(terms, (c8 * cf, c8 * sf, -s8))):
            polar[f, pl.ds(at, 8), :] = value
        for f, value in enumerate(flux_along(terms, (-sf, cf, None))):
            azimuth[f, pl.ds(at, 8), :] = value
        rho, m = u[0], u[1:4]
        turn = (
            spin_second * m[2] - spin_third * m[1], spin_third * m[0], -spin_second * m[0]
        )
        acc[0, pl.ds(at, 8), :] = u[0]
        for i in range(3):
            acc[1 + i, pl.ds(at, 8), :] = m[i] - tau * (2.0 * turn[i] + GRAVITY * (rho * er[i]))
            acc[4 + i, pl.ds(at, 8), :] = u[4 + i]
        acc[7, pl.ds(at, 8), :] = u[7] - (tau * GRAVITY) * (m[0] * er[0] + m[1] * er[1] + m[2] * er[2])
        return 0

    ends = {1: 8.0 / 12.0, 2: -1.0 / 12.0}

    def gives(along, across, n, step):
        even = (ends[n] / step * math.cos(n * step)) * along
        odd = (ends[n] / step * math.sin(n * step)) * across
        return even + odd, odd - even

    radius = [1.0 - (SHELLS - 1 - k) * RADIAL_STEP for k in range(SHELLS)]

    def one_field(f, _):
        fr = [radial[f, pl.ds(CT * k, CT), :] for k in range(SHELLS)]
        for k in range(SHELLS):
            here = pl.ds(CT * k, CT)
            ft, fp = polar[f, here, :], azimuth[f, here, :]
            flat = st * fr[k] + ct * ft
            total_t = jnp.zeros((CT, CP), jnp.float32)
            total_p = total_t
            for n in (1, 2):
                before, after = gives(ft, fr[k], n, ht)
                total_t = total_t + jnp.where(row_at < CT - n, pltpu.roll(before, CT - n, 0), 0.0)
                total_t = total_t + jnp.where(row_at >= n, pltpu.roll(after, n, 0), 0.0)
                before, after = gives(fp, flat, n, hp)
                total_p = total_p + jnp.where(lane32 < CP - n, pltpu.roll(before, CP - n, 1), 0.0)
                total_p = total_p + jnp.where(lane32 >= n, pltpu.roll(after, n, 1), 0.0)
            low, high = max(k - 1, 0), min(k + 1, SHELLS - 1)
            slope = (fr[high] - fr[low]) * (1.0 / ((high - low) * RADIAL_STEP))
            whole = slope + (1.0 / radius[k]) * (total_t + total_p / st)
            acc[f, here, :] = acc[f, here, :] - tau * whole
        return 0

    def own_cells():
        lax.fori_loop(0, TALL // 8, one_block, 0)
        lax.fori_loop(0, FIELDS, one_field, 0)

    idle = (p == 0) & (place < RUN - 1)
    pl.when(idle)(own_cells)

    def one(flag):
        return flag.astype(jnp.int32)

    expected = one(up) + one(down) + one(near_left) + one(near_right)
    for flow, shut in zip(flows_out, shut_out):
        expected = expected + one(flow & ~shut & ~helped_0)
    expected = expected + one(opposite)
    expected = expected + one(helper_1) * (6 + 2 * one(place == RUN - 1)) + 8 * one(helper_0)
    served = jnp.where(at_helper, 3, 1)
    at_panel_1 = 2 * served + jnp.where(at_helper, 9, 3)
    expected = expected + one(end_helper) * jnp.where(p == 1, at_panel_1, 7 * served)
    pl.semaphore_wait(barrier, expected)

    def remote(src, dst, sent, arrived, *device):
        return pltpu.make_async_remote_copy(
            src_ref=src, dst_ref=dst, send_sem=send_sem.at[sent], recv_sem=recv_sem.at[arrived],
            device_id=device, device_id_type=MESH,
        )

    slot_copies = [
        remote(slots, slots_in.at[8 - j], 0, (8 - j) // 3, 1 - p, la, ca) for j, (la, ca) in enumerate(others)
    ]

    def whole(sent, arrived, sets):
        return remote(sets, sets, sent, arrived, 1 - p, l, c)

    def send_slots(wave):
        for j in SEND_ORDER:
            la, ca = others[j]
            spot = lax.rem(la, RUN)
            turn = jnp.where((p == 0) | ((spot == 5) & (place == 6)), 2, jnp.where(spot == 1, 0, 1))
            pl.when(flows_out[j] & ~shut_out[j] & ~helped_0 & (turn == wave))(slot_copies[j].start)

    send_slots(0)
    send_slots(1)

    def tell(*device):
        pl.semaphore_signal(told, inc=1, device_id=device, device_id_type=MESH)

    @pl.when(helper_0 | helper_1)
    def _():
        first = jnp.where(c == 2, 0, nc - 2)
        for more in range(2):
            tell(p, jnp.where(p == 0, l + 1, l), first + more)

    @pl.when(end_helper)
    def _():
        tell(p, nl - 1, c)
        pl.when(p == 1)(lambda: tell(p, 0, c))

        @pl.when(at_helper)
        def _():
            first = jnp.where(c == 2, 0, nc - 2)
            for more in range(2):
                tell(p, nl - 1, first + more)
                pl.when(p == 1)(lambda: tell(p, 0, first + more))
                pl.when(p == 1)(lambda: tell(p, nl - 2, first + more))

    to_up = remote(row_out.at[0], row_in.at[1], 1, 4, p, l, c - 1)
    to_down = remote(row_out.at[1], row_in.at[0], 1, 3, p, l, c + 1)
    to_left = remote(col_out.at[0], col_in.at[1], 2, 6, p, l - 1, c)
    to_right = remote(col_out.at[1], col_in.at[0], 2, 5, p, l + 1, c)
    pl.when(near_left)(to_left.start)
    pl.when(near_right)(to_right.start)
    pl.when(up)(to_up.start)
    pl.when(down)(to_down.start)
    send_slots(2)

    pl.when(~idle)(own_cells)

    @pl.when(helped_0 | helped_1)
    def _():
        pl.semaphore_wait(told, 1)
        pl.when(over_left & seam_by_help)(to_left.start)
        pl.when(over_right & seam_by_help)(to_right.start)
        for j in SEND_ORDER:
            pl.when(flows_out[j] & (shut_out[j] | helped_0))(slot_copies[j].start)

    def near(n):
        return tau * ends[n]

    shell8 = lax.rem(sub8, 4).astype(jnp.float32)
    inverse_r = 1.0 / ((1.0 - (SHELLS - 1 - shell8) * RADIAL_STEP) * ht)
    upper = sub8 < 4

    row_jobs = []
    for jobs in (
        ((0, -near(2), -near(1)), (1, 0.0, -near(2))),
        ((CT - 1, near(1), near(2)), (CT - 2, near(2), 0.0)),
    ):
        row_jobs.append([])
        for row, one_w, two_w in jobs:
            th = angle_t(jnp.full((8, 128), row, jnp.float32))
            s8, c8 = jnp.sin(th), jnp.cos(th)
            row_jobs[-1].append((row, jnp.where(upper, one_w, two_w) * inverse_r, (c8 * cf, c8 * sf, -s8)))

    def add_rows(side, fields):
        terms = cell_terms(fields)
        for row, scale, e in row_jobs[side]:
            where = pl.ds(row, SHELLS, stride=CT)
            for f, value in enumerate(flux_along(terms, e)):
                value = value * scale
                acc[f, where, :] = acc[f, where, :] - (value[0:4] + value[4:8])

    rim = (lanes < 2) | (lanes >= CP - 2)

    sub4 = lax.broadcasted_iota(jnp.int32, (4, 128), 0)
    lane4 = lax.broadcasted_iota(jnp.int32, (4, 128), 1)
    th = angle_t(lax.rem(lane4, CT).astype(jnp.float32))
    shell4 = (lane4 // CT).astype(jnp.float32)
    share = 1.0 / ((1.0 - (SHELLS - 1 - shell4) * RADIAL_STEP) * jnp.sin(th) * hp)
    column_jobs = []
    for from_left, from_right, weights in (
        (0, CP - 1, (-near(2), -near(1), near(1), near(2))),
        (1, CP - 2, (0.0, -near(2), near(2), 0.0)),
    ):
        ph = angle_f(jnp.where(sub4 < 2, from_left, from_right).astype(jnp.float32))
        scale = jnp.where(
            sub4 < 2,
            jnp.where(sub4 == 0, weights[0], weights[1]),
            jnp.where(sub4 == 2, weights[2], weights[3]),
        ) * share
        column_jobs.append((scale, (-jnp.sin(ph), jnp.cos(ph), None)))

    def add_columns():
        u = [jnp.concatenate([col_in[0, f], col_in[1, f]], axis=0) for f in range(FIELDS)]
        terms = cell_terms(u)
        parts = [[v * scale for v in flux_along(terms, e)] for scale, e in column_jobs]
        lines = []
        for f in range(FIELDS):
            close, far = parts[0][f], parts[1][f]
            lines += [far[2:3] + far[3:4], close[2:3] + close[3:4], close[0:1] + close[1:2], far[0:1] + far[1:2]]
        stood = jnp.concatenate(lines + [jnp.zeros((TALL - 4 * FIELDS, CP), jnp.float32)], axis=0).T
        for f in range(FIELDS):
            shift = (CP - 2 - 4 * f) % CP
            acc[f] = acc[f] - jnp.where(rim, pltpu.roll(stood, shift, 1) if shift else stood, 0.0)

    def name(kind, lines):
        for r, line in enumerate(lines):
            named[kind, r] = line

    def name_row(side):
        name(0, [jnp.broadcast_to(wanted[0, 0, :, pl.ds(256 * side + 128 * r, 128)], (8, 128)) for r in range(2)])

    def name_column(side):
        line = jnp.broadcast_to(wanted[0, 0, :, pl.ds(512, 128)], (8, 128))
        name(1, [lanes_at(line, 64 * side + 2 * lax.rem(lane8, CT) + r) for r in range(2)])

    pl.when(c == 0)(lambda: name_row(0))
    pl.when(c == nc - 1)(lambda: name_row(1))
    pl.when(l == 0)(lambda: name_column(0))
    pl.when(l == nl - 1)(lambda: name_column(1))

    def pick_ghosts(kind, group, fresh):
        for r in range(2):
            index = named[kind, r]
            owner = index // SLOTS
            lane = lax.rem(index, SLOTS)
            found = [None if fresh else picked[kind, r, 8 * m : 8 * m + 8, :] for m in range(4)]
            for j in range(3 * group, 3 * group + 3):
                here = owner == others[j][0] * nc + others[j][1]
                for m in range(4):
                    value = lanes_at(slots_in[j, 8 * m : 8 * m + 8, :], lane)
                    found[m] = value if found[m] is None else jnp.where(here, value, found[m])
            for m in range(4):
                picked[kind, r, 8 * m : 8 * m + 8, :] = found[m]

    def add_panel_rims():
        pl.when(left)(to_right.wait_recv)
        pl.when(right)(to_left.wait_recv)
        pl.when(left & right)(add_columns)

        @pl.when(up)
        def _():
            to_down.wait_recv()
            add_rows(0, [row_in[0, f] for f in range(FIELDS)])

        @pl.when(down)
        def _():
            to_up.wait_recv()
            add_rows(1, [row_in[1, f] for f in range(FIELDS)])

    straight = (p == 0) & (place < 4)
    pl.when(~straight)(add_panel_rims)

    pass_on = [
        remote(slots_in.at[3:6], slots_in.at[6:9], 3, 2, p, l - 1, c),
        remote(slots_in.at[3:6], slots_in.at[0:3], 3, 0, p, l + 1, c),
    ]
    to_mate = [
        remote(slots_in.at[3 * group : 3 * group + 2], slots_in.at[3 * group + 1 : 3 * group + 3], 4, group, p, l, c - 1)
        for group in range(3)
    ]
    to_corner = [remote(slots_in.at[3 * g + 1], slots_in.at[3 * g], 4, g, p, l, 0) for g in range(3)]
    for turn, group in enumerate((1, 0, 2)):
        pl.when(edge)(whole(0, group, slots_in.at[3 * group : 3 * group + 3]).wait_recv)
        if group == 1:
            pl.when(pass_left)(pass_on[0].start)
            pl.when(pass_right)(pass_on[1].start)
        pl.when(mate_gives)(to_mate[group].start)
        pl.when(opposite)(to_corner[group].start)
        pl.when(row_edge)(lambda: pick_ghosts(0, group, turn == 0))
        pl.when(at_end)(lambda: pick_ghosts(1, group, turn == 0))

    pl.when(straight)(add_panel_rims)

    @pl.when(at_end)
    def _():
        side = jnp.where(l == 0, 0, 1)
        mine = lane8 // CT == lax.rem(sub8, 4)
        for r in range(2):
            for m in range(4):
                own = jnp.where(mine, picked[1, r, 8 * m : 8 * m + 8, :], 0.0)
                own = own + pltpu.roll(own, 7, 0)
                own = own + pltpu.roll(own, 6, 0)
                col_in[side, 2 * m, r : r + 1, :] = own[0:1]
                col_in[side, 2 * m + 1, r : r + 1, :] = own[4:5]
        add_columns()

    def add_ghost_rows(side):
        fields = [
            jnp.concatenate([picked[0, r, SHELLS * f : SHELLS * f + SHELLS, :] for r in range(2)], axis=0)
            for f in range(FIELDS)
        ]
        add_rows(side, fields)

    pl.when(c == 0)(lambda: add_ghost_rows(0))
    pl.when(c == nc - 1)(lambda: add_ghost_rows(1))

    def wait_sent(sent, number, sets):
        for n in range(1, len(sets) + 1):
            pl.when(number == n)(whole(sent, 0, sets[n - 1]).wait_send)

    number = 0
    for flow in flows_out:
        number = number + one(flow)
    wait_sent(0, number, [slots_in.at[0:n] for n in range(1, 10)])
    wait_sent(1, one(up) + one(down), [row_in.at[0:n] for n in (1, 2)])
    wait_sent(2, one(left) + one(right), [col_in.at[0:n] for n in (1, 2)])
    wait_sent(3, one(pass_left) + one(pass_right), [slots_in.at[0:n] for n in (3, 6)])
    pl.when(mate_gives & ~opposite)(whole(4, 0, slots_in.at[0:6]).wait_send)
    pl.when(opposite)(whole(4, 0, slots_in.at[0:9]).wait_send)


def body(state_now, send_row, send_col, send_weight, ghost_slot):
    f32, i32 = jnp.float32, jnp.int32
    out = pl.pallas_call(
        kernel,
        out_shape=pltpu.VMEM((FIELDS, TALL, CP), f32),
        in_specs=[pl.BlockSpec(memory_space=pltpu.HBM)] * 5,
        out_specs=pl.BlockSpec(memory_space=pltpu.VMEM),
        scratch_shapes=[
            pltpu.VMEM((FIELDS, TALL, CP), f32),
            pltpu.VMEM((1, 1, 1, SLOTS), i32),
            pltpu.VMEM((1, 1, 1, SLOTS), i32),
            pltpu.VMEM((1, 1, 1, 4, SLOTS), f32),
            pltpu.VMEM((1, 1, 1, 640), i32),
            pltpu.VMEM((FIELDS * SHELLS, SLOTS), f32),
            pltpu.VMEM((9, FIELDS * SHELLS, SLOTS), f32),
            pltpu.VMEM((2, FIELDS, 8, CP), f32),
            pltpu.VMEM((2, FIELDS, 8, CP), f32),
            pltpu.VMEM((2, FIELDS, 2, TALL), f32),
            pltpu.VMEM((2, FIELDS, 2, TALL), f32),
            pltpu.VMEM((FIELDS, TALL, CP), f32),
            pltpu.VMEM((FIELDS, TALL, CP), f32),
            pltpu.VMEM((FIELDS, TALL, CP), f32),
            pltpu.VMEM((2, 2, FIELDS * SHELLS, CP), f32),
            pltpu.VMEM((2, 2, 8, CP), i32),
            pltpu.SemaphoreType.DMA((7,)),
            pltpu.SemaphoreType.DMA((5,)),
            pltpu.SemaphoreType.DMA((7,)),
            pltpu.SemaphoreType.REGULAR,
        ],
        compiler_params=pltpu.CompilerParams(
            collective_id=0, has_side_effects=True, vmem_limit_bytes=32 * 1024 * 1024
        ),
    )(*[pltpu.with_memory_space_constraint(a, pltpu.HBM) for a in (state_now.reshape(FIELDS, TALL, CP), send_row, send_col, send_weight, ghost_slot)])
    return out.reshape(1, FIELDS, SHELLS, CT, CP)


def solution(mesh):
    placed = (
        P("panel", None, None, "colat", "lon"),
        P("panel", "lon", "colat", None),
        P("panel", "lon", "colat", None),
        P("panel", "lon", "colat", None, None),
        P("panel", "lon", "colat", None),
    )
    return jax.shard_map(
        body,
        mesh=mesh,
        in_specs=placed,
        out_specs=P("panel", None, None, "colat", "lon"),
        check_vma=False,
    )
```
